32 devices in a mesh: vox: 4 (over y, core), fas: 8 (over z, x).
Axes of the slice: x: 2, y: 2, z: 4, core: 2. Of those that a mesh axis runs over, the one named last changes fastest.
Arguments:
- signal: float32 [64, 6144], P('vox', 'fas'), may hold values from -6 to 6
- initial_weights: float32 [262144], P('fas'), may hold values from 0.1 to 2
- coefficients: bfloat16 [8192, 4096], P(('vox', 'fas')), may hold values from 0 to 0.032958984
- block_rows: int32 [8192], P(('vox', 'fas')), may hold values from 0 to 63, as said below
- block_cols: int32 [8192], P(('vox', 'fas')), may hold values from 0 to 4095, as said below
- block_atoms: int32 [8192, 64], P(('vox', 'fas')), may hold values from 0 to 359
- block_count: int32 [32], P(('vox', 'fas')), may hold values from 64 to 256, as said below
- dictionary: bfloat16 [360, 96], replicated, may hold values from -6 to 6
Outputs:
- weights: float32 [262144], P('fas')
- residual: float32 [64, 6144], P('vox', 'fas')
The draws below stay inside these ranges and needn't reach their ends.
Inputs may be any that keep to these rules, and one draw needn't show every extreme that they name: Block slots are stored device by device: the device with vox index i and fas index f holds slots (i * 8 + f) * 256 to (i * 8 + f + 1) * 256 - 1, and every block_rows value there lies in i * 16 to (i + 1) * 16 - 1. For the slots of the device with fas index f, every block_cols value lies in f * 512 to (f + 1) * 512 - 1. `block_count`: entry i * 8 + f is the number of live slots of the device with vox index i and fas index f, its first slots; some device has all 256 live.
All inputs are finite; a program needn't handle non-finite values.
Results may differ from the reference program's by a relative error of at most 0.0003.
Values sent between devices are 32-bit elements; how exact they have to be, the bound alone decides.
No kernel may reach another device: no remote copies, remote signals or barrier semaphores. Data moves between devices by JAX's collectives and lax.ppermute only.
A program may use at most 128 MiB of HBM per device.

```python
import math
import jax
import jax.numpy as jnp
from jax import lax

BV = 64
BF = 64
DIRS = 96
ATOMS = 360
VB_DEV = 16
FB_DEV = 512
KDEV = 256
ITERS = 5
VBLOCKS = 64
FASC = 262144
BLOCKS = 8192
N_VOX = 4
N_FAS = 8


def draw_block_rows(key, part):
    slot_index = jnp.arange(KDEV * N_VOX * N_FAS, dtype=jnp.int32) // KDEV
    vox_index = slot_index // N_FAS
    offsets = jax.random.randint(key, (KDEV * N_VOX * N_FAS,), 0, VB_DEV, dtype=jnp.int32)
    return (vox_index * VB_DEV + offsets).astype(jnp.int32)


def draw_block_cols(key, part):
    slot_index = jnp.arange(KDEV * N_VOX * N_FAS, dtype=jnp.int32) // KDEV
    fas_index = slot_index % N_FAS
    offsets = jax.random.randint(key, (KDEV * N_VOX * N_FAS,), 0, FB_DEV, dtype=jnp.int32)
    return (fas_index * FB_DEV + offsets).astype(jnp.int32)


def draw_block_count(key, part):
    counts = jax.random.randint(key, (N_VOX * N_FAS,), KDEV // 4, KDEV + 1, dtype=jnp.int32)
    fullest = jax.random.randint(jax.random.fold_in(key, 7), (), 0, N_VOX * N_FAS, dtype=jnp.int32)
    places = jnp.arange(N_VOX * N_FAS, dtype=jnp.int32)
    return jnp.where(places == fullest, KDEV, counts).astype(jnp.int32)


def place_ends(entries, stream_key, smallest, largest):
    spot = [jax.random.randint(jax.random.fold_in(stream_key, axis), (), 0, length) for axis, length in enumerate(entries.shape)]
    longest = entries.shape.index(max(entries.shape))
    next_to = spot[:longest] + [(spot[longest] + 1) % entries.shape[longest]] + spot[longest + 1:]
    return entries.at[tuple(spot)].set(smallest).at[tuple(next_to)].set(largest)


def shard_levels(rng, extent, shards, least, top_value):
    level, own = 1.0, jax.random.fold_in(rng, 6)
    for position, blocks in shards:
        heights = jnp.exp(jax.random.uniform(jax.random.fold_in(own, position), (blocks,), jnp.float32, least / len(shards), top_value / len(shards)))
        level = level * jnp.repeat(heights, extent[position] // blocks).reshape([-1 if axis == position else 1 for axis in range(len(extent))])
    return level


def bell_draw(stream_key, dims, width, reach, shards=(), kind=jnp.bfloat16):
    values = jax.random.normal(stream_key, dims, jnp.float32) * width
    if len(shards) > 0:
        values = shard_levels(stream_key, dims, shards, -0.22, 0.18) * values
    return jnp.clip(values, min=-reach, max=reach).astype(kind)


def setup_inputs(seed: int = 0) -> dict:
    key_of = jax.random.split(jax.random.key(seed), 9)
    signal = bell_draw(key_of[0], (VBLOCKS, BV * DIRS), 1.0, 6.0, ((0, 4), (1, 8)), jnp.float32)
    initial_weights = jnp.clip(jnp.exp(math.log(2.0) - 2.9957323 * jax.random.uniform(key_of[1], (FASC,), jnp.float32) ** shard_levels(key_of[1], (FASC,), ((0, 8),), -0.2, 0.2)), 0.1, 2.0)
    coefficients = jnp.clip(0.032958984 * jax.random.uniform(key_of[2], (BLOCKS, BV * BF), jnp.float32) ** shard_levels(key_of[2], (BLOCKS, BV * BF), ((0, 32),), -0.2, 0.2), 0.0, 0.032958984).astype(jnp.bfloat16)
    block_rows = draw_block_rows(jax.random.fold_in(key_of[8], 71), 0)
    block_cols = draw_block_cols(jax.random.fold_in(key_of[8], 71), 0)
    block_atoms = place_ends(jax.random.randint(key_of[5], (BLOCKS, BF), 0, ATOMS), jax.random.fold_in(key_of[5], 1), 0, ATOMS - 1).astype(jnp.int32)
    block_count = draw_block_count(jax.random.fold_in(key_of[8], 71), 0)
    dictionary = bell_draw(key_of[7], (ATOMS, DIRS), 1.0, 6.0)
    return {"signal": signal, "initial_weights": initial_weights, "coefficients": coefficients, "block_rows": block_rows, "block_cols": block_cols, "block_atoms": block_atoms, "block_count": block_count, "dictionary": dictionary}


def reference(signal, initial_weights, coefficients, block_rows, block_cols, block_atoms, block_count, dictionary):
    device_total = N_VOX * N_FAS
    coef_all = coefficients.reshape(device_total, KDEV, BV, BF)
    rows_all = block_rows.reshape(device_total, KDEV)
    cols_all = block_cols.reshape(device_total, KDEV)
    atoms_all = block_atoms.reshape(device_total, KDEV, BF)
    live_all = (jnp.arange(KDEV, dtype=jnp.int32)[None, :] < block_count[:, None]).astype(jnp.float32)
    vox_blocks = signal.shape[0]
    fas_blocks = initial_weights.shape[0] // BF

    def forward(values):
        table = values.reshape(fas_blocks, BF)

        def accumulate(running, pieces):
            coef_blk, rows_blk, cols_blk, atoms_blk, live_blk = pieces
            atom_rows = dictionary[atoms_blk].astype(jnp.float32)
            scaled = coef_blk.astype(jnp.float32) * table[cols_blk][:, None, :]
            image_blk = jnp.einsum("kvj,kjd->kvd", scaled, atom_rows, precision=lax.Precision.HIGHEST)
            return running.at[rows_blk].add(image_blk * live_blk[:, None, None]), None

        start = jnp.zeros((vox_blocks, BV, DIRS), jnp.float32)
        running, _ = lax.scan(accumulate, start, (coef_all, rows_all, cols_all, atoms_all, live_all))
        return running.reshape(vox_blocks, BV * DIRS)

    def backward(resid):
        rows_view = resid.reshape(vox_blocks, BV, DIRS)

        def accumulate(running, pieces):
            coef_blk, rows_blk, cols_blk, atoms_blk, live_blk = pieces
            atom_rows = dictionary[atoms_blk].astype(jnp.float32)
            gathered = rows_view[rows_blk].astype(jnp.float32)
            inner = jnp.einsum("kvj,kvd->kjd", coef_blk.astype(jnp.float32), gathered, precision=lax.Precision.HIGHEST)
            contrib = jnp.sum(atom_rows * inner, axis=-1) * live_blk[:, None]
            return running.at[cols_blk].add(contrib), None

        start = jnp.zeros((fas_blocks, BF), jnp.float32)
        running, _ = lax.scan(accumulate, start, (coef_all, rows_all, cols_all, atoms_all, live_all))
        return running.reshape(-1)

    weights = initial_weights
    residual = forward(weights) - signal
    for sweep in range(ITERS):
        gradient = backward(residual)
        projected = jnp.where((weights > 0) | (gradient < 0), gradient, 0.0)
        image_pred = forward(projected)
        step_size = jnp.sum(projected * projected) / (jnp.sum(image_pred * image_pred) + 1e-6)
        weights = jnp.maximum(weights - step_size * projected, 0.0)
        residual = forward(weights) - signal
    return weights, residual
```

```python
import functools

import jax
import jax.numpy as jnp
from jax import lax
from jax.experimental import pallas as pl
from jax.experimental.pallas import tpu as pltpu
from jax.sharding import PartitionSpec as P

BV = 64
BF = 64
DIRS = 96
ITERS = 5
LANES = 128
GROUP = 4
UNROLL = 4
PACK = BV * DIRS // LANES
HALF = BV // 2
QUART = BV // 4
VMEM_LIMIT = 48 * 1024 * 1024


def group_cap(slots, rows):
    groups = slots // GROUP + rows
    return -(-groups // UNROLL) * UNROLL


def lane_ids(rows):
    return lax.broadcasted_iota(jnp.int32, (rows, LANES), 1)


def setup_kernel(
    vox_rows,
    fas_rows,
    cap,
    rows_ref,
    cols_ref,
    count_ref,
    coef_ref,
    atom_ref,
    dict_ref,
    cp_ref,
    at_ref,
    a_ref,
    meta_ref,
    place_ref,
    slot_ref,
):
    slots = coef_ref.shape[0]
    live = count_ref[0]

    def clear_row(r, carry):
        place_ref[r] = 0
        return carry

    lax.fori_loop(0, vox_rows, clear_row, 0)

    def count_row(k, carry):
        r = lax.rem(rows_ref[k], vox_rows)
        place_ref[r] = place_ref[r] + 1
        return carry

    lax.fori_loop(0, live, count_row, 0)

    def clear_slot(p, carry):
        slot_ref[p] = -1
        meta_ref[p] = 0
        return carry

    lax.fori_loop(0, cap * GROUP, clear_slot, 0)

    def clear_group(q, carry):
        meta_ref[cap * GROUP + q] = 0
        return carry

    lax.fori_loop(0, cap, clear_group, 0)

    def place_row(r, start):
        groups = (place_ref[r] + GROUP - 1) // GROUP
        place_ref[r] = start * GROUP

        def name_group(q, carry):
            meta_ref[cap * GROUP + q] = r
            return carry

        lax.fori_loop(start, start + groups, name_group, 0)
        return start + groups

    total = lax.fori_loop(0, vox_rows, place_row, 0)
    turns = (total + UNROLL - 1) // UNROLL
    meta_ref[cap * (GROUP + 1)] = turns

    def place_slot(k, carry):
        r = lax.rem(rows_ref[k], vox_rows)
        p = place_ref[r]
        place_ref[r] = p + 1
        slot_ref[p] = k
        meta_ref[p] = lax.rem(cols_ref[k], fas_rows)
        return carry

    lax.fori_loop(0, live, place_slot, 0)

    atoms_pad = dict_ref.shape[1]
    left32 = lane_ids(HALF) < BF
    left1 = lane_ids(1) < BF
    atom_ids = lax.broadcasted_iota(jnp.int32, (atoms_pad, LANES), 0)

    def build(q, carry):
        tops, bottoms, marks = [], [], []
        for pair in range(GROUP // 2):
            s0 = slot_ref[q * GROUP + 2 * pair]
            s1 = slot_ref[q * GROUP + 2 * pair + 1]
            k0 = jnp.maximum(s0, 0)
            k1 = jnp.maximum(s1, 0)
            m0 = (s0 >= 0).astype(jnp.float32)
            m1 = (s1 >= 0).astype(jnp.float32)
            c0 = coef_ref[k0].astype(jnp.float32) * m0
            c1 = coef_ref[k1].astype(jnp.float32) * m1
            tops.append(jnp.where(left32, c0, pltpu.roll(c1, BF, 1)))
            bottoms.append(jnp.where(left32, pltpu.roll(c0, BF, 1), c1))
            ids = jnp.where(left1, atom_ref[pl.ds(k0, 1), :], atom_ref[pl.ds(k1, 1), :])
            marks.append((atom_ids == ids).astype(jnp.float32).astype(jnp.bfloat16))
        top = jnp.concatenate(tops, axis=1)
        bottom = jnp.concatenate(bottoms, axis=1)
        cp_ref[q] = jnp.concatenate([top, bottom], axis=0).astype(jnp.bfloat16)
        marked = jnp.concatenate(marks, axis=1)
        table = jnp.dot(dict_ref[...], marked, preferred_element_type=jnp.float32)
        at_ref[q] = table.astype(jnp.bfloat16)
        a_ref[q] = table.T.astype(jnp.bfloat16)
        return carry

    lax.fori_loop(0, turns * UNROLL, build, 0)


def spread_table(values, table_ref):
    rows = values.shape[0]
    left = lane_ids(rows) < BF
    turned = pltpu.roll(values, BF, 1)
    table_ref[pl.ds(0, rows, stride=2), :] = jnp.where(left, values, turned)
    table_ref[pl.ds(1, rows, stride=2), :] = jnp.where(left, turned, values)


def run_forward(cap, meta_ref, cp_ref, a_ref, table_ref, acc_ref):
    left = lane_ids(1) < BF

    def turn(t, carry):
        outs = []
        for n in range(UNROLL):
            q = t * UNROLL + n
            u = []
            for pair in range(GROUP // 2):
                p = q * GROUP + 2 * pair
                u0 = table_ref[pl.ds(meta_ref[p], 1), :]
                u1 = table_ref[pl.ds(meta_ref[p + 1], 1), :]
                u.append(jnp.where(left, u0, u1))
            scaled = cp_ref[q].astype(jnp.float32) * jnp.concatenate(u, axis=1)
            high = scaled.astype(jnp.bfloat16)
            low = (scaled - high.astype(jnp.float32)).astype(jnp.bfloat16)
            both = jnp.concatenate([high, low], axis=0)
            out = jnp.dot(both, a_ref[q], preferred_element_type=jnp.float32)
            outs.append(out[:BV] + out[BV:])
        for n in range(UNROLL):
            r = meta_ref[cap * GROUP + t * UNROLL + n]
            acc_ref[r] = acc_ref[r] + outs[n]
        return carry

    lax.fori_loop(0, meta_ref[cap * (GROUP + 1)], turn, 0)


def pack_rows(acc_ref, out_ref):
    lane = lane_ids(QUART)
    for r in range(acc_ref.shape[0]):
        last = acc_ref[r, 3 * QUART :, :]
        for i in range(3):
            tail = pltpu.roll(last, DIRS - 32 * i, 1)
            out_ref[pl.ds(r * PACK + i * QUART, QUART), :] = jnp.where(
                lane < DIRS, acc_ref[r, i * QUART : (i + 1) * QUART, :], tail
            )


def first_kernel(cap, meta_ref, w_ref, sig_ref, cp_ref, a_ref, out_ref, table_ref, acc_ref):
    spread_table(w_ref[...], table_ref)
    acc_ref[...] = sig_ref[...]
    run_forward(cap, meta_ref, cp_ref, a_ref, table_ref, acc_ref)
    pack_rows(acc_ref, out_ref)


def image_kernel(cap, meta_ref, g_ref, w_ref, cp_ref, a_ref, out_ref, p_ref, sq_ref, table_ref, acc_ref):
    gradient = g_ref[...]
    projected = jnp.where((w_ref[...] > 0) | (gradient < 0), gradient, 0.0)
    p_ref[...] = projected
    sq_ref[...] = jnp.sum((projected * projected).reshape(-1, 8, LANES), axis=0)
    spread_table(projected, table_ref)
    acc_ref[...] = jnp.zeros_like(acc_ref)
    run_forward(cap, meta_ref, cp_ref, a_ref, table_ref, acc_ref)
    pack_rows(acc_ref, out_ref)


def update_kernel(
    cap,
    vox_total,
    last,
    meta_ref,
    sums_ref,
    p_ref,
    w_ref,
    sig_ref,
    cp_ref,
    a_ref,
    out_ref,
    new_ref,
    table_ref,
    acc_ref,
):
    sums = jnp.sum(sums_ref[...], axis=0)
    upper = lax.broadcasted_iota(jnp.int32, (8, LANES), 0) < 4
    image_sq = jnp.sum(jnp.where(upper, sums, 0.0), keepdims=True)
    grad_sq = jnp.sum(jnp.where(upper, 0.0, sums), keepdims=True) * (1.0 / vox_total)
    step = grad_sq / (image_sq + 1e-6)
    updated = jnp.maximum(w_ref[...] - step * p_ref[...], 0.0)
    new_ref[...] = updated
    spread_table(updated, table_ref)
    acc_ref[...] = sig_ref[...]
    run_forward(cap, meta_ref, cp_ref, a_ref, table_ref, acc_ref)
    if last:
        out_ref[...] = acc_ref[...]
    else:
        pack_rows(acc_ref, out_ref)


def backward_kernel(cap, vox_rows, meta_ref, res_ref, cp_ref, at_ref, out_ref, split_ref, table_ref):
    lane = lane_ids(QUART)
    for r in range(vox_rows):
        packed = [res_ref[pl.ds(r * PACK + i * QUART, QUART), :] for i in range(3)]
        turned = [pltpu.roll(packed[i], 32 * (i + 1), 1) for i in range(3)]
        last = jnp.where(lane < 32, turned[0], jnp.where(lane < 64, turned[1], turned[2]))
        whole = jnp.concatenate(packed + [last], axis=0)
        whole = jnp.where(lane_ids(BV) < DIRS, whole, 0.0)
        high = whole.astype(jnp.bfloat16)
        low = (whole - high.astype(jnp.float32)).astype(jnp.bfloat16)
        split_ref[r] = jnp.concatenate([high, low], axis=0)
    table_ref[...] = jnp.zeros_like(table_ref)
    left = lane_ids(1) < BF

    def turn(t, carry):
        sums = []
        for n in range(UNROLL):
            q = t * UNROLL + n
            r = meta_ref[cap * GROUP + q]
            part = jnp.dot(split_ref[r], at_ref[q], preferred_element_type=jnp.float32)
            part = (part[:BV] + part[BV:]) * cp_ref[q].astype(jnp.float32)
            sums.append(jnp.sum(part, axis=0, keepdims=True))
        for n in range(UNROLL):
            for pair in range(GROUP // 2):
                p = (t * UNROLL + n) * GROUP + 2 * pair
                row = sums[n][:, pair * LANES : (pair + 1) * LANES]
                c0 = pl.ds(meta_ref[p], 1)
                table_ref[c0, :] = table_ref[c0, :] + jnp.where(left, row, 0.0)
                c1 = pl.ds(meta_ref[p + 1], 1)
                table_ref[c1, :] = table_ref[c1, :] + jnp.where(left, 0.0, row)
        return carry

    lax.fori_loop(0, meta_ref[cap * (GROUP + 1)], turn, 0)
    rows = out_ref.shape[0]
    even = table_ref[pl.ds(0, rows, stride=2), :]
    odd = table_ref[pl.ds(1, rows, stride=2), :]
    even = even + pltpu.roll(even, BF, 1)
    odd = odd + pltpu.roll(odd, BF, 1)
    out_ref[...] = jnp.where(lane_ids(rows) < BF, even, odd)


def call(kernel, outs, ins, scratch=()):
    spaces = {"v": pltpu.VMEM, "s": pltpu.SMEM}
    return pl.pallas_call(
        kernel,
        out_shape=tuple(jax.ShapeDtypeStruct(shape, dtype) for shape, dtype, _ in outs),
        in_specs=[pl.BlockSpec(memory_space=spaces[kind]) for kind in ins],
        out_specs=tuple(pl.BlockSpec(memory_space=spaces[kind]) for _, _, kind in outs),
        scratch_shapes=list(scratch),
        compiler_params=pltpu.CompilerParams(vmem_limit_bytes=VMEM_LIMIT),
    )


def local(
    n_vox,
    n_fas,
    signal,
    initial_weights,
    coefficients,
    block_rows,
    block_cols,
    block_atoms,
    block_count,
    dictionary,
):
    f32, bf16, i32 = jnp.float32, jnp.bfloat16, jnp.int32
    vox_rows = signal.shape[0]
    fas_rows = initial_weights.shape[0] // BF
    slots = coefficients.shape[0]
    cap = group_cap(slots, vox_rows)
    atoms = dictionary.shape[0]
    atoms_pad = -(-atoms // LANES) * LANES
    meta_size = -(-(cap * (GROUP + 1) + 1) // LANES) * LANES
    wide = GROUP * BF
    half_rows = fas_rows // 2

    coef_view = coefficients.reshape(slots, HALF, LANES)
    atom_view = jnp.concatenate([block_atoms, block_atoms], axis=1)
    dict_t = jnp.pad(dictionary.T, ((0, LANES - DIRS), (0, atoms_pad - atoms)))

    cp, at, a, meta = call(
        functools.partial(setup_kernel, vox_rows, fas_rows, cap),
        [
            ((cap, BV, wide), bf16, "v"),
            ((cap, LANES, wide), bf16, "v"),
            ((cap, wide, LANES), bf16, "v"),
            ((meta_size,), i32, "s"),
        ],
        "sssvvv",
        [pltpu.SMEM((vox_rows,), i32), pltpu.SMEM((cap * GROUP,), i32)],
    )(block_rows, block_cols, block_count, coef_view, atom_view, dict_t)

    own = signal.shape[1] // DIRS // 2
    fas_place = lax.axis_index("fas")
    negative = -signal.reshape(vox_rows, own, 2, DIRS).transpose(0, 2, 1, 3)
    negative = jnp.pad(negative, ((0, 0), (0, 0), (0, 0), (0, LANES - DIRS)))
    sig = lax.dynamic_update_slice(
        jnp.zeros((vox_rows, 2, HALF, LANES), f32), negative, (0, 0, fas_place * own, 0)
    ).reshape(vox_rows, BV, LANES)

    image_rows = vox_rows * PACK
    table = pltpu.VMEM((fas_rows, LANES), f32)
    acc = pltpu.VMEM((vox_rows, BV, LANES), f32)
    image_out = ((image_rows, LANES), f32, "v")
    flat_out = ((half_rows, LANES), f32, "v")

    def swap(x, axis):
        return lax.all_to_all(x, axis, 0, 0)

    def collect(partial):
        shares = swap(partial.reshape(n_fas, image_rows // n_fas, LANES), "fas")
        return jnp.sum(shares, axis=0)

    weights = initial_weights.reshape(half_rows, LANES)
    (partial,) = call(
        functools.partial(first_kernel, cap), [image_out], "svvvv", [table, acc]
    )(meta, weights, sig, cp, a)
    for sweep in range(ITERS):
        last = sweep == ITERS - 1
        residual = collect(partial)
        whole = swap(jnp.broadcast_to(residual[None], (n_fas,) + residual.shape), "fas")
        (gradient,) = call(
            functools.partial(backward_kernel, cap, vox_rows),
            [flat_out],
            "svvv",
            [pltpu.VMEM((vox_rows, 2 * BV, LANES), bf16), table],
        )(meta, whole.reshape(image_rows, LANES), cp, at)
        bit = 1
        while bit < n_vox:
            gradient = gradient + lax.ppermute(
                gradient, "vox", [(i, i ^ bit) for i in range(n_vox)]
            )
            bit *= 2
        partial, projected, proj_sq = call(
            functools.partial(image_kernel, cap),
            [image_out, flat_out, ((8, LANES), f32, "v")],
            "svvvv",
            [table, acc],
        )(meta, gradient, weights, cp, a)
        image = collect(partial)
        image_sq = jnp.sum((image * image).reshape(-1, 4, LANES), axis=0)
        proj_sq = proj_sq[:4] + proj_sq[4:]
        sums = jnp.concatenate([image_sq, proj_sq], axis=0)
        sums = swap(jnp.broadcast_to(sums[None], (n_vox * n_fas, 8, LANES)), ("vox", "fas"))
        out = ((vox_rows, BV, LANES), f32, "v") if last else image_out
        partial, weights = call(
            functools.partial(update_kernel, cap, n_vox, last),
            [out, flat_out],
            "svvvvvv",
            [table, acc],
        )(meta, sums, projected, weights, sig, cp, a)
    final = partial.reshape(vox_rows, 2, n_fas, own, LANES)[..., :DIRS].transpose(2, 0, 3, 1, 4)
    final = swap(final.reshape(n_fas, vox_rows, own * 2 * DIRS), "fas")
    return (weights.reshape(-1), jnp.sum(final, axis=0))


def solution(mesh):
    placed = (
        P("vox", "fas"),
        P("fas"),
        P(("vox", "fas"), None),
        P(("vox", "fas")),
        P(("vox", "fas")),
        P(("vox", "fas"), None),
        P(("vox", "fas")),
        P(),
    )
    return jax.shard_map(
        functools.partial(local, mesh.shape["vox"], mesh.shape["fas"]),
        mesh=mesh,
        in_specs=placed,
        out_specs=(P("fas"), P("vox", "fas")),
        check_vma=False,
    )
```

```python
import functools

import jax
import jax.numpy as jnp
from jax import lax
from jax.experimental import pallas as pl
from jax.experimental.pallas import tpu as pltpu
from jax.sharding import PartitionSpec as P

BV = 64
BF = 64
DIRS = 96
ITERS = 5
LANES = 128
GROUP = 4
UNROLL = 4
PACK = BV * DIRS // LANES
HALF = BV // 2
QUART = BV // 4
VMEM_LIMIT = 16 * 1024 * 1024


def group_cap(slots, rows):
    groups = slots // GROUP + rows
    return -(-groups // UNROLL) * UNROLL


def lane_ids(rows):
    return lax.broadcasted_iota(jnp.int32, (rows, LANES), 1)


def setup_kernel(
    vox_rows,
    fas_rows,
    cap,
    rows_ref,
    cols_ref,
    count_ref,
    coef_ref,
    atom_ref,
    dict_ref,
    cp_ref,
    at_ref,
    a_ref,
    meta_ref,
    place_ref,
    slot_ref,
):
    slots = coef_ref.shape[0]
    live = count_ref[0]

    def clear_row(r, carry):
        place_ref[r] = 0
        return carry

    lax.fori_loop(0, vox_rows, clear_row, 0)

    def count_row(k, carry):
        r = lax.rem(rows_ref[k], vox_rows)
        place_ref[r] = place_ref[r] + 1
        return carry

    lax.fori_loop(0, live, count_row, 0)

    def clear_slot(p, carry):
        slot_ref[p] = -1
        meta_ref[p] = 0
        return carry

    lax.fori_loop(0, cap * GROUP, clear_slot, 0)

    def clear_group(q, carry):
        meta_ref[cap * GROUP + q] = 0
        return carry

    lax.fori_loop(0, cap, clear_group, 0)

    def place_row(r, start):
        groups = (place_ref[r] + GROUP - 1) // GROUP
        place_ref[r] = start * GROUP

        def name_group(q, carry):
            meta_ref[cap * GROUP + q] = r
            return carry

        lax.fori_loop(start, start + groups, name_group, 0)
        return start + groups

    total = lax.fori_loop(0, vox_rows, place_row, 0)
    turns = (total + UNROLL - 1) // UNROLL
    meta_ref[cap * (GROUP + 1)] = turns

    def place_slot(k, carry):
        r = lax.rem(rows_ref[k], vox_rows)
        p = place_ref[r]
        place_ref[r] = p + 1
        slot_ref[p] = k
        meta_ref[p] = lax.rem(cols_ref[k], fas_rows)
        return carry

    lax.fori_loop(0, live, place_slot, 0)

    atoms_pad = dict_ref.shape[1]
    left32 = lane_ids(HALF) < BF
    left1 = lane_ids(1) < BF
    atom_ids = lax.broadcasted_iota(jnp.int32, (atoms_pad, LANES), 0)

    def build(q, carry):
        tops, bottoms, marks = [], [], []
        for pair in range(GROUP // 2):
            s0 = slot_ref[q * GROUP + 2 * pair]
            s1 = slot_ref[q * GROUP + 2 * pair + 1]
            k0 = jnp.maximum(s0, 0)
            k1 = jnp.maximum(s1, 0)
            m0 = (s0 >= 0).astype(jnp.float32)
            m1 = (s1 >= 0).astype(jnp.float32)
            c0 = coef_ref[k0].astype(jnp.float32) * m0
            c1 = coef_ref[k1].astype(jnp.float32) * m1
            tops.append(jnp.where(left32, c0, pltpu.roll(c1, BF, 1)))
            bottoms.append(jnp.where(left32, pltpu.roll(c0, BF, 1), c1))
            ids = jnp.where(left1, atom_ref[pl.ds(k0, 1), :], atom_ref[pl.ds(k1, 1), :])
            marks.append((atom_ids == ids).astype(jnp.float32).astype(jnp.bfloat16))
        top = jnp.concatenate(tops, axis=1)
        bottom = jnp.concatenate(bottoms, axis=1)
        cp_ref[q] = jnp.concatenate([top, bottom], axis=0).astype(jnp.bfloat16)
        marked = jnp.concatenate(marks, axis=1)
        table = jnp.dot(dict_ref[...], marked, preferred_element_type=jnp.float32)
        at_ref[q] = table.astype(jnp.bfloat16)
        a_ref[q] = table.T.astype(jnp.bfloat16)
        return carry

    lax.fori_loop(0, turns * UNROLL, build, 0)


def spread_table(values, table_ref):
    rows = values.shape[0]
    left = lane_ids(rows) < BF
    turned = pltpu.roll(values, BF, 1)
    table_ref[pl.ds(0, rows, stride=2), :] = jnp.where(left, values, turned)
    table_ref[pl.ds(1, rows, stride=2), :] = jnp.where(left, turned, values)


def run_forward(cap, meta_ref, cp_ref, a_ref, table_ref, acc_ref):
    left = lane_ids(1) < BF

    def turn(t, carry):
        outs = []
        for n in range(UNROLL):
            q = t * UNROLL + n
            u = []
            for pair in range(GROUP // 2):
                p = q * GROUP + 2 * pair
                u0 = table_ref[pl.ds(meta_ref[p], 1), :]
                u1 = table_ref[pl.ds(meta_ref[p + 1], 1), :]
                u.append(jnp.where(left, u0, u1))
            scaled = cp_ref[q].astype(jnp.float32) * jnp.concatenate(u, axis=1)
            high = scaled.astype(jnp.bfloat16)
            low = (scaled - high.astype(jnp.float32)).astype(jnp.bfloat16)
            both = jnp.concatenate([high, low], axis=0)
            out = jnp.dot(both, a_ref[q], preferred_element_type=jnp.float32)
            outs.append(out[:BV] + out[BV:])
        for n in range(UNROLL):
            r = meta_ref[cap * GROUP + t * UNROLL + n]
            acc_ref[r] = acc_ref[r] + outs[n]
        return carry

    lax.fori_loop(0, meta_ref[cap * (GROUP + 1)], turn, 0)


def pack_rows(acc_ref, out_ref):
    lane = lane_ids(QUART)
    for r in range(acc_ref.shape[0]):
        last = acc_ref[r, 3 * QUART :, :]
        for i in range(3):
            tail = pltpu.roll(last, DIRS - 32 * i, 1)
            out_ref[pl.ds(r * PACK + i * QUART, QUART), :] = jnp.where(
                lane < DIRS, acc_ref[r, i * QUART : (i + 1) * QUART, :], tail
            )


def first_kernel(cap, meta_ref, w_ref, sig_ref, cp_ref, a_ref, out_ref, table_ref, acc_ref):
    spread_table(w_ref[...], table_ref)
    acc_ref[...] = sig_ref[...]
    run_forward(cap, meta_ref, cp_ref, a_ref, table_ref, acc_ref)
    pack_rows(acc_ref, out_ref)


def image_kernel(cap, meta_ref, g_ref, w_ref, cp_ref, a_ref, out_ref, p_ref, sq_ref, table_ref, acc_ref):
    gradient = g_ref[...]
    projected = jnp.where((w_ref[...] > 0) | (gradient < 0), gradient, 0.0)
    p_ref[...] = projected
    sq_ref[...] = jnp.sum((projected * projected).reshape(-1, 8, LANES), axis=0)
    spread_table(projected, table_ref)
    acc_ref[...] = jnp.zeros_like(acc_ref)
    run_forward(cap, meta_ref, cp_ref, a_ref, table_ref, acc_ref)
    pack_rows(acc_ref, out_ref)


def update_kernel(
    cap,
    vox_total,
    last,
    meta_ref,
    sums_ref,
    p_ref,
    w_ref,
    sig_ref,
    cp_ref,
    a_ref,
    out_ref,
    new_ref,
    table_ref,
    acc_ref,
):
    sums = jnp.sum(sums_ref[...], axis=0)
    upper = lax.broadcasted_iota(jnp.int32, (8, LANES), 0) < 4
    image_sq = jnp.sum(jnp.where(upper, sums, 0.0), keepdims=True)
    grad_sq = jnp.sum(jnp.where(upper, 0.0, sums), keepdims=True) * (1.0 / vox_total)
    step = grad_sq / (image_sq + 1e-6)
    updated = jnp.maximum(w_ref[...] - step * p_ref[...], 0.0)
    new_ref[...] = updated
    spread_table(updated, table_ref)
    acc_ref[...] = sig_ref[...]
    run_forward(cap, meta_ref, cp_ref, a_ref, table_ref, acc_ref)
    if last:
        out_ref[...] = acc_ref[...]
    else:
        pack_rows(acc_ref, out_ref)


def backward_kernel(cap, vox_rows, meta_ref, res_ref, cp_ref, at_ref, out_ref, split_ref, table_ref):
    lane = lane_ids(QUART)
    for r in range(vox_rows):
        packed = [res_ref[pl.ds(r * PACK + i * QUART, QUART), :] for i in range(3)]
        turned = [pltpu.roll(packed[i], 32 * (i + 1), 1) for i in range(3)]
        last = jnp.where(lane < 32, turned[0], jnp.where(lane < 64, turned[1], turned[2]))
        whole = jnp.concatenate(packed + [last], axis=0)
        whole = jnp.where(lane_ids(BV) < DIRS, whole, 0.0)
        high = whole.astype(jnp.bfloat16)
        low = (whole - high.astype(jnp.float32)).astype(jnp.bfloat16)
        split_ref[r] = jnp.concatenate([high, low], axis=0)
    table_ref[...] = jnp.zeros_like(table_ref)
    left = lane_ids(1) < BF

    def turn(t, carry):
        sums = []
        for n in range(UNROLL):
            q = t * UNROLL + n
            r = meta_ref[cap * GROUP + q]
            part = jnp.dot(split_ref[r], at_ref[q], preferred_element_type=jnp.float32)
            part = (part[:BV] + part[BV:]) * cp_ref[q].astype(jnp.float32)
            sums.append(jnp.sum(part, axis=0, keepdims=True))
        for n in range(UNROLL):
            for pair in range(GROUP // 2):
                p = (t * UNROLL + n) * GROUP + 2 * pair
                row = sums[n][:, pair * LANES : (pair + 1) * LANES]
                c0 = pl.ds(meta_ref[p], 1)
                table_ref[c0, :] = table_ref[c0, :] + jnp.where(left, row, 0.0)
                c1 = pl.ds(meta_ref[p + 1], 1)
                table_ref[c1, :] = table_ref[c1, :] + jnp.where(left, 0.0, row)
        return carry

    lax.fori_loop(0, meta_ref[cap * (GROUP + 1)], turn, 0)
    rows = out_ref.shape[0]
    even = table_ref[pl.ds(0, rows, stride=2), :]
    odd = table_ref[pl.ds(1, rows, stride=2), :]
    even = even + pltpu.roll(even, BF, 1)
    odd = odd + pltpu.roll(odd, BF, 1)
    out_ref[...] = jnp.where(lane_ids(rows) < BF, even, odd)


def share_kernel(shares_ref, out_ref):
    total = jnp.sum(shares_ref[...], axis=0)
    for i in range(out_ref.shape[0]):
        out_ref[i] = total


def norm_kernel(shares_ref, sq_ref, out_ref):
    image = jnp.sum(shares_ref[...], axis=0)
    image_sq = jnp.sum((image * image).reshape(-1, 8, LANES), axis=0)
    sums = jnp.concatenate([image_sq[:4] + image_sq[4:], sq_ref[:4] + sq_ref[4:]], axis=0)

    def copy_out(i, carry):
        out_ref[i] = sums
        return carry

    lax.fori_loop(0, out_ref.shape[0], copy_out, 0)


def call(kernel, outs, ins, scratch=()):
    spaces = {"v": pltpu.VMEM, "s": pltpu.SMEM}
    run = pl.pallas_call(
        kernel,
        out_shape=tuple(
            pltpu.VMEM(shape, dtype) if kind == "v" else jax.ShapeDtypeStruct(shape, dtype)
            for shape, dtype, kind in outs
        ),
        in_specs=[pl.BlockSpec(memory_space=spaces[kind]) for kind in ins],
        out_specs=tuple(pl.BlockSpec(memory_space=spaces[kind]) for _, _, kind in outs),
        scratch_shapes=list(scratch),
        compiler_params=pltpu.CompilerParams(vmem_limit_bytes=VMEM_LIMIT),
    )

    def placed(*args):
        return run(
            *(
                pltpu.with_memory_space_constraint(x, pltpu.VMEM) if kind == "v" else x
                for x, kind in zip(args, ins)
            )
        )

    return placed


def local(
    n_vox,
    n_fas,
    signal,
    initial_weights,
    coefficients,
    block_rows,
    block_cols,
    block_atoms,
    block_count,
    dictionary,
):
    f32, bf16, i32 = jnp.float32, jnp.bfloat16, jnp.int32
    vox_rows = signal.shape[0]
    fas_rows = initial_weights.shape[0] // BF
    slots = coefficients.shape[0]
    cap = group_cap(slots, vox_rows)
    atoms = dictionary.shape[0]
    atoms_pad = -(-atoms // LANES) * LANES
    meta_size = -(-(cap * (GROUP + 1) + 1) // LANES) * LANES
    wide = GROUP * BF
    half_rows = fas_rows // 2

    coef_view = coefficients.reshape(slots, HALF, LANES)
    atom_view = jnp.concatenate([block_atoms, block_atoms], axis=1)
    dict_t = jnp.pad(dictionary.T, ((0, LANES - DIRS), (0, atoms_pad - atoms)))

    cp, at, a, meta = call(
        functools.partial(setup_kernel, vox_rows, fas_rows, cap),
        [
            ((cap, BV, wide), bf16, "v"),
            ((cap, LANES, wide), bf16, "v"),
            ((cap, wide, LANES), bf16, "v"),
            ((meta_size,), i32, "s"),
        ],
        "sssvvv",
        [pltpu.SMEM((vox_rows,), i32), pltpu.SMEM((cap * GROUP,), i32)],
    )(block_rows, block_cols, block_count, coef_view, atom_view, dict_t)

    own = signal.shape[1] // DIRS // 2
    fas_place = lax.axis_index("fas")
    negative = -signal.reshape(vox_rows, own, 2, DIRS).transpose(0, 2, 1, 3)
    negative = jnp.pad(negative, ((0, 0), (0, 0), (0, 0), (0, LANES - DIRS)))
    sig = lax.dynamic_update_slice(
        jnp.zeros((vox_rows, 2, HALF, LANES), f32), negative, (0, 0, fas_place * own, 0)
    ).reshape(vox_rows, BV, LANES)

    image_rows = vox_rows * PACK
    table = pltpu.VMEM((fas_rows, LANES), f32)
    acc = pltpu.VMEM((vox_rows, BV, LANES), f32)
    image_out = ((image_rows, LANES), f32, "v")
    flat_out = ((half_rows, LANES), f32, "v")

    def swap(x, axis):
        return lax.all_to_all(x, axis, 0, 0)

    share_rows = image_rows // n_fas

    def collect(partial):
        return swap(partial.reshape(n_fas, share_rows, LANES), "fas")

    weights = initial_weights.reshape(half_rows, LANES)
    (partial,) = call(
        functools.partial(first_kernel, cap), [image_out], "svvvv", [table, acc]
    )(meta, weights, sig, cp, a)
    for sweep in range(ITERS):
        last = sweep == ITERS - 1
        (residual,) = call(share_kernel, [((n_fas, share_rows, LANES), f32, "v")], "v")(
            collect(partial)
        )
        whole = swap(residual, "fas")
        (gradient,) = call(
            functools.partial(backward_kernel, cap, vox_rows),
            [flat_out],
            "svvv",
            [pltpu.VMEM((vox_rows, 2 * BV, LANES), bf16), table],
        )(meta, whole.reshape(image_rows, LANES), cp, at)
        bit = 1
        while bit < n_vox:
            gradient = gradient + lax.ppermute(
                gradient, "vox", [(i, i ^ bit) for i in range(n_vox)]
            )
            bit *= 2
        partial, projected, proj_sq = call(
            functools.partial(image_kernel, cap),
            [image_out, flat_out, ((8, LANES), f32, "v")],
            "svvvv",
            [table, acc],
        )(meta, gradient, weights, cp, a)
        (sums,) = call(norm_kernel, [((n_vox * n_fas, 8, LANES), f32, "v")], "vv")(
            collect(partial), proj_sq
        )
        sums = swap(sums, ("vox", "fas"))
        out = ((vox_rows, BV, LANES), f32, "v") if last else image_out
        partial, weights = call(
            functools.partial(update_kernel, cap, n_vox, last),
            [out, flat_out],
            "svvvvvv",
            [table, acc],
        )(meta, sums, projected, weights, sig, cp, a)
    final = partial.reshape(vox_rows, 2, n_fas, own, LANES)[..., :DIRS].transpose(2, 0, 3, 1, 4)
    final = swap(final.reshape(n_fas, vox_rows, own * 2 * DIRS), "fas")
    return (weights.reshape(-1), jnp.sum(final, axis=0))


def solution(mesh):
    placed = (
        P("vox", "fas"),
        P("fas"),
        P(("vox", "fas"), None),
        P(("vox", "fas")),
        P(("vox", "fas")),
        P(("vox", "fas"), None),
        P(("vox", "fas")),
        P(),
    )
    return jax.shard_map(
        functools.partial(local, mesh.shape["vox"], mesh.shape["fas"]),
        mesh=mesh,
        in_specs=placed,
        out_specs=(P("fas"), P("vox", "fas")),
        check_vma=False,
    )
```

```python
import functools

import jax
import jax.numpy as jnp
from jax import lax
from jax.experimental import pallas as pl
from jax.experimental.pallas import tpu as pltpu
from jax.sharding import PartitionSpec as P

BV = 64
BF = 64
DIRS = 96
ITERS = 5
LANES = 128
GROUP = 4
BUILD = 8
UNROLL = 40
PACK = BV * DIRS // LANES
HALF = BV // 2
QUART = BV // 4
VMEM_LIMIT = 16 * 1024 * 1024


def group_cap(slots, rows):
    groups = slots // GROUP + rows
    return -(-groups // UNROLL) * UNROLL


def lane_ids(rows):
    return lax.broadcasted_iota(jnp.int32, (rows, LANES), 1)


def setup_kernel(slot_ref, turns_ref, coef_ref, atom_ref, dict_ref, cp_ref, at_ref, a_ref):
    atoms_pad = dict_ref.shape[1]
    left32 = lane_ids(HALF) < BF
    left1 = lane_ids(1) < BF
    atom_ids = lax.broadcasted_iota(jnp.int32, (atoms_pad, LANES), 0)

    def build(q):
        tops, bottoms, marks = [], [], []
        for pair in range(GROUP // 2):
            s0 = slot_ref[q * GROUP + 2 * pair]
            s1 = slot_ref[q * GROUP + 2 * pair + 1]
            k0 = jnp.maximum(s0, 0)
            k1 = jnp.maximum(s1, 0)
            m0 = (s0 >= 0).astype(jnp.float32)
            m1 = (s1 >= 0).astype(jnp.float32)
            c0 = coef_ref[k0].astype(jnp.float32) * m0
            c1 = coef_ref[k1].astype(jnp.float32) * m1
            tops.append(jnp.where(left32, c0, pltpu.roll(c1, BF, 1)))
            bottoms.append(jnp.where(left32, pltpu.roll(c0, BF, 1), c1))
            ids = jnp.where(left1, atom_ref[pl.ds(k0, 1), :], atom_ref[pl.ds(k1, 1), :])
            marks.append((atom_ids == ids).astype(jnp.float32).astype(jnp.bfloat16))
        top = jnp.concatenate(tops, axis=1)
        bottom = jnp.concatenate(bottoms, axis=1)
        cp_ref[q] = jnp.concatenate([top, bottom], axis=0).astype(jnp.bfloat16)
        marked = jnp.concatenate(marks, axis=1)
        table = jnp.dot(dict_ref[...], marked, preferred_element_type=jnp.float32)
        at_ref[q] = table.astype(jnp.bfloat16)
        a_ref[q] = table.T.astype(jnp.bfloat16)

    def turn(t, carry):
        for n in range(BUILD):
            build(t * BUILD + n)
        return carry

    lax.fori_loop(0, turns_ref[0] * (UNROLL // BUILD), turn, 0)


def sort_slots(rows, cols, count, vox_rows, cap):
    i32 = jnp.int32
    slots = rows.shape[0]
    k = jnp.arange(slots, dtype=i32)
    rows = jnp.where(k < count, rows, vox_rows)
    r = jnp.arange(vox_rows, dtype=i32)
    member = rows[:, None] == r[None, :]
    groups = (jnp.sum(member.astype(i32), axis=0) + GROUP - 1) // GROUP
    start = jnp.sum(jnp.where(r[:, None] < r[None, :], groups[:, None], 0), axis=0)
    total = jnp.sum(groups)
    before = (rows[:, None] == rows[None, :]) & (k[None, :] < k[:, None])
    rank = jnp.sum(before.astype(i32), axis=1)
    first = jnp.sum(jnp.where(member, start[None, :], 0), axis=1)
    place = jnp.where(rows < vox_rows, first * GROUP + rank, -1)
    chosen = jnp.arange(cap * GROUP, dtype=i32)[:, None] == place[None, :]
    slot = jnp.sum(jnp.where(chosen, k[None, :] + 1, 0), axis=1) - 1
    col = jnp.sum(jnp.where(chosen, cols[None, :], 0), axis=1)
    q = jnp.arange(cap, dtype=i32)
    row = jnp.sum((start[None, :] <= q[:, None]).astype(i32), axis=1) - 1
    turns = (total + UNROLL - 1) // UNROLL
    return slot, jnp.concatenate([col, row, turns[None]]), turns[None]


def spread_table(values, table_ref):
    rows = values.shape[0]
    left = lane_ids(rows) < BF
    turned = pltpu.roll(values, BF, 1)
    table_ref[pl.ds(0, rows, stride=2), :] = jnp.where(left, values, turned)
    table_ref[pl.ds(1, rows, stride=2), :] = jnp.where(left, turned, values)


def run_forward(cap, meta_ref, cp_ref, a_ref, table_ref, acc_ref):
    left = lane_ids(1) < BF

    def turn(t, carry):
        outs = []
        for n in range(UNROLL):
            q = t * UNROLL + n
            u = []
            for pair in range(GROUP // 2):
                p = q * GROUP + 2 * pair
                u0 = table_ref[pl.ds(meta_ref[p], 1), :]
                u1 = table_ref[pl.ds(meta_ref[p + 1], 1), :]
                u.append(jnp.where(left, u0, u1))
            scaled = cp_ref[q].astype(jnp.float32) * jnp.concatenate(u, axis=1)
            high = scaled.astype(jnp.bfloat16)
            low = (scaled - high.astype(jnp.float32)).astype(jnp.bfloat16)
            both = jnp.concatenate([high, low], axis=0)
            out = jnp.dot(both, a_ref[q], preferred_element_type=jnp.float32)
            outs.append(out[:BV] + out[BV:])
        for n in range(UNROLL):
            r = meta_ref[cap * GROUP + t * UNROLL + n]
            acc_ref[r] = acc_ref[r] + outs[n]
        return carry

    lax.fori_loop(0, meta_ref[cap * (GROUP + 1)], turn, 0)


def pack_rows(acc_ref, out_ref):
    lane = lane_ids(QUART)
    for r in range(acc_ref.shape[0]):
        last = acc_ref[r, 3 * QUART :, :]
        for i in range(3):
            tail = pltpu.roll(last, DIRS - 32 * i, 1)
            out_ref[pl.ds(r * PACK + i * QUART, QUART), :] = jnp.where(
                lane < DIRS, acc_ref[r, i * QUART : (i + 1) * QUART, :], tail
            )


def first_kernel(cap, meta_ref, w_ref, sig_ref, cp_ref, a_ref, out_ref, table_ref, acc_ref):
    spread_table(w_ref[...], table_ref)
    acc_ref[...] = sig_ref[...]
    run_forward(cap, meta_ref, cp_ref, a_ref, table_ref, acc_ref)
    pack_rows(acc_ref, out_ref)


def image_kernel(cap, meta_ref, g_ref, w_ref, cp_ref, a_ref, out_ref, p_ref, sq_ref, table_ref, acc_ref):
    gradient = g_ref[...]
    projected = jnp.where((w_ref[...] > 0) | (gradient < 0), gradient, 0.0)
    p_ref[...] = projected
    sq_ref[...] = jnp.sum((projected * projected).reshape(-1, 8, LANES), axis=0)
    spread_table(projected, table_ref)
    acc_ref[...] = jnp.zeros_like(acc_ref)
    run_forward(cap, meta_ref, cp_ref, a_ref, table_ref, acc_ref)
    pack_rows(acc_ref, out_ref)


def update_kernel(
    cap,
    vox_total,
    last,
    meta_ref,
    sums_ref,
    p_ref,
    w_ref,
    sig_ref,
    cp_ref,
    a_ref,
    out_ref,
    new_ref,
    table_ref,
    acc_ref,
):
    sums = jnp.sum(sums_ref[...], axis=0)
    upper = lax.broadcasted_iota(jnp.int32, (8, LANES), 0) < 4
    image_sq = jnp.sum(jnp.where(upper, sums, 0.0), keepdims=True)
    grad_sq = jnp.sum(jnp.where(upper, 0.0, sums), keepdims=True) * (1.0 / vox_total)
    step = grad_sq / (image_sq + 1e-6)
    updated = jnp.maximum(w_ref[...] - step * p_ref[...], 0.0)
    new_ref[...] = updated
    spread_table(updated, table_ref)
    acc_ref[...] = sig_ref[...]
    run_forward(cap, meta_ref, cp_ref, a_ref, table_ref, acc_ref)
    if last:
        out_ref[...] = acc_ref[...]
    else:
        pack_rows(acc_ref, out_ref)


def backward_kernel(cap, vox_rows, meta_ref, res_ref, cp_ref, at_ref, out_ref, split_ref, table_ref):
    lane = lane_ids(QUART)
    for r in range(vox_rows):
        packed = [res_ref[pl.ds(r * PACK + i * QUART, QUART), :] for i in range(3)]
        turned = [pltpu.roll(packed[i], 32 * (i + 1), 1) for i in range(3)]
        last = jnp.where(lane < 32, turned[0], jnp.where(lane < 64, turned[1], turned[2]))
        whole = jnp.concatenate(packed + [last], axis=0)
        whole = jnp.where(lane_ids(BV) < DIRS, whole, 0.0)
        high = whole.astype(jnp.bfloat16)
        low = (whole - high.astype(jnp.float32)).astype(jnp.bfloat16)
        split_ref[r] = jnp.concatenate([high, low], axis=0)
    table_ref[...] = jnp.zeros_like(table_ref)
    left = lane_ids(1) < BF

    def turn(t, carry):
        sums = []
        for n in range(UNROLL):
            q = t * UNROLL + n
            r = meta_ref[cap * GROUP + q]
            part = jnp.dot(split_ref[r], at_ref[q], preferred_element_type=jnp.float32)
            part = (part[:BV] + part[BV:]) * cp_ref[q].astype(jnp.float32)
            sums.append(jnp.sum(part, axis=0, keepdims=True))
        for n in range(UNROLL):
            for pair in range(GROUP // 2):
                p = (t * UNROLL + n) * GROUP + 2 * pair
                row = sums[n][:, pair * LANES : (pair + 1) * LANES]
                c0 = pl.ds(meta_ref[p], 1)
                table_ref[c0, :] = table_ref[c0, :] + jnp.where(left, row, 0.0)
                c1 = pl.ds(meta_ref[p + 1], 1)
                table_ref[c1, :] = table_ref[c1, :] + jnp.where(left, 0.0, row)
        return carry

    lax.fori_loop(0, meta_ref[cap * (GROUP + 1)], turn, 0)
    rows = out_ref.shape[0]
    even = table_ref[pl.ds(0, rows, stride=2), :]
    odd = table_ref[pl.ds(1, rows, stride=2), :]
    even = even + pltpu.roll(even, BF, 1)
    odd = odd + pltpu.roll(odd, BF, 1)
    out_ref[...] = jnp.where(lane_ids(rows) < BF, even, odd)


def share_kernel(shares_ref, out_ref):
    total = jnp.sum(shares_ref[...], axis=0)
    for i in range(out_ref.shape[0]):
        out_ref[i] = total


def norm_kernel(shares_ref, sq_ref, out_ref):
    image = jnp.sum(shares_ref[...], axis=0)
    image_sq = jnp.sum((image * image).reshape(-1, 8, LANES), axis=0)
    sums = jnp.concatenate([image_sq[:4] + image_sq[4:], sq_ref[:4] + sq_ref[4:]], axis=0)

    def copy_out(i, carry):
        out_ref[i] = sums
        return carry

    lax.fori_loop(0, out_ref.shape[0], copy_out, 0)


def call(kernel, outs, ins, scratch=()):
    spaces = {"v": pltpu.VMEM, "s": pltpu.SMEM}
    run = pl.pallas_call(
        kernel,
        out_shape=tuple(
            pltpu.VMEM(shape, dtype) if kind == "v" else jax.ShapeDtypeStruct(shape, dtype)
            for shape, dtype, kind in outs
        ),
        in_specs=[pl.BlockSpec(memory_space=spaces[kind]) for kind in ins],
        out_specs=tuple(pl.BlockSpec(memory_space=spaces[kind]) for _, _, kind in outs),
        scratch_shapes=list(scratch),
        compiler_params=pltpu.CompilerParams(vmem_limit_bytes=VMEM_LIMIT),
    )

    def placed(*args):
        return run(
            *(
                pltpu.with_memory_space_constraint(x, pltpu.VMEM) if kind == "v" else x
                for x, kind in zip(args, ins)
            )
        )

    return placed


def local(
    n_vox,
    n_fas,
    signal,
    initial_weights,
    coefficients,
    block_rows,
    block_cols,
    block_atoms,
    block_count,
    dictionary,
):
    f32, bf16, i32 = jnp.float32, jnp.bfloat16, jnp.int32
    vox_rows = signal.shape[0]
    fas_rows = initial_weights.shape[0] // BF
    slots = coefficients.shape[0]
    cap = group_cap(slots, vox_rows)
    atoms = dictionary.shape[0]
    atoms_pad = -(-atoms // LANES) * LANES
    wide = GROUP * BF
    half_rows = fas_rows // 2

    coef_view = coefficients.reshape(slots, HALF, LANES)
    atom_view = jnp.concatenate([block_atoms, block_atoms], axis=1)
    dict_t = jnp.pad(dictionary.T, ((0, LANES - DIRS), (0, atoms_pad - atoms)))
    fas_place = lax.axis_index("fas")
    slot, meta, turns = sort_slots(
        block_rows - lax.axis_index("vox") * vox_rows,
        block_cols - fas_place * fas_rows,
        block_count[0],
        vox_rows,
        cap,
    )
    cp, at, a = call(
        setup_kernel,
        [
            ((cap, BV, wide), bf16, "v"),
            ((cap, LANES, wide), bf16, "v"),
            ((cap, wide, LANES), bf16, "v"),
        ],
        "ssvvv",
    )(slot, turns, coef_view, atom_view, dict_t)

    own = signal.shape[1] // DIRS // 2
    negative = -signal.reshape(vox_rows, own, 2, DIRS).transpose(0, 2, 1, 3)
    negative = jnp.pad(negative, ((0, 0), (0, 0), (0, 0), (0, LANES - DIRS)))
    sig = lax.dynamic_update_slice(
        jnp.zeros((vox_rows, 2, HALF, LANES), f32), negative, (0, 0, fas_place * own, 0)
    ).reshape(vox_rows, BV, LANES)

    image_rows = vox_rows * PACK
    table = pltpu.VMEM((fas_rows, LANES), f32)
    acc = pltpu.VMEM((vox_rows, BV, LANES), f32)
    image_out = ((image_rows, LANES), f32, "v")
    flat_out = ((half_rows, LANES), f32, "v")

    def swap(x, axis):
        return lax.all_to_all(x, axis, 0, 0)

    share_rows = image_rows // n_fas

    def collect(partial):
        return swap(partial.reshape(n_fas, share_rows, LANES), "fas")

    weights = initial_weights.reshape(half_rows, LANES)
    (partial,) = call(
        functools.partial(first_kernel, cap), [image_out], "svvvv", [table, acc]
    )(meta, weights, sig, cp, a)
    for sweep in range(ITERS):
        last = sweep == ITERS - 1
        (residual,) = call(share_kernel, [((n_fas, share_rows, LANES), f32, "v")], "v")(
            collect(partial)
        )
        whole = swap(residual, "fas")
        (gradient,) = call(
            functools.partial(backward_kernel, cap, vox_rows),
            [flat_out],
            "svvv",
            [pltpu.VMEM((vox_rows, 2 * BV, LANES), bf16), table],
        )(meta, whole.reshape(image_rows, LANES), cp, at)
        bit = 1
        while bit < n_vox:
            gradient = gradient + lax.ppermute(
                gradient, "vox", [(i, i ^ bit) for i in range(n_vox)]
            )
            bit *= 2
        partial, projected, proj_sq = call(
            functools.partial(image_kernel, cap),
            [image_out, flat_out, ((8, LANES), f32, "v")],
            "svvvv",
            [table, acc],
        )(meta, gradient, weights, cp, a)
        (sums,) = call(norm_kernel, [((n_vox * n_fas, 8, LANES), f32, "v")], "vv")(
            collect(partial), proj_sq
        )
        sums = swap(sums, ("vox", "fas"))
        out = ((vox_rows, BV, LANES), f32, "v") if last else image_out
        partial, weights = call(
            functools.partial(update_kernel, cap, n_vox, last),
            [out, flat_out],
            "svvvvvv",
            [table, acc],
        )(meta, sums, projected, weights, sig, cp, a)
    final = partial.reshape(vox_rows, 2, n_fas, own, LANES)[..., :DIRS].transpose(2, 0, 3, 1, 4)
    final = swap(final.reshape(n_fas, vox_rows, own * 2 * DIRS), "fas")
    return (weights.reshape(-1), jnp.sum(final, axis=0))


def solution(mesh):
    placed = (
        P("vox", "fas"),
        P("fas"),
        P(("vox", "fas"), None),
        P(("vox", "fas")),
        P(("vox", "fas")),
        P(("vox", "fas"), None),
        P(("vox", "fas")),
        P(),
    )
    return jax.shard_map(
        functools.partial(local, mesh.shape["vox"], mesh.shape["fas"]),
        mesh=mesh,
        in_specs=placed,
        out_specs=(P("fas"), P("vox", "fas")),
        check_vma=False,
    )
```

```python
import functools

import jax
import jax.numpy as jnp
from jax import lax
from jax.experimental import pallas as pl
from jax.experimental.pallas import tpu as pltpu
from jax.sharding import PartitionSpec as P

BV = 64
BF = 64
DIRS = 96
ITERS = 5
LANES = 128
GROUP = 4
BUILD = 8
UNROLL = 40
PACK = BV * DIRS // LANES
HALF = BV // 2
QUART = BV // 4
VMEM_LIMIT = 16 * 1024 * 1024


def group_cap(slots, rows):
    groups = slots // GROUP + rows
    return -(-groups // UNROLL) * UNROLL


def lane_ids(rows):
    return lax.broadcasted_iota(jnp.int32, (rows, LANES), 1)


def setup_kernel(slot_ref, turns_ref, coef_ref, atom_ref, dict_ref, cp_ref, at_ref, a_ref):
    atoms_pad = dict_ref.shape[1]
    left32 = lane_ids(HALF) < BF
    left1 = lane_ids(1) < BF
    atom_ids = lax.broadcasted_iota(jnp.int32, (atoms_pad, LANES), 0)

    def build(q):
        tops, bottoms, marks = [], [], []
        for pair in range(GROUP // 2):
            s0 = slot_ref[q * GROUP + 2 * pair]
            s1 = slot_ref[q * GROUP + 2 * pair + 1]
            k0 = jnp.maximum(s0, 0)
            k1 = jnp.maximum(s1, 0)
            m0 = (s0 >= 0).astype(jnp.float32)
            m1 = (s1 >= 0).astype(jnp.float32)
            c0 = coef_ref[k0].astype(jnp.float32) * m0
            c1 = coef_ref[k1].astype(jnp.float32) * m1
            tops.append(jnp.where(left32, c0, pltpu.roll(c1, BF, 1)))
            bottoms.append(jnp.where(left32, pltpu.roll(c0, BF, 1), c1))
            ids = jnp.where(left1, atom_ref[pl.ds(k0, 1), :], atom_ref[pl.ds(k1, 1), :])
            marks.append((atom_ids == ids).astype(jnp.float32).astype(jnp.bfloat16))
        top = jnp.concatenate(tops, axis=1)
        bottom = jnp.concatenate(bottoms, axis=1)
        cp_ref[q] = jnp.concatenate([top, bottom], axis=0).astype(jnp.bfloat16)
        marked = jnp.concatenate(marks, axis=1)
        table = jnp.dot(dict_ref[...], marked, preferred_element_type=jnp.float32)
        at_ref[q] = table.astype(jnp.bfloat16)
        a_ref[q] = table.T.astype(jnp.bfloat16)

    def turn(t, carry):
        for n in range(BUILD):
            build(t * BUILD + n)
        return carry

    lax.fori_loop(0, turns_ref[0] * (UNROLL // BUILD), turn, 0)


def sort_slots(rows, cols, count, vox_rows, cap):
    i32 = jnp.int32
    slots = rows.shape[0]
    k = jnp.arange(slots, dtype=i32)
    rows = jnp.where(k < count, rows, vox_rows)
    r = jnp.arange(vox_rows, dtype=i32)
    member = rows[:, None] == r[None, :]
    groups = (jnp.sum(member.astype(i32), axis=0) + GROUP - 1) // GROUP
    start = jnp.sum(jnp.where(r[:, None] < r[None, :], groups[:, None], 0), axis=0)
    total = jnp.sum(groups)
    before = (rows[:, None] == rows[None, :]) & (k[None, :] < k[:, None])
    rank = jnp.sum(before.astype(i32), axis=1)
    first = jnp.sum(jnp.where(member, start[None, :], 0), axis=1)
    place = jnp.where(rows < vox_rows, first * GROUP + rank, -1)
    chosen = jnp.arange(cap * GROUP, dtype=i32)[:, None] == place[None, :]
    slot = jnp.sum(jnp.where(chosen, k[None, :] + 1, 0), axis=1) - 1
    col = jnp.sum(jnp.where(chosen, cols[None, :], 0), axis=1)
    q = jnp.arange(cap, dtype=i32)
    row = jnp.sum((start[None, :] <= q[:, None]).astype(i32), axis=1) - 1
    turns = (total + UNROLL - 1) // UNROLL
    return slot, jnp.concatenate([col, row, turns[None]]), turns[None]


def spread_table(values, table_ref):
    rows = values.shape[0]
    left = lane_ids(rows) < BF
    turned = pltpu.roll(values, BF, 1)
    table_ref[pl.ds(0, rows, stride=2), :] = jnp.where(left, values, turned)
    table_ref[pl.ds(1, rows, stride=2), :] = jnp.where(left, turned, values)


def run_forward(cap, meta_ref, cp_ref, a_ref, table_ref, acc_ref):
    left = lane_ids(1) < BF

    def turn(t, carry):
        outs = []
        for n in range(UNROLL):
            q = t * UNROLL + n
            u = []
            for pair in range(GROUP // 2):
                p = q * GROUP + 2 * pair
                u0 = table_ref[pl.ds(meta_ref[p], 1), :]
                u1 = table_ref[pl.ds(meta_ref[p + 1], 1), :]
                u.append(jnp.where(left, u0, u1))
            scaled = cp_ref[q].astype(jnp.float32) * jnp.concatenate(u, axis=1)
            high = scaled.astype(jnp.bfloat16)
            low = (scaled - high.astype(jnp.float32)).astype(jnp.bfloat16)
            both = jnp.concatenate([high, low], axis=0)
            out = jnp.dot(both, a_ref[q], preferred_element_type=jnp.float32)
            outs.append(out[:BV] + out[BV:])
        for n in range(UNROLL):
            r = meta_ref[cap * GROUP + t * UNROLL + n]
            acc_ref[r] = acc_ref[r] + outs[n]
        return carry

    lax.fori_loop(0, meta_ref[cap * (GROUP + 1)], turn, 0)


def pack_rows(acc_ref, out_ref):
    lane = lane_ids(QUART)
    for r in range(acc_ref.shape[0]):
        last = acc_ref[r, 3 * QUART :, :]
        for i in range(3):
            tail = pltpu.roll(last, DIRS - 32 * i, 1)
            out_ref[pl.ds(r * PACK + i * QUART, QUART), :] = jnp.where(
                lane < DIRS, acc_ref[r, i * QUART : (i + 1) * QUART, :], tail
            )


def first_kernel(cap, meta_ref, w_ref, sig_ref, cp_ref, a_ref, out_ref, table_ref, acc_ref):
    spread_table(w_ref[...], table_ref)
    acc_ref[...] = sig_ref[...]
    run_forward(cap, meta_ref, cp_ref, a_ref, table_ref, acc_ref)
    pack_rows(acc_ref, out_ref)


def image_kernel(cap, meta_ref, g_ref, w_ref, cp_ref, a_ref, out_ref, p_ref, sq_ref, table_ref, acc_ref):
    gradient = g_ref[...]
    projected = jnp.where((w_ref[...] > 0) | (gradient < 0), gradient, 0.0)
    p_ref[...] = projected
    sq_ref[...] = jnp.sum((projected * projected).reshape(-1, 8, LANES), axis=0)
    spread_table(projected, table_ref)
    acc_ref[...] = jnp.zeros_like(acc_ref)
    run_forward(cap, meta_ref, cp_ref, a_ref, table_ref, acc_ref)
    pack_rows(acc_ref, out_ref)


def update_kernel(
    cap,
    vox_total,
    last,
    meta_ref,
    sums_ref,
    p_ref,
    w_ref,
    sig_ref,
    cp_ref,
    a_ref,
    out_ref,
    new_ref,
    table_ref,
    acc_ref,
):
    sums = jnp.sum(sums_ref[...], axis=0)
    left = lane_ids(1) < BF
    image_sq = jnp.sum(jnp.where(left, sums, 0.0), keepdims=True)
    grad_sq = jnp.sum(jnp.where(left, 0.0, sums), keepdims=True) * (1.0 / vox_total)
    step = grad_sq / (image_sq + 1e-6)
    updated = jnp.maximum(w_ref[...] - step * p_ref[...], 0.0)
    new_ref[...] = updated
    spread_table(updated, table_ref)
    acc_ref[...] = sig_ref[...]
    run_forward(cap, meta_ref, cp_ref, a_ref, table_ref, acc_ref)
    if last:
        out_ref[...] = acc_ref[...]
    else:
        pack_rows(acc_ref, out_ref)


def backward_kernel(cap, vox_rows, meta_ref, res_ref, cp_ref, at_ref, out_ref, split_ref, table_ref):
    lane = lane_ids(QUART)
    for r in range(vox_rows):
        packed = [res_ref[pl.ds(r * PACK + i * QUART, QUART), :] for i in range(3)]
        turned = [pltpu.roll(packed[i], 32 * (i + 1), 1) for i in range(3)]
        last = jnp.where(lane < 32, turned[0], jnp.where(lane < 64, turned[1], turned[2]))
        whole = jnp.concatenate(packed + [last], axis=0)
        whole = jnp.where(lane_ids(BV) < DIRS, whole, 0.0)
        high = whole.astype(jnp.bfloat16)
        low = (whole - high.astype(jnp.float32)).astype(jnp.bfloat16)
        split_ref[r] = jnp.concatenate([high, low], axis=0)
    table_ref[...] = jnp.zeros_like(table_ref)
    left = lane_ids(1) < BF

    def turn(t, carry):
        sums = []
        for n in range(UNROLL):
            q = t * UNROLL + n
            r = meta_ref[cap * GROUP + q]
            part = jnp.dot(split_ref[r], at_ref[q], preferred_element_type=jnp.float32)
            part = (part[:BV] + part[BV:]) * cp_ref[q].astype(jnp.float32)
            sums.append(jnp.sum(part, axis=0, keepdims=True))
        for n in range(UNROLL):
            for pair in range(GROUP // 2):
                p = (t * UNROLL + n) * GROUP + 2 * pair
                row = sums[n][:, pair * LANES : (pair + 1) * LANES]
                c0 = pl.ds(meta_ref[p], 1)
                table_ref[c0, :] = table_ref[c0, :] + jnp.where(left, row, 0.0)
                c1 = pl.ds(meta_ref[p + 1], 1)
                table_ref[c1, :] = table_ref[c1, :] + jnp.where(left, 0.0, row)
        return carry

    lax.fori_loop(0, meta_ref[cap * (GROUP + 1)], turn, 0)
    rows = out_ref.shape[0]
    even = table_ref[pl.ds(0, rows, stride=2), :]
    odd = table_ref[pl.ds(1, rows, stride=2), :]
    even = even + pltpu.roll(even, BF, 1)
    odd = odd + pltpu.roll(odd, BF, 1)
    out_ref[...] = jnp.where(lane_ids(rows) < BF, even, odd)


def share_kernel(shares_ref, out_ref):
    out_ref[...] = jnp.sum(shares_ref[...], axis=0)


def spread_kernel(mine_ref, other_ref, out_ref):
    total = mine_ref[...] + other_ref[...]
    for i in range(out_ref.shape[0]):
        out_ref[i] = total


def norm_kernel(shares_ref, sq_ref, out_ref):
    image = jnp.sum(shares_ref[...], axis=0)
    image_sq = jnp.sum(image * image, axis=0, keepdims=True)
    proj_sq = jnp.sum(sq_ref[...], axis=0, keepdims=True)
    image_sq = image_sq + pltpu.roll(image_sq, BF, 1)
    proj_sq = proj_sq + pltpu.roll(proj_sq, BF, 1)
    sums = jnp.where(lane_ids(1) < BF, image_sq, proj_sq)
    out_ref[...] = jnp.broadcast_to(sums[None], out_ref.shape)


def call(kernel, outs, ins, scratch=()):
    spaces = {"v": pltpu.VMEM, "s": pltpu.SMEM}
    run = pl.pallas_call(
        kernel,
        out_shape=tuple(
            pltpu.VMEM(shape, dtype) if kind == "v" else jax.ShapeDtypeStruct(shape, dtype)
            for shape, dtype, kind in outs
        ),
        in_specs=[pl.BlockSpec(memory_space=spaces[kind]) for kind in ins],
        out_specs=tuple(pl.BlockSpec(memory_space=spaces[kind]) for _, _, kind in outs),
        scratch_shapes=list(scratch),
        compiler_params=pltpu.CompilerParams(vmem_limit_bytes=VMEM_LIMIT),
    )

    def placed(*args):
        return run(
            *(
                pltpu.with_memory_space_constraint(x, pltpu.VMEM) if kind == "v" else x
                for x, kind in zip(args, ins)
            )
        )

    return placed


def local(
    n_vox,
    n_fas,
    signal,
    initial_weights,
    coefficients,
    block_rows,
    block_cols,
    block_atoms,
    block_count,
    dictionary,
):
    f32, bf16, i32 = jnp.float32, jnp.bfloat16, jnp.int32
    vox_rows = signal.shape[0]
    fas_rows = initial_weights.shape[0] // BF
    slots = coefficients.shape[0]
    cap = group_cap(slots, vox_rows)
    atoms = dictionary.shape[0]
    atoms_pad = -(-atoms // LANES) * LANES
    wide = GROUP * BF
    half_rows = fas_rows // 2

    coef_view = coefficients.reshape(slots, HALF, LANES)
    atom_view = jnp.concatenate([block_atoms, block_atoms], axis=1)
    dict_t = jnp.pad(dictionary.T, ((0, LANES - DIRS), (0, atoms_pad - atoms)))
    fas_place = lax.axis_index("fas")
    slot, meta, turns = sort_slots(
        block_rows - lax.axis_index("vox") * vox_rows,
        block_cols - fas_place * fas_rows,
        block_count[0],
        vox_rows,
        cap,
    )
    cp, at, a = call(
        setup_kernel,
        [
            ((cap, BV, wide), bf16, "v"),
            ((cap, LANES, wide), bf16, "v"),
            ((cap, wide, LANES), bf16, "v"),
        ],
        "ssvvv",
    )(slot, turns, coef_view, atom_view, dict_t)

    own = signal.shape[1] // DIRS // 2
    negative = -signal.reshape(vox_rows, own, 2, DIRS).transpose(0, 2, 1, 3)
    negative = jnp.pad(negative, ((0, 0), (0, 0), (0, 0), (0, LANES - DIRS)))
    sig = lax.dynamic_update_slice(
        jnp.zeros((vox_rows, 2, HALF, LANES), f32), negative, (0, 0, fas_place * own, 0)
    ).reshape(vox_rows, BV, LANES)

    image_rows = vox_rows * PACK
    table = pltpu.VMEM((fas_rows, LANES), f32)
    acc = pltpu.VMEM((vox_rows, BV, LANES), f32)
    image_out = ((image_rows, LANES), f32, "v")
    flat_out = ((half_rows, LANES), f32, "v")

    def swap(x, axis, groups=None):
        return lax.all_to_all(x, axis, 0, 0, axis_index_groups=groups)

    half = n_fas // 2
    halves = [list(range(half)), list(range(half, n_fas))]
    across = [(i, (i + half) % n_fas) for i in range(n_fas)]
    share_rows = image_rows // n_fas
    half_share = image_rows // half

    def sum_all(partial):
        shares = swap(partial.reshape(half, half_share, LANES), "fas", halves)
        (mine,) = call(share_kernel, [((half_share, LANES), f32, "v")], "v")(shares)
        other = lax.ppermute(mine, "fas", across)
        (total,) = call(spread_kernel, [((half, half_share, LANES), f32, "v")], "vv")(mine, other)
        return swap(total, "fas", halves).reshape(image_rows, LANES)

    weights = initial_weights.reshape(half_rows, LANES)
    (partial,) = call(
        functools.partial(first_kernel, cap), [image_out], "svvvv", [table, acc]
    )(meta, weights, sig, cp, a)
    for sweep in range(ITERS):
        last = sweep == ITERS - 1
        whole = sum_all(partial)
        (gradient,) = call(
            functools.partial(backward_kernel, cap, vox_rows),
            [flat_out],
            "svvv",
            [pltpu.VMEM((vox_rows, 2 * BV, LANES), bf16), table],
        )(meta, whole, cp, at)
        bit = 1
        while bit < n_vox:
            gradient = gradient + lax.ppermute(
                gradient, "vox", [(i, i ^ bit) for i in range(n_vox)]
            )
            bit *= 2
        partial, projected, proj_sq = call(
            functools.partial(image_kernel, cap),
            [image_out, flat_out, ((8, LANES), f32, "v")],
            "svvvv",
            [table, acc],
        )(meta, gradient, weights, cp, a)
        shares = swap(partial.reshape(n_fas, share_rows, LANES), "fas")
        (sums,) = call(norm_kernel, [((n_vox * n_fas, 1, LANES), f32, "v")], "vv")(shares, proj_sq)
        sums = swap(sums, ("vox", "fas"))
        out = ((vox_rows, BV, LANES), f32, "v") if last else image_out
        partial, weights = call(
            functools.partial(update_kernel, cap, n_vox, last),
            [out, flat_out],
            "svvvvvv",
            [table, acc],
        )(meta, sums, projected, weights, sig, cp, a)
    final = partial.reshape(vox_rows, 2, n_fas, own, LANES)[..., :DIRS].transpose(2, 0, 3, 1, 4)
    final = swap(final.reshape(n_fas, vox_rows, own * 2 * DIRS), "fas")
    return (weights.reshape(-1), jnp.sum(final, axis=0))


def solution(mesh):
    placed = (
        P("vox", "fas"),
        P("fas"),
        P(("vox", "fas"), None),
        P(("vox", "fas")),
        P(("vox", "fas")),
        P(("vox", "fas"), None),
        P(("vox", "fas")),
        P(),
    )
    return jax.shard_map(
        functools.partial(local, mesh.shape["vox"], mesh.shape["fas"]),
        mesh=mesh,
        in_specs=placed,
        out_specs=(P("fas"), P("vox", "fas")),
        check_vma=False,
    )
```

```python
import functools

import jax
import jax.numpy as jnp
from jax import lax
from jax.experimental import pallas as pl
from jax.experimental.pallas import tpu as pltpu
from jax.sharding import PartitionSpec as P

BV = 64
BF = 64
DIRS = 96
ITERS = 5
LANES = 128
GROUP = 4
BUILD = 20
UNROLL = 80
PACK = BV * DIRS // LANES
HALF = BV // 2
QUART = BV // 4
VMEM_LIMIT = 16 * 1024 * 1024


def group_cap(slots, rows):
    groups = slots // GROUP + rows
    return -(-groups // UNROLL) * UNROLL


def lane_ids(rows):
    return lax.broadcasted_iota(jnp.int32, (rows, LANES), 1)


def plan_slots(vox_rows, fas_rows, cap, row_ref, side_ref, count_ref, plan_ref):
    f32, i32 = jnp.float32, jnp.int32
    slots = row_ref.shape[1]
    places = cap * GROUP
    count = count_ref[...]
    down = lax.broadcasted_iota(i32, (slots, 1), 0)
    along = lax.broadcasted_iota(i32, (1, slots), 1)
    rows_down = jnp.where(down < count, lax.rem(side_ref[:, 0:1], vox_rows), vox_rows)
    cols_down = lax.rem(side_ref[:, 1:2], fas_rows)
    rows_along = jnp.where(along < count, lax.rem(row_ref[...], vox_rows), vox_rows)
    lane = lane_ids(1)
    member = (rows_down == lane) & (lane < vox_rows)
    counts = jnp.sum(member.astype(i32), axis=0, keepdims=True)
    groups = (counts + GROUP - 1) // GROUP
    earlier = lax.broadcasted_iota(i32, (LANES, LANES), 0) < lane_ids(LANES)
    start = jnp.dot(
        jnp.broadcast_to(groups, (8, LANES)).astype(f32).astype(jnp.bfloat16),
        earlier.astype(f32).astype(jnp.bfloat16),
        preferred_element_type=f32,
    )[0:1].astype(i32)
    rank = jnp.sum(
        ((rows_along == rows_down) & (along < down)).astype(i32), axis=1, keepdims=True
    )
    first = jnp.sum(jnp.where(member, start, 0), axis=1, keepdims=True)
    place = jnp.where(rows_down < vox_rows, first * GROUP + rank, -1)
    spots = lax.broadcasted_iota(i32, (1, places), 1)
    chosen = place == spots
    plan_ref[:, 0:places] = jnp.sum(jnp.where(chosen, cols_down, 0), axis=0, keepdims=True)
    slot = jnp.sum(jnp.where(chosen, down + 1, 0), axis=0, keepdims=True) - 1
    plan_ref[:, places : 2 * places] = slot
    heads = lax.broadcasted_iota(i32, (1, cap), 1) * GROUP
    row = jnp.sum(jnp.where(place == heads, rows_down, 0), axis=0, keepdims=True)
    plan_ref[:, 2 * places : 2 * places + cap] = row
    total = jnp.sum(groups, axis=1, keepdims=True)
    turns = (total + UNROLL - 1) // UNROLL
    rest = plan_ref.shape[1] - 2 * places - cap
    plan_ref[:, 2 * places + cap :] = jnp.broadcast_to(turns, (1, rest))


def setup_kernel(
    vox_rows,
    fas_rows,
    cap,
    row_ref,
    side_ref,
    count_ref,
    coef_ref,
    atom_ref,
    dict_ref,
    cp_ref,
    at_ref,
    a_ref,
    meta_ref,
    plan_ref,
    sem,
):
    plan_slots(vox_rows, fas_rows, cap, row_ref, side_ref, count_ref, plan_ref)
    plan = pltpu.make_async_copy(plan_ref, meta_ref, sem)
    plan.start()
    plan.wait()
    atoms_pad = dict_ref.shape[1]
    left32 = lane_ids(HALF) < BF
    left1 = lane_ids(1) < BF
    atom_ids = lax.broadcasted_iota(jnp.int16, (atoms_pad, LANES), 0)

    def build(q):
        tops, bottoms, marks = [], [], []
        for pair in range(GROUP // 2):
            s0 = meta_ref[0, cap * GROUP + q * GROUP + 2 * pair]
            s1 = meta_ref[0, cap * GROUP + q * GROUP + 2 * pair + 1]
            k0 = jnp.maximum(s0, 0)
            k1 = jnp.maximum(s1, 0)
            m0 = (s0 >= 0).astype(jnp.float32)
            m1 = (s1 >= 0).astype(jnp.float32)
            c0 = coef_ref[k0].astype(jnp.float32) * m0
            c1 = coef_ref[k1].astype(jnp.float32) * m1
            tops.append(jnp.where(left32, c0, pltpu.roll(c1, BF, 1)))
            bottoms.append(jnp.where(left32, pltpu.roll(c0, BF, 1), c1))
            ids = jnp.where(left1, atom_ref[pl.ds(k0, 1), :], atom_ref[pl.ds(k1, 1), :])
            ids = jnp.broadcast_to(ids, (atoms_pad, LANES)).astype(jnp.int16)
            marks.append(jnp.where(atom_ids == ids, jnp.bfloat16(1), jnp.bfloat16(0)))
        top = jnp.concatenate(tops, axis=1)
        bottom = jnp.concatenate(bottoms, axis=1)
        cp_ref[q] = jnp.concatenate([top, bottom], axis=0).astype(jnp.bfloat16)
        marked = jnp.concatenate(marks, axis=1)
        table = jnp.dot(dict_ref[...], marked, preferred_element_type=jnp.float32)
        at_ref[q] = table.astype(jnp.bfloat16)
        a_ref[q] = table.T.astype(jnp.bfloat16)

    def turn(t, carry):
        for n in range(BUILD):
            build(t * BUILD + n)
        return carry

    lax.fori_loop(0, meta_ref[0, cap * (2 * GROUP + 1)] * (UNROLL // BUILD), turn, 0)


def spread_table(values, table_ref):
    rows = values.shape[0]
    left = lane_ids(rows) < BF
    turned = pltpu.roll(values, BF, 1)
    table_ref[pl.ds(0, rows, stride=2), :] = jnp.where(left, values, turned)
    table_ref[pl.ds(1, rows, stride=2), :] = jnp.where(left, turned, values)


def run_forward(cap, meta_ref, cp_ref, a_ref, table_ref, acc_ref):
    left = lane_ids(1) < BF

    def turn(t, carry):
        outs = []
        for n in range(UNROLL):
            q = t * UNROLL + n
            u = []
            for pair in range(GROUP // 2):
                p = q * GROUP + 2 * pair
                u0 = table_ref[pl.ds(meta_ref[0, p], 1), :]
                u1 = table_ref[pl.ds(meta_ref[0, p + 1], 1), :]
                u.append(jnp.where(left, u0, u1))
            scaled = cp_ref[q].astype(jnp.float32) * jnp.concatenate(u, axis=1)
            high = scaled.astype(jnp.bfloat16)
            low = (scaled - high.astype(jnp.float32)).astype(jnp.bfloat16)
            both = jnp.concatenate([high, low], axis=0)
            out = jnp.dot(both, a_ref[q], preferred_element_type=jnp.float32)
            outs.append(out[:BV] + out[BV:])
        for n in range(UNROLL):
            r = meta_ref[0, cap * 2 * GROUP + t * UNROLL + n]
            acc_ref[r] = acc_ref[r] + outs[n]
        return carry

    lax.fori_loop(0, meta_ref[0, cap * (2 * GROUP + 1)], turn, 0)


def pack_rows(acc_ref, out_ref):
    lane = lane_ids(QUART)
    for r in range(acc_ref.shape[0]):
        last = acc_ref[r, 3 * QUART :, :]
        for i in range(3):
            tail = pltpu.roll(last, DIRS - 32 * i, 1)
            out_ref[pl.ds(r * PACK + i * QUART, QUART), :] = jnp.where(
                lane < DIRS, acc_ref[r, i * QUART : (i + 1) * QUART, :], tail
            )


def first_kernel(cap, meta_ref, w_ref, sig_ref, cp_ref, a_ref, out_ref, table_ref, acc_ref):
    spread_table(w_ref[...], table_ref)
    acc_ref[...] = sig_ref[...]
    run_forward(cap, meta_ref, cp_ref, a_ref, table_ref, acc_ref)
    pack_rows(acc_ref, out_ref)


def image_kernel(cap, meta_ref, g_ref, w_ref, cp_ref, a_ref, out_ref, p_ref, sq_ref, table_ref, acc_ref):
    gradient = g_ref[...]
    projected = jnp.where((w_ref[...] > 0) | (gradient < 0), gradient, 0.0)
    p_ref[...] = projected
    sq_ref[...] = jnp.sum((projected * projected).reshape(-1, 8, LANES), axis=0)
    spread_table(projected, table_ref)
    acc_ref[...] = jnp.zeros_like(acc_ref)
    run_forward(cap, meta_ref, cp_ref, a_ref, table_ref, acc_ref)
    pack_rows(acc_ref, out_ref)


def update_kernel(
    cap,
    vox_total,
    last,
    meta_ref,
    sums_ref,
    p_ref,
    w_ref,
    sig_ref,
    cp_ref,
    a_ref,
    out_ref,
    new_ref,
    table_ref,
    acc_ref,
):
    sums = jnp.sum(sums_ref[...], axis=0)
    left = lane_ids(1) < BF
    image_sq = jnp.sum(jnp.where(left, sums, 0.0), keepdims=True)
    grad_sq = jnp.sum(jnp.where(left, 0.0, sums), keepdims=True) * (1.0 / vox_total)
    step = grad_sq / (image_sq + 1e-6)
    updated = jnp.maximum(w_ref[...] - step * p_ref[...], 0.0)
    new_ref[...] = updated
    spread_table(updated, table_ref)
    acc_ref[...] = sig_ref[...]
    run_forward(cap, meta_ref, cp_ref, a_ref, table_ref, acc_ref)
    if last:
        out_ref[...] = acc_ref[...]
    else:
        pack_rows(acc_ref, out_ref)


def backward_kernel(cap, vox_rows, meta_ref, res_ref, cp_ref, at_ref, out_ref, split_ref, table_ref):
    lane = lane_ids(QUART)
    for r in range(vox_rows):
        packed = [res_ref[pl.ds(r * PACK + i * QUART, QUART), :] for i in range(3)]
        turned = [pltpu.roll(packed[i], 32 * (i + 1), 1) for i in range(3)]
        last = jnp.where(lane < 32, turned[0], jnp.where(lane < 64, turned[1], turned[2]))
        whole = jnp.concatenate(packed + [last], axis=0)
        whole = jnp.where(lane_ids(BV) < DIRS, whole, 0.0)
        high = whole.astype(jnp.bfloat16)
        low = (whole - high.astype(jnp.float32)).astype(jnp.bfloat16)
        split_ref[r] = jnp.concatenate([high, low], axis=0)
    table_ref[...] = jnp.zeros_like(table_ref)
    left = lane_ids(1) < BF

    def turn(t, carry):
        sums = []
        for n in range(UNROLL):
            q = t * UNROLL + n
            r = meta_ref[0, cap * 2 * GROUP + q]
            part = jnp.dot(split_ref[r], at_ref[q], preferred_element_type=jnp.float32)
            part = (part[:BV] + part[BV:]) * cp_ref[q].astype(jnp.float32)
            sums.append(jnp.sum(part, axis=0, keepdims=True))
        for n in range(UNROLL):
            for pair in range(GROUP // 2):
                p = (t * UNROLL + n) * GROUP + 2 * pair
                row = sums[n][:, pair * LANES : (pair + 1) * LANES]
                c0 = pl.ds(meta_ref[0, p], 1)
                table_ref[c0, :] = table_ref[c0, :] + jnp.where(left, row, 0.0)
                c1 = pl.ds(meta_ref[0, p + 1], 1)
                table_ref[c1, :] = table_ref[c1, :] + jnp.where(left, 0.0, row)
        return carry

    lax.fori_loop(0, meta_ref[0, cap * (2 * GROUP + 1)], turn, 0)
    rows = out_ref.shape[0]
    even = table_ref[pl.ds(0, rows, stride=2), :]
    odd = table_ref[pl.ds(1, rows, stride=2), :]
    even = even + pltpu.roll(even, BF, 1)
    odd = odd + pltpu.roll(odd, BF, 1)
    out_ref[...] = jnp.where(lane_ids(rows) < BF, even, odd)


def share_kernel(shares_ref, out_ref):
    out_ref[...] = jnp.sum(shares_ref[...], axis=0)


def spread_kernel(mine_ref, other_ref, out_ref):
    total = mine_ref[...] + other_ref[...]
    for i in range(out_ref.shape[0]):
        out_ref[i] = total


def norm_kernel(shares_ref, sq_ref, out_ref):
    image = jnp.sum(shares_ref[...], axis=0)
    image_sq = jnp.sum(image * image, axis=0, keepdims=True)
    proj_sq = jnp.sum(sq_ref[...], axis=0, keepdims=True)
    image_sq = image_sq + pltpu.roll(image_sq, BF, 1)
    proj_sq = proj_sq + pltpu.roll(proj_sq, BF, 1)
    sums = jnp.where(lane_ids(1) < BF, image_sq, proj_sq)
    out_ref[...] = jnp.broadcast_to(sums[None], out_ref.shape)


def call(kernel, outs, ins, scratch=()):
    spaces = {"v": pltpu.VMEM, "s": pltpu.SMEM, "m": pltpu.SMEM, "n": pltpu.VMEM}
    run = pl.pallas_call(
        kernel,
        out_shape=tuple(
            spaces[kind](shape, dtype) for shape, dtype, kind in outs
        ),
        in_specs=[pl.BlockSpec(memory_space=spaces[kind]) for kind in ins],
        out_specs=tuple(pl.BlockSpec(memory_space=spaces[kind]) for _, _, kind in outs),
        scratch_shapes=list(scratch),
        compiler_params=pltpu.CompilerParams(vmem_limit_bytes=VMEM_LIMIT),
    )

    def placed(*args):
        return run(
            *(
                pltpu.with_memory_space_constraint(x, spaces[kind]) if kind in "vm" else x
                for x, kind in zip(args, ins)
            )
        )

    return placed


def local(
    n_vox,
    n_fas,
    signal,
    initial_weights,
    coefficients,
    block_rows,
    block_cols,
    block_atoms,
    block_count,
    dictionary,
):
    f32, bf16, i32 = jnp.float32, jnp.bfloat16, jnp.int32
    vox_rows = signal.shape[0]
    fas_rows = initial_weights.shape[0] // BF
    slots = coefficients.shape[0]
    cap = group_cap(slots, vox_rows)
    atoms = dictionary.shape[0]
    atoms_pad = -(-atoms // LANES) * LANES
    wide = GROUP * BF
    half_rows = fas_rows // 2

    coef_view = coefficients.reshape(slots, HALF, LANES)
    atom_view = jnp.concatenate([block_atoms, block_atoms], axis=1)
    dict_t = jnp.pad(dictionary.T, ((0, LANES - DIRS), (0, atoms_pad - atoms)))
    fas_place = lax.axis_index("fas")
    side = jnp.stack([block_rows, block_cols], axis=1)
    side = jnp.pad(side, ((0, 0), (0, LANES - 2)))
    plan_size = -(-(cap * (2 * GROUP + 1) + 1) // LANES) * LANES
    cp, at, a, meta = call(
        functools.partial(setup_kernel, vox_rows, fas_rows, cap),
        [
            ((cap, BV, wide), bf16, "v"),
            ((cap, LANES, wide), bf16, "v"),
            ((cap, wide, LANES), bf16, "v"),
            ((1, plan_size), i32, "m"),
        ],
        "nvnvvv",
        [pltpu.VMEM((1, plan_size), i32), pltpu.SemaphoreType.DMA],
    )(block_rows[None], side, block_count[None], coef_view, atom_view, dict_t)

    own = signal.shape[1] // DIRS // 2
    negative = -signal.reshape(vox_rows, own, 2, DIRS).transpose(0, 2, 1, 3)
    negative = jnp.pad(negative, ((0, 0), (0, 0), (0, 0), (0, LANES - DIRS)))
    sig = lax.dynamic_update_slice(
        jnp.zeros((vox_rows, 2, HALF, LANES), f32), negative, (0, 0, fas_place * own, 0)
    ).reshape(vox_rows, BV, LANES)

    image_rows = vox_rows * PACK
    table = pltpu.VMEM((fas_rows, LANES), f32)
    acc = pltpu.VMEM((vox_rows, BV, LANES), f32)
    image_out = ((image_rows, LANES), f32, "v")
    flat_out = ((half_rows, LANES), f32, "v")

    def swap(x, axis, groups=None):
        return lax.all_to_all(x, axis, 0, 0, axis_index_groups=groups)

    half = n_fas // 2
    halves = [list(range(half)), list(range(half, n_fas))]
    across = [(i, (i + half) % n_fas) for i in range(n_fas)]
    share_rows = image_rows // n_fas
    half_share = image_rows // half

    def sum_all(partial):
        shares = swap(partial.reshape(half, half_share, LANES), "fas", halves)
        (mine,) = call(share_kernel, [((half_share, LANES), f32, "v")], "v")(shares)
        other = lax.ppermute(mine, "fas", across)
        (total,) = call(spread_kernel, [((half, half_share, LANES), f32, "v")], "vv")(mine, other)
        return swap(total, "fas", halves).reshape(image_rows, LANES)

    weights = initial_weights.reshape(half_rows, LANES)
    (partial,) = call(
        functools.partial(first_kernel, cap), [image_out], "mvvvv", [table, acc]
    )(meta, weights, sig, cp, a)
    for sweep in range(ITERS):
        last = sweep == ITERS - 1
        whole = sum_all(partial)
        (gradient,) = call(
            functools.partial(backward_kernel, cap, vox_rows),
            [flat_out],
            "mvvv",
            [pltpu.VMEM((vox_rows, 2 * BV, LANES), bf16), table],
        )(meta, whole, cp, at)
        bit = 1
        while bit < n_vox:
            gradient = gradient + lax.ppermute(
                gradient, "vox", [(i, i ^ bit) for i in range(n_vox)]
            )
            bit *= 2
        partial, projected, proj_sq = call(
            functools.partial(image_kernel, cap),
            [image_out, flat_out, ((8, LANES), f32, "v")],
            "mvvvv",
            [table, acc],
        )(meta, gradient, weights, cp, a)
        shares = swap(partial.reshape(n_fas, share_rows, LANES), "fas")
        (sums,) = call(norm_kernel, [((n_vox * n_fas, 1, LANES), f32, "v")], "vv")(shares, proj_sq)
        sums = swap(sums, ("vox", "fas"))
        out = ((vox_rows, BV, LANES), f32, "v") if last else image_out
        partial, weights = call(
            functools.partial(update_kernel, cap, n_vox, last),
            [out, flat_out],
            "mvvvvvv",
            [table, acc],
        )(meta, sums, projected, weights, sig, cp, a)
    final = partial.reshape(vox_rows, 2, n_fas, own, LANES)[..., :DIRS].transpose(2, 0, 3, 1, 4)
    final = swap(final.reshape(n_fas, vox_rows, own * 2 * DIRS), "fas")
    return (weights.reshape(-1), jnp.sum(final, axis=0))


def solution(mesh):
    placed = (
        P("vox", "fas"),
        P("fas"),
        P(("vox", "fas"), None),
        P(("vox", "fas")),
        P(("vox", "fas")),
        P(("vox", "fas"), None),
        P(("vox", "fas")),
        P(),
    )
    return jax.shard_map(
        functools.partial(local, mesh.shape["vox"], mesh.shape["fas"]),
        mesh=mesh,
        in_specs=placed,
        out_specs=(P("fas"), P("vox", "fas")),
        check_vma=False,
    )
```

```python
import functools

import jax
import jax.numpy as jnp
from jax import lax
from jax.experimental import pallas as pl
from jax.experimental.pallas import tpu as pltpu
from jax.sharding import PartitionSpec as P

BV = 64
BF = 64
DIRS = 96
ITERS = 5
LANES = 128
GROUP = 4
BUILD = 19
UNROLL = 38
PACK = BV * DIRS // LANES
HALF = BV // 2
QUART = BV // 4
VMEM_LIMIT = 16 * 1024 * 1024


def group_cap(slots, rows):
    groups = (slots + (GROUP - 1) * rows) // GROUP
    return -(-groups // UNROLL) * UNROLL


def plan_spots(cap):
    places = -(-cap * GROUP // LANES) * LANES
    return places, 2 * places, 2 * places + -(-cap // LANES) * LANES


def lane_ids(rows):
    return lax.broadcasted_iota(jnp.int32, (rows, LANES), 1)


def plan_slots(vox_rows, fas_rows, cap, row_ref, side_ref, count_ref, plan_ref):
    f32, i32 = jnp.float32, jnp.int32
    slots = row_ref.shape[1]
    places = cap * GROUP
    count = count_ref[...]
    down = lax.broadcasted_iota(i32, (slots, 1), 0)
    along = lax.broadcasted_iota(i32, (1, slots), 1)
    rows_down = jnp.where(down < count, lax.rem(side_ref[:, 0:1], vox_rows), vox_rows)
    cols_down = lax.rem(side_ref[:, 1:2], fas_rows)
    rows_along = jnp.where(along < count, lax.rem(row_ref[...], vox_rows), vox_rows)
    lane = lane_ids(1)
    member = (rows_down == lane) & (lane < vox_rows)
    counts = jnp.sum(member.astype(i32), axis=0, keepdims=True)
    groups = (counts + GROUP - 1) // GROUP
    earlier = lax.broadcasted_iota(i32, (LANES, LANES), 0) < lane_ids(LANES)
    start = jnp.dot(
        jnp.broadcast_to(groups, (8, LANES)).astype(f32).astype(jnp.bfloat16),
        earlier.astype(f32).astype(jnp.bfloat16),
        preferred_element_type=f32,
    )[0:1].astype(i32)
    rank = jnp.sum(
        ((rows_along == rows_down) & (along < down)).astype(i32), axis=1, keepdims=True
    )
    first = jnp.sum(jnp.where(member, start, 0), axis=1, keepdims=True)
    place = jnp.where(rows_down < vox_rows, first * GROUP + rank, -1)
    spots = lax.broadcasted_iota(i32, (1, places), 1)
    chosen = place == spots
    slot_at, row_at, turns_at = plan_spots(cap)
    plan_ref[:, 0:places] = jnp.sum(jnp.where(chosen, cols_down, 0), axis=0, keepdims=True)
    slot = jnp.sum(jnp.where(chosen, down + 1, 0), axis=0, keepdims=True) - 1
    plan_ref[:, slot_at : slot_at + places] = slot
    heads = lax.broadcasted_iota(i32, (1, cap), 1) * GROUP
    row = jnp.sum(jnp.where(place == heads, rows_down, 0), axis=0, keepdims=True)
    plan_ref[:, row_at : row_at + cap] = row
    total = jnp.sum(groups, axis=1, keepdims=True)
    turns = (total + UNROLL - 1) // UNROLL
    plan_ref[:, turns_at:] = jnp.broadcast_to(turns, (1, LANES))


def setup_kernel(
    vox_rows,
    fas_rows,
    cap,
    row_ref,
    side_ref,
    count_ref,
    coef_ref,
    atom_ref,
    dict_ref,
    cp_ref,
    at_ref,
    a_ref,
    meta_ref,
    plan_ref,
    sem,
):
    plan_slots(vox_rows, fas_rows, cap, row_ref, side_ref, count_ref, plan_ref)
    plan = pltpu.make_async_copy(plan_ref, meta_ref, sem)
    plan.start()
    plan.wait()
    slot_at, _, turns_at = plan_spots(cap)
    atoms_pad = dict_ref.shape[1]
    left32 = lane_ids(HALF) < BF
    left1 = lane_ids(1) < BF
    atom_ids = lax.broadcasted_iota(jnp.int16, (atoms_pad, LANES), 0)

    def build(q):
        tops, bottoms, marks = [], [], []
        for pair in range(GROUP // 2):
            s0 = meta_ref[0, slot_at + q * GROUP + 2 * pair]
            s1 = meta_ref[0, slot_at + q * GROUP + 2 * pair + 1]
            k0 = jnp.maximum(s0, 0)
            k1 = jnp.maximum(s1, 0)
            m0 = (s0 >= 0).astype(jnp.float32)
            m1 = (s1 >= 0).astype(jnp.float32)
            c0 = coef_ref[k0].astype(jnp.float32) * m0
            c1 = coef_ref[k1].astype(jnp.float32) * m1
            tops.append(jnp.where(left32, c0, pltpu.roll(c1, BF, 1)))
            bottoms.append(jnp.where(left32, pltpu.roll(c0, BF, 1), c1))
            ids = jnp.where(left1, atom_ref[pl.ds(k0, 1), :], atom_ref[pl.ds(k1, 1), :])
            ids = jnp.broadcast_to(ids, (atoms_pad, LANES)).astype(jnp.int16)
            marks.append(jnp.where(atom_ids == ids, jnp.bfloat16(1), jnp.bfloat16(0)))
        top = jnp.concatenate(tops, axis=1)
        bottom = jnp.concatenate(bottoms, axis=1)
        cp_ref[q] = jnp.concatenate([top, bottom], axis=0).astype(jnp.bfloat16)
        marked = jnp.concatenate(marks, axis=1)
        table = jnp.dot(dict_ref[...], marked, preferred_element_type=jnp.float32)
        at_ref[q] = table.astype(jnp.bfloat16)
        a_ref[q] = table.T.astype(jnp.bfloat16)

    def turn(t, carry):
        for n in range(BUILD):
            build(t * BUILD + n)
        return carry

    lax.fori_loop(0, meta_ref[0, turns_at] * (UNROLL // BUILD), turn, 0)


def spread_table(values, table_ref):
    rows = values.shape[0]
    left = lane_ids(rows) < BF
    turned = pltpu.roll(values, BF, 1)
    table_ref[pl.ds(0, rows, stride=2), :] = jnp.where(left, values, turned)
    table_ref[pl.ds(1, rows, stride=2), :] = jnp.where(left, turned, values)


def run_forward(cap, meta_ref, cp_ref, a_ref, table_ref, acc_ref):
    left = lane_ids(1) < BF
    _, row_at, turns_at = plan_spots(cap)

    def turn(t, carry):
        outs = []
        for n in range(UNROLL):
            q = t * UNROLL + n
            u = []
            for pair in range(GROUP // 2):
                p = q * GROUP + 2 * pair
                u0 = table_ref[pl.ds(meta_ref[0, p], 1), :]
                u1 = table_ref[pl.ds(meta_ref[0, p + 1], 1), :]
                u.append(jnp.where(left, u0, u1))
            scaled = cp_ref[q].astype(jnp.float32) * jnp.concatenate(u, axis=1)
            high = scaled.astype(jnp.bfloat16)
            low = (scaled - high.astype(jnp.float32)).astype(jnp.bfloat16)
            both = jnp.concatenate([high, low], axis=0)
            out = jnp.dot(both, a_ref[q], preferred_element_type=jnp.float32)
            outs.append(out[:BV] + out[BV:])
        for n in range(UNROLL):
            r = meta_ref[0, row_at + t * UNROLL + n]
            acc_ref[r] = acc_ref[r] + outs[n]
        return carry

    lax.fori_loop(0, meta_ref[0, turns_at], turn, 0)


def packed_row(acc_ref, r):
    lane = lane_ids(QUART)
    last = acc_ref[r, 3 * QUART :, :]
    return [
        jnp.where(
            lane < DIRS,
            acc_ref[r, i * QUART : (i + 1) * QUART, :],
            pltpu.roll(last, DIRS - 32 * i, 1),
        )
        for i in range(3)
    ]


def pack_rows(acc_ref, out_refs):
    parts = len(out_refs)
    rows = acc_ref.shape[0] // parts
    place = lax.rem(lax.axis_index("fas"), parts) if parts > 1 else 0
    for s in range(parts):
        for n in range(rows):
            r = (place ^ s) * rows + n if parts > 1 else n
            for i, piece in enumerate(packed_row(acc_ref, r)):
                out_refs[s][pl.ds(n * PACK + i * QUART, QUART), :] = piece


def first_kernel(cap, meta_ref, w_ref, sig_ref, cp_ref, a_ref, *refs):
    *out_refs, table_ref, acc_ref = refs
    spread_table(w_ref[...], table_ref)
    acc_ref[...] = sig_ref[...]
    run_forward(cap, meta_ref, cp_ref, a_ref, table_ref, acc_ref)
    pack_rows(acc_ref, out_refs)


def image_kernel(cap, meta_ref, g_ref, w_ref, cp_ref, a_ref, out_ref, p_ref, sq_ref, table_ref, acc_ref):
    gradient = g_ref[...]
    projected = jnp.where((w_ref[...] > 0) | (gradient < 0), gradient, 0.0)
    p_ref[...] = projected
    sq_ref[...] = jnp.sum((projected * projected).reshape(-1, 8, LANES), axis=0)
    spread_table(projected, table_ref)
    acc_ref[...] = jnp.zeros_like(acc_ref)
    run_forward(cap, meta_ref, cp_ref, a_ref, table_ref, acc_ref)
    pack_rows(acc_ref, [out_ref])


def update_kernel(
    cap,
    vox_total,
    last,
    meta_ref,
    sums_ref,
    p_ref,
    w_ref,
    sig_ref,
    cp_ref,
    a_ref,
    new_ref,
    *refs,
):
    *out_refs, table_ref, acc_ref = refs
    sums = jnp.sum(sums_ref[...], axis=0)
    left = lane_ids(1) < BF
    image_sq = jnp.sum(jnp.where(left, sums, 0.0), keepdims=True)
    grad_sq = jnp.sum(jnp.where(left, 0.0, sums), keepdims=True) * (1.0 / vox_total)
    step = grad_sq / (image_sq + 1e-6)
    updated = jnp.maximum(w_ref[...] - step * p_ref[...], 0.0)
    new_ref[...] = updated
    spread_table(updated, table_ref)
    acc_ref[...] = sig_ref[...]
    run_forward(cap, meta_ref, cp_ref, a_ref, table_ref, acc_ref)
    if last:
        out_refs[0][...] = acc_ref[...]
    else:
        pack_rows(acc_ref, out_refs)


def backward_kernel(cap, vox_rows, meta_ref, cp_ref, at_ref, *refs):
    *res_refs, out_ref, split_ref, table_ref = refs
    lane = lane_ids(QUART)
    parts = len(res_refs)
    rows = vox_rows // parts
    place = lax.rem(lax.axis_index("fas"), parts) if parts > 1 else 0
    for s, n in [(s, n) for s in range(parts) for n in range(rows)]:
        r = (place ^ s) * rows + n if parts > 1 else n
        packed = [res_refs[s][pl.ds(n * PACK + i * QUART, QUART), :] for i in range(3)]
        turned = [pltpu.roll(packed[i], 32 * (i + 1), 1) for i in range(3)]
        last = jnp.where(lane < 32, turned[0], jnp.where(lane < 64, turned[1], turned[2]))
        whole = jnp.concatenate(packed + [last], axis=0)
        whole = jnp.where(lane_ids(BV) < DIRS, whole, 0.0)
        high = whole.astype(jnp.bfloat16)
        low = (whole - high.astype(jnp.float32)).astype(jnp.bfloat16)
        split_ref[r] = jnp.concatenate([high, low], axis=0)
    table_ref[...] = jnp.zeros_like(table_ref)
    left = lane_ids(1) < BF
    _, row_at, turns_at = plan_spots(cap)

    def turn(t, carry):
        sums = []
        for n in range(UNROLL):
            q = t * UNROLL + n
            r = meta_ref[0, row_at + q]
            part = jnp.dot(split_ref[r], at_ref[q], preferred_element_type=jnp.float32)
            part = (part[:BV] + part[BV:]) * cp_ref[q].astype(jnp.float32)
            sums.append(jnp.sum(part, axis=0, keepdims=True))
        for n in range(UNROLL):
            for pair in range(GROUP // 2):
                p = (t * UNROLL + n) * GROUP + 2 * pair
                row = sums[n][:, pair * LANES : (pair + 1) * LANES]
                c0 = pl.ds(meta_ref[0, p], 1)
                table_ref[c0, :] = table_ref[c0, :] + jnp.where(left, row, 0.0)
                c1 = pl.ds(meta_ref[0, p + 1], 1)
                table_ref[c1, :] = table_ref[c1, :] + jnp.where(left, 0.0, row)
        return carry

    lax.fori_loop(0, meta_ref[0, turns_at], turn, 0)
    rows = out_ref.shape[0]
    even = table_ref[pl.ds(0, rows, stride=2), :]
    odd = table_ref[pl.ds(1, rows, stride=2), :]
    even = even + pltpu.roll(even, BF, 1)
    odd = odd + pltpu.roll(odd, BF, 1)
    out_ref[...] = jnp.where(lane_ids(rows) < BF, even, odd)


def share_kernel(shares_ref, out_ref):
    out_ref[...] = jnp.sum(shares_ref[...], axis=0)


def sum_kernel(*refs):
    *in_refs, out_ref = refs
    total = in_refs[0][...]
    for ref in in_refs[1:]:
        total = total + ref[...]
    out_ref[...] = total


def spread_kernel(mine_ref, other_ref, out_ref):
    total = mine_ref[...] + other_ref[...]
    for i in range(out_ref.shape[0]):
        out_ref[i] = total


def norm_kernel(shares_ref, sq_ref, out_ref):
    image = jnp.sum(shares_ref[...], axis=0)
    image_sq = jnp.sum(image * image, axis=0, keepdims=True)
    proj_sq = jnp.sum(sq_ref[...], axis=0, keepdims=True)
    image_sq = image_sq + pltpu.roll(image_sq, BF, 1)
    proj_sq = proj_sq + pltpu.roll(proj_sq, BF, 1)
    sums = jnp.where(lane_ids(1) < BF, image_sq, proj_sq)
    out_ref[...] = jnp.broadcast_to(sums[None], out_ref.shape)


def call(kernel, outs, ins, scratch=()):
    spaces = {"v": pltpu.VMEM, "s": pltpu.SMEM, "m": pltpu.SMEM, "n": pltpu.VMEM}
    run = pl.pallas_call(
        kernel,
        out_shape=tuple(
            spaces[kind](shape, dtype) for shape, dtype, kind in outs
        ),
        in_specs=[pl.BlockSpec(memory_space=spaces[kind]) for kind in ins],
        out_specs=tuple(pl.BlockSpec(memory_space=spaces[kind]) for _, _, kind in outs),
        scratch_shapes=list(scratch),
        compiler_params=pltpu.CompilerParams(vmem_limit_bytes=VMEM_LIMIT),
    )

    def placed(*args):
        return run(
            *(
                pltpu.with_memory_space_constraint(x, spaces[kind]) if kind in "vm" else x
                for x, kind in zip(args, ins)
            )
        )

    return placed


def local(
    n_vox,
    n_fas,
    signal,
    initial_weights,
    coefficients,
    block_rows,
    block_cols,
    block_atoms,
    block_count,
    dictionary,
):
    f32, bf16, i32 = jnp.float32, jnp.bfloat16, jnp.int32
    vox_rows = signal.shape[0]
    fas_rows = initial_weights.shape[0] // BF
    slots = coefficients.shape[0]
    cap = group_cap(slots, vox_rows)
    atoms = dictionary.shape[0]
    atoms_pad = -(-atoms // LANES) * LANES
    wide = GROUP * BF
    half_rows = fas_rows // 2

    coef_view = coefficients.reshape(slots, HALF, LANES)
    atom_view = jnp.concatenate([block_atoms, block_atoms], axis=1)
    dict_t = jnp.pad(dictionary.T, ((0, LANES - DIRS), (0, atoms_pad - atoms)))
    fas_place = lax.axis_index("fas")
    side = jnp.stack([block_rows, block_cols], axis=1)
    side = jnp.pad(side, ((0, 0), (0, LANES - 2)))
    plan_size = plan_spots(cap)[2] + LANES
    cp, at, a, meta = call(
        functools.partial(setup_kernel, vox_rows, fas_rows, cap),
        [
            ((cap, BV, wide), bf16, "v"),
            ((cap, LANES, wide), bf16, "v"),
            ((cap, wide, LANES), bf16, "v"),
            ((1, plan_size), i32, "m"),
        ],
        "nvnvvv",
        [pltpu.VMEM((1, plan_size), i32), pltpu.SemaphoreType.DMA],
    )(block_rows[None], side, block_count[None], coef_view, atom_view, dict_t)

    own = signal.shape[1] // DIRS // 2
    negative = -signal.reshape(vox_rows, own, 2, DIRS).transpose(0, 2, 1, 3)
    negative = jnp.pad(negative, ((0, 0), (0, 0), (0, 0), (0, LANES - DIRS)))
    sig = lax.dynamic_update_slice(
        jnp.zeros((vox_rows, 2, HALF, LANES), f32), negative, (0, 0, fas_place * own, 0)
    ).reshape(vox_rows, BV, LANES)

    image_rows = vox_rows * PACK
    table = pltpu.VMEM((fas_rows, LANES), f32)
    acc = pltpu.VMEM((vox_rows, BV, LANES), f32)
    image_out = ((image_rows, LANES), f32, "v")
    flat_out = ((half_rows, LANES), f32, "v")

    def swap(x, axis, groups=None):
        return lax.all_to_all(x, axis, 0, 0, axis_index_groups=groups)

    half = n_fas // 2
    halves = [list(range(half)), list(range(half, n_fas))]
    across = [(i, (i + half) % n_fas) for i in range(n_fas)]
    share_rows = image_rows // n_fas
    half_share = image_rows // half

    parts = half if half <= 4 else 1
    share_out = ((half_share, LANES), f32, "v")
    image_outs = [share_out] * parts if parts > 1 else [image_out]

    def to_place(x, s):
        return lax.ppermute(x, "fas", [(i, i ^ s) for i in range(n_fas)])

    def sum_all(partial):
        if parts > 1:
            shares = [partial[0]] + [to_place(partial[s], s) for s in range(1, parts)]
            (mine,) = call(sum_kernel, [share_out], "v" * parts)(*shares)
            other = lax.ppermute(mine, "fas", across)
            (total,) = call(sum_kernel, [share_out], "vv")(mine, other)
            return [total] + [to_place(total, s) for s in range(1, parts)]
        shares = swap(partial[0].reshape(half, half_share, LANES), "fas", halves)
        (mine,) = call(share_kernel, [share_out], "v")(shares)
        other = lax.ppermute(mine, "fas", across)
        (total,) = call(spread_kernel, [((half, half_share, LANES), f32, "v")], "vv")(mine, other)
        return [swap(total, "fas", halves).reshape(image_rows, LANES)]

    weights = initial_weights.reshape(half_rows, LANES)
    partial = call(
        functools.partial(first_kernel, cap), image_outs, "mvvvv", [table, acc]
    )(meta, weights, sig, cp, a)
    for sweep in range(ITERS):
        last = sweep == ITERS - 1
        whole = sum_all(partial)
        (gradient,) = call(
            functools.partial(backward_kernel, cap, vox_rows),
            [flat_out],
            "mvv" + "v" * parts,
            [pltpu.VMEM((vox_rows, 2 * BV, LANES), bf16), table],
        )(meta, cp, at, *whole)
        bit = 1
        while bit < n_vox:
            gradient = gradient + lax.ppermute(
                gradient, "vox", [(i, i ^ bit) for i in range(n_vox)]
            )
            bit *= 2
        image, projected, proj_sq = call(
            functools.partial(image_kernel, cap),
            [image_out, flat_out, ((8, LANES), f32, "v")],
            "mvvvv",
            [table, acc],
        )(meta, gradient, weights, cp, a)
        shares = swap(image.reshape(n_fas, share_rows, LANES), "fas")
        (sums,) = call(norm_kernel, [((n_vox * n_fas, 1, LANES), f32, "v")], "vv")(shares, proj_sq)
        sums = swap(sums, ("vox", "fas"))
        outs = [((vox_rows, BV, LANES), f32, "v")] if last else image_outs
        weights, *partial = call(
            functools.partial(update_kernel, cap, n_vox, last),
            [flat_out, *outs],
            "mvvvvvv",
            [table, acc],
        )(meta, sums, projected, weights, sig, cp, a)
    final = partial[0].reshape(vox_rows, 2, n_fas, own, LANES)[..., :DIRS].transpose(2, 0, 3, 1, 4)
    final = swap(final.reshape(n_fas, vox_rows, own * 2 * DIRS), "fas")
    return (weights.reshape(-1), jnp.sum(final, axis=0))


def solution(mesh):
    placed = (
        P("vox", "fas"),
        P("fas"),
        P(("vox", "fas"), None),
        P(("vox", "fas")),
        P(("vox", "fas")),
        P(("vox", "fas"), None),
        P(("vox", "fas")),
        P(),
    )
    return jax.shard_map(
        functools.partial(local, mesh.shape["vox"], mesh.shape["fas"]),
        mesh=mesh,
        in_specs=placed,
        out_specs=(P("fas"), P("vox", "fas")),
        check_vma=False,
    )
```

```python
import functools

import jax
import jax.numpy as jnp
from jax import lax
from jax.experimental import pallas as pl
from jax.experimental.pallas import tpu as pltpu
from jax.sharding import PartitionSpec as P

BV = 64
BF = 64
DIRS = 96
ITERS = 5
LANES = 128
GROUP = 4
BUILD = 19
UNROLL = 38
PACK = BV * DIRS // LANES
HALF = BV // 2
QUART = BV // 4
VMEM_LIMIT = 16 * 1024 * 1024


def group_cap(slots, rows):
    groups = (slots + (GROUP - 1) * rows) // GROUP
    return -(-groups // UNROLL) * UNROLL


def plan_spots(cap):
    places = -(-cap * GROUP // LANES) * LANES
    return places, 2 * places, 2 * places + -(-cap // LANES) * LANES


def lane_ids(rows):
    return lax.broadcasted_iota(jnp.int32, (rows, LANES), 1)


def plan_slots(vox_rows, fas_rows, cap, row_ref, side_ref, count_ref, plan_ref):
    f32, i32 = jnp.float32, jnp.int32
    slots = row_ref.shape[1]
    places = cap * GROUP
    count = count_ref[...]
    down = lax.broadcasted_iota(i32, (slots, 1), 0)
    along = lax.broadcasted_iota(i32, (1, slots), 1)
    rows_down = jnp.where(down < count, lax.rem(side_ref[:, 0:1], vox_rows), vox_rows)
    cols_down = lax.rem(side_ref[:, 1:2], fas_rows)
    rows_along = jnp.where(along < count, lax.rem(row_ref[...], vox_rows), vox_rows)
    lane = lane_ids(1)
    member = (rows_down == lane) & (lane < vox_rows)
    counts = jnp.sum(member.astype(i32), axis=0, keepdims=True)
    groups = (counts + GROUP - 1) // GROUP
    earlier = lax.broadcasted_iota(i32, (LANES, LANES), 0) < lane_ids(LANES)
    start = jnp.dot(
        jnp.broadcast_to(groups, (8, LANES)).astype(f32).astype(jnp.bfloat16),
        earlier.astype(f32).astype(jnp.bfloat16),
        preferred_element_type=f32,
    )[0:1].astype(i32)
    rank = jnp.sum(
        ((rows_along == rows_down) & (along < down)).astype(i32), axis=1, keepdims=True
    )
    first = jnp.sum(jnp.where(member, start, 0), axis=1, keepdims=True)
    place = jnp.where(rows_down < vox_rows, first * GROUP + rank, -1)
    spots = lax.broadcasted_iota(i32, (1, places), 1)
    chosen = place == spots
    slot_at, row_at, turns_at = plan_spots(cap)
    plan_ref[:, 0:places] = jnp.sum(jnp.where(chosen, cols_down, 0), axis=0, keepdims=True)
    slot = jnp.sum(jnp.where(chosen, down + 1, 0), axis=0, keepdims=True) - 1
    plan_ref[:, slot_at : slot_at + places] = slot
    heads = lax.broadcasted_iota(i32, (1, cap), 1) * GROUP
    row = jnp.sum(jnp.where(place == heads, rows_down, 0), axis=0, keepdims=True)
    plan_ref[:, row_at : row_at + cap] = row
    total = jnp.sum(groups, axis=1, keepdims=True)
    turns = (total + UNROLL - 1) // UNROLL
    plan_ref[:, turns_at:] = jnp.broadcast_to(turns, (1, LANES))


def setup_kernel(
    vox_rows,
    fas_rows,
    cap,
    row_ref,
    side_ref,
    count_ref,
    coef_ref,
    atom_ref,
    dict_ref,
    cp_ref,
    at_ref,
    a_ref,
    meta_ref,
    plan_ref,
    sem,
):
    plan_slots(vox_rows, fas_rows, cap, row_ref, side_ref, count_ref, plan_ref)
    plan = pltpu.make_async_copy(plan_ref, meta_ref, sem)
    plan.start()
    plan.wait()
    slot_at, _, turns_at = plan_spots(cap)
    atoms_pad = dict_ref.shape[1]
    left32 = lane_ids(HALF) < BF
    left1 = lane_ids(1) < BF
    atom_ids = lax.broadcasted_iota(jnp.int16, (atoms_pad, LANES), 0)

    def build(q):
        tops, bottoms, marks = [], [], []
        for pair in range(GROUP // 2):
            s0 = meta_ref[0, slot_at + q * GROUP + 2 * pair]
            s1 = meta_ref[0, slot_at + q * GROUP + 2 * pair + 1]
            k0 = jnp.maximum(s0, 0)
            k1 = jnp.maximum(s1, 0)
            m0 = (s0 >= 0).astype(jnp.float32)
            m1 = (s1 >= 0).astype(jnp.float32)
            c0 = coef_ref[k0].astype(jnp.float32) * m0
            c1 = coef_ref[k1].astype(jnp.float32) * m1
            tops.append(jnp.where(left32, c0, pltpu.roll(c1, BF, 1)))
            bottoms.append(jnp.where(left32, pltpu.roll(c0, BF, 1), c1))
            ids = jnp.where(left1, atom_ref[pl.ds(k0, 1), :], atom_ref[pl.ds(k1, 1), :])
            ids = jnp.broadcast_to(ids, (atoms_pad, LANES)).astype(jnp.int16)
            marks.append(jnp.where(atom_ids == ids, jnp.bfloat16(1), jnp.bfloat16(0)))
        top = jnp.concatenate(tops, axis=1)
        bottom = jnp.concatenate(bottoms, axis=1)
        cp_ref[q] = jnp.concatenate([top, bottom], axis=0).astype(jnp.bfloat16)
        marked = jnp.concatenate(marks, axis=1)
        table = jnp.dot(dict_ref[...], marked, preferred_element_type=jnp.float32)
        at_ref[q] = table.astype(jnp.bfloat16)
        a_ref[q] = table.T.astype(jnp.bfloat16)

    def turn(t, carry):
        for n in range(BUILD):
            build(t * BUILD + n)
        return carry

    lax.fori_loop(0, meta_ref[0, turns_at] * (UNROLL // BUILD), turn, 0)


def spread_table(values, table_ref):
    rows = values.shape[0]
    left = lane_ids(rows) < BF
    turned = pltpu.roll(values, BF, 1)
    table_ref[pl.ds(0, rows, stride=2), :] = jnp.where(left, values, turned)
    table_ref[pl.ds(1, rows, stride=2), :] = jnp.where(left, turned, values)


def run_forward(cap, meta_ref, cp_ref, a_ref, table_ref, acc_ref):
    left = lane_ids(1) < BF
    _, row_at, turns_at = plan_spots(cap)

    def turn(t, carry):
        outs = []
        for n in range(UNROLL):
            q = t * UNROLL + n
            u = []
            for pair in range(GROUP // 2):
                p = q * GROUP + 2 * pair
                u0 = table_ref[pl.ds(meta_ref[0, p], 1), :]
                u1 = table_ref[pl.ds(meta_ref[0, p + 1], 1), :]
                u.append(jnp.where(left, u0, u1))
            scaled = cp_ref[q].astype(jnp.float32) * jnp.concatenate(u, axis=1)
            high = scaled.astype(jnp.bfloat16)
            low = (scaled - high.astype(jnp.float32)).astype(jnp.bfloat16)
            both = jnp.concatenate([high, low], axis=0)
            out = jnp.dot(both, a_ref[q], preferred_element_type=jnp.float32)
            outs.append(out[:BV] + out[BV:])
        for n in range(UNROLL):
            r = meta_ref[0, row_at + t * UNROLL + n]
            acc_ref[r] = acc_ref[r] + outs[n]
        return carry

    lax.fori_loop(0, meta_ref[0, turns_at], turn, 0)


def packed_row(acc_ref, r):
    lane = lane_ids(QUART)
    last = acc_ref[r, 3 * QUART :, :]
    return [
        jnp.where(
            lane < DIRS,
            acc_ref[r, i * QUART : (i + 1) * QUART, :],
            pltpu.roll(last, DIRS - 32 * i, 1),
        )
        for i in range(3)
    ]


def pack_rows(acc_ref, out_refs):
    parts = len(out_refs)
    rows = acc_ref.shape[0] // parts
    place = lax.rem(lax.axis_index("fas"), parts) if parts > 1 else 0
    for s in range(parts):
        for n in range(rows):
            r = (place ^ s) * rows + n if parts > 1 else n
            for i, piece in enumerate(packed_row(acc_ref, r)):
                out_refs[s][pl.ds(n * PACK + i * QUART, QUART), :] = piece


def first_kernel(cap, meta_ref, w_ref, sig_ref, cp_ref, a_ref, *refs):
    *out_refs, table_ref, acc_ref = refs
    spread_table(w_ref[...], table_ref)
    acc_ref[...] = sig_ref[...]
    run_forward(cap, meta_ref, cp_ref, a_ref, table_ref, acc_ref)
    pack_rows(acc_ref, out_refs)


def image_kernel(cap, meta_ref, g_ref, w_ref, cp_ref, a_ref, p_ref, sq_ref, *refs):
    *out_refs, table_ref, acc_ref = refs
    gradient = g_ref[...]
    projected = jnp.where((w_ref[...] > 0) | (gradient < 0), gradient, 0.0)
    p_ref[...] = projected
    sq_ref[...] = jnp.sum((projected * projected).reshape(-1, 8, LANES), axis=0)
    spread_table(projected, table_ref)
    acc_ref[...] = jnp.zeros_like(acc_ref)
    run_forward(cap, meta_ref, cp_ref, a_ref, table_ref, acc_ref)
    pack_rows(acc_ref, out_refs)


def update_kernel(
    cap,
    vox_total,
    last,
    meta_ref,
    sums_ref,
    p_ref,
    w_ref,
    sig_ref,
    cp_ref,
    a_ref,
    new_ref,
    *refs,
):
    *out_refs, table_ref, acc_ref = refs
    sums = jnp.sum(sums_ref[...], axis=0)
    left = lane_ids(1) < BF
    image_sq = jnp.sum(jnp.where(left, sums, 0.0), keepdims=True)
    grad_sq = jnp.sum(jnp.where(left, 0.0, sums), keepdims=True) * (1.0 / vox_total)
    step = grad_sq / (image_sq + 1e-6)
    updated = jnp.maximum(w_ref[...] - step * p_ref[...], 0.0)
    new_ref[...] = updated
    spread_table(updated, table_ref)
    acc_ref[...] = sig_ref[...]
    run_forward(cap, meta_ref, cp_ref, a_ref, table_ref, acc_ref)
    if last:
        out_refs[0][...] = acc_ref[...]
    else:
        pack_rows(acc_ref, out_refs)


def backward_kernel(cap, vox_rows, meta_ref, cp_ref, at_ref, *refs):
    *res_refs, out_ref, split_ref, table_ref = refs
    lane = lane_ids(QUART)
    parts = len(res_refs)
    rows = vox_rows // parts
    place = lax.rem(lax.axis_index("fas"), parts) if parts > 1 else 0
    for s, n in [(s, n) for s in range(parts) for n in range(rows)]:
        r = (place ^ s) * rows + n if parts > 1 else n
        packed = [res_refs[s][pl.ds(n * PACK + i * QUART, QUART), :] for i in range(3)]
        turned = [pltpu.roll(packed[i], 32 * (i + 1), 1) for i in range(3)]
        last = jnp.where(lane < 32, turned[0], jnp.where(lane < 64, turned[1], turned[2]))
        whole = jnp.concatenate(packed + [last], axis=0)
        whole = jnp.where(lane_ids(BV) < DIRS, whole, 0.0)
        high = whole.astype(jnp.bfloat16)
        low = (whole - high.astype(jnp.float32)).astype(jnp.bfloat16)
        split_ref[r] = jnp.concatenate([high, low], axis=0)
    table_ref[...] = jnp.zeros_like(table_ref)
    left = lane_ids(1) < BF
    _, row_at, turns_at = plan_spots(cap)

    def turn(t, carry):
        sums = []
        for n in range(UNROLL):
            q = t * UNROLL + n
            r = meta_ref[0, row_at + q]
            part = jnp.dot(split_ref[r], at_ref[q], preferred_element_type=jnp.float32)
            part = (part[:BV] + part[BV:]) * cp_ref[q].astype(jnp.float32)
            sums.append(jnp.sum(part, axis=0, keepdims=True))
        for n in range(UNROLL):
            for pair in range(GROUP // 2):
                p = (t * UNROLL + n) * GROUP + 2 * pair
                row = sums[n][:, pair * LANES : (pair + 1) * LANES]
                c0 = pl.ds(meta_ref[0, p], 1)
                table_ref[c0, :] = table_ref[c0, :] + jnp.where(left, row, 0.0)
                c1 = pl.ds(meta_ref[0, p + 1], 1)
                table_ref[c1, :] = table_ref[c1, :] + jnp.where(left, 0.0, row)
        return carry

    lax.fori_loop(0, meta_ref[0, turns_at], turn, 0)
    rows = out_ref.shape[0]
    even = table_ref[pl.ds(0, rows, stride=2), :]
    odd = table_ref[pl.ds(1, rows, stride=2), :]
    even = even + pltpu.roll(even, BF, 1)
    odd = odd + pltpu.roll(odd, BF, 1)
    out_ref[...] = jnp.where(lane_ids(rows) < BF, even, odd)


def share_kernel(shares_ref, out_ref):
    out_ref[...] = jnp.sum(shares_ref[...], axis=0)


def sum_kernel(*refs):
    *in_refs, out_ref = refs
    total = in_refs[0][...]
    for ref in in_refs[1:]:
        total = total + ref[...]
    out_ref[...] = total


def spread_kernel(mine_ref, other_ref, out_ref):
    total = mine_ref[...] + other_ref[...]
    for i in range(out_ref.shape[0]):
        out_ref[i] = total


def join_kernel(sq_ref, *refs):
    *in_refs, out_ref = refs
    total = in_refs[0][...]
    for ref in in_refs[1:]:
        total = total + ref[...]
    if len(total.shape) == 3:
        total = jnp.sum(total, axis=0)
    rows = total.shape[0]
    out_ref[:rows, :] = total
    out_ref[rows:, :] = sq_ref[...]


def norm_kernel(mine_ref, other_ref, out_ref):
    rows = mine_ref.shape[0] - 8
    image = mine_ref[:rows, :] + other_ref[:rows, :]
    image_sq = jnp.sum(image * image, axis=0, keepdims=True)
    proj_sq = jnp.sum(mine_ref[rows:, :] + other_ref[rows:, :], axis=0, keepdims=True)
    image_sq = image_sq + pltpu.roll(image_sq, BF, 1)
    proj_sq = proj_sq + pltpu.roll(proj_sq, BF, 1)
    sums = jnp.where(lane_ids(1) < BF, image_sq, proj_sq)
    out_ref[...] = jnp.broadcast_to(sums[None], out_ref.shape)


def call(kernel, outs, ins, scratch=()):
    spaces = {"v": pltpu.VMEM, "s": pltpu.SMEM, "m": pltpu.SMEM, "n": pltpu.VMEM}
    run = pl.pallas_call(
        kernel,
        out_shape=tuple(
            spaces[kind](shape, dtype) for shape, dtype, kind in outs
        ),
        in_specs=[pl.BlockSpec(memory_space=spaces[kind]) for kind in ins],
        out_specs=tuple(pl.BlockSpec(memory_space=spaces[kind]) for _, _, kind in outs),
        scratch_shapes=list(scratch),
        compiler_params=pltpu.CompilerParams(vmem_limit_bytes=VMEM_LIMIT),
    )

    def placed(*args):
        return run(
            *(
                pltpu.with_memory_space_constraint(x, spaces[kind]) if kind in "vm" else x
                for x, kind in zip(args, ins)
            )
        )

    return placed


def local(
    n_vox,
    n_fas,
    signal,
    initial_weights,
    coefficients,
    block_rows,
    block_cols,
    block_atoms,
    block_count,
    dictionary,
):
    f32, bf16, i32 = jnp.float32, jnp.bfloat16, jnp.int32
    vox_rows = signal.shape[0]
    fas_rows = initial_weights.shape[0] // BF
    slots = coefficients.shape[0]
    cap = group_cap(slots, vox_rows)
    atoms = dictionary.shape[0]
    atoms_pad = -(-atoms // LANES) * LANES
    wide = GROUP * BF
    half_rows = fas_rows // 2

    coef_view = coefficients.reshape(slots, HALF, LANES)
    atom_view = jnp.concatenate([block_atoms, block_atoms], axis=1)
    dict_t = jnp.pad(dictionary.T, ((0, LANES - DIRS), (0, atoms_pad - atoms)))
    fas_place = lax.axis_index("fas")
    side = jnp.stack([block_rows, block_cols], axis=1)
    side = jnp.pad(side, ((0, 0), (0, LANES - 2)))
    plan_size = plan_spots(cap)[2] + LANES
    cp, at, a, meta = call(
        functools.partial(setup_kernel, vox_rows, fas_rows, cap),
        [
            ((cap, BV, wide), bf16, "v"),
            ((cap, LANES, wide), bf16, "v"),
            ((cap, wide, LANES), bf16, "v"),
            ((1, plan_size), i32, "m"),
        ],
        "nvnvvv",
        [pltpu.VMEM((1, plan_size), i32), pltpu.SemaphoreType.DMA],
    )(block_rows[None], side, block_count[None], coef_view, atom_view, dict_t)

    own = signal.shape[1] // DIRS // 2
    negative = -signal.reshape(vox_rows, own, 2, DIRS).transpose(0, 2, 1, 3)
    negative = jnp.pad(negative, ((0, 0), (0, 0), (0, 0), (0, LANES - DIRS)))
    sig = lax.dynamic_update_slice(
        jnp.zeros((vox_rows, 2, HALF, LANES), f32), negative, (0, 0, fas_place * own, 0)
    ).reshape(vox_rows, BV, LANES)

    image_rows = vox_rows * PACK
    table = pltpu.VMEM((fas_rows, LANES), f32)
    acc = pltpu.VMEM((vox_rows, BV, LANES), f32)
    image_out = ((image_rows, LANES), f32, "v")
    flat_out = ((half_rows, LANES), f32, "v")

    def swap(x, axis, groups=None):
        return lax.all_to_all(x, axis, 0, 0, axis_index_groups=groups)

    half = n_fas // 2
    halves = [list(range(half)), list(range(half, n_fas))]
    both_axes = [[i * n_fas + f for i in range(n_vox) for f in group] for group in halves]
    across = [(i, (i + half) % n_fas) for i in range(n_fas)]
    half_share = image_rows // half

    parts = half if half <= 4 else 1
    share_out = ((half_share, LANES), f32, "v")
    image_outs = [share_out] * parts if parts > 1 else [image_out]

    def to_place(x, s):
        return lax.ppermute(x, "fas", [(i, i ^ s) for i in range(n_fas)])

    def gather_shares(partial):
        if parts > 1:
            return [partial[0]] + [to_place(partial[s], s) for s in range(1, parts)]
        return [swap(partial[0].reshape(half, half_share, LANES), "fas", halves)]

    def sum_all(partial):
        shares = gather_shares(partial)
        if parts > 1:
            (mine,) = call(sum_kernel, [share_out], "v" * parts)(*shares)
            other = lax.ppermute(mine, "fas", across)
            (total,) = call(sum_kernel, [share_out], "vv")(mine, other)
            return [total] + [to_place(total, s) for s in range(1, parts)]
        (mine,) = call(share_kernel, [share_out], "v")(*shares)
        other = lax.ppermute(mine, "fas", across)
        (total,) = call(spread_kernel, [((half, half_share, LANES), f32, "v")], "vv")(mine, other)
        return [swap(total, "fas", halves).reshape(image_rows, LANES)]

    weights = initial_weights.reshape(half_rows, LANES)
    partial = call(
        functools.partial(first_kernel, cap), image_outs, "mvvvv", [table, acc]
    )(meta, weights, sig, cp, a)
    for sweep in range(ITERS):
        last = sweep == ITERS - 1
        whole = sum_all(partial)
        (gradient,) = call(
            functools.partial(backward_kernel, cap, vox_rows),
            [flat_out],
            "mvv" + "v" * parts,
            [pltpu.VMEM((vox_rows, 2 * BV, LANES), bf16), table],
        )(meta, cp, at, *whole)
        bit = 1
        while bit < n_vox:
            gradient = gradient + lax.ppermute(
                gradient, "vox", [(i, i ^ bit) for i in range(n_vox)]
            )
            bit *= 2
        projected, proj_sq, *image = call(
            functools.partial(image_kernel, cap),
            [flat_out, ((8, LANES), f32, "v"), *image_outs],
            "mvvvv",
            [table, acc],
        )(meta, gradient, weights, cp, a)
        shares = gather_shares(image)
        (mine,) = call(
            join_kernel, [((half_share + 8, LANES), f32, "v")], "v" * (1 + len(shares))
        )(proj_sq, *shares)
        other = lax.ppermute(mine, "fas", across)
        (sums,) = call(norm_kernel, [((n_vox * half, 1, LANES), f32, "v")], "vv")(mine, other)
        sums = swap(sums, ("vox", "fas"), both_axes)
        outs = [((vox_rows, BV, LANES), f32, "v")] if last else image_outs
        weights, *partial = call(
            functools.partial(update_kernel, cap, n_vox, last),
            [flat_out, *outs],
            "mvvvvvv",
            [table, acc],
        )(meta, sums, projected, weights, sig, cp, a)
    final = partial[0].reshape(vox_rows, 2, n_fas, own, LANES)[..., :DIRS].transpose(2, 0, 3, 1, 4)
    final = swap(final.reshape(n_fas, vox_rows, own * 2 * DIRS), "fas")
    return (weights.reshape(-1), jnp.sum(final, axis=0))


def solution(mesh):
    placed = (
        P("vox", "fas"),
        P("fas"),
        P(("vox", "fas"), None),
        P(("vox", "fas")),
        P(("vox", "fas")),
        P(("vox", "fas"), None),
        P(("vox", "fas")),
        P(),
    )
    return jax.shard_map(
        functools.partial(local, mesh.shape["vox"], mesh.shape["fas"]),
        mesh=mesh,
        in_specs=placed,
        out_specs=(P("fas"), P("vox", "fas")),
        check_vma=False,
    )
```

```python
import functools

import jax
import jax.numpy as jnp
from jax import lax
from jax.experimental import pallas as pl
from jax.experimental.pallas import tpu as pltpu
from jax.sharding import PartitionSpec as P

BV = 64
BF = 64
DIRS = 96
ITERS = 5
LANES = 128
GROUP = 4
BUILD = 19
UNROLL = 38
PACK = BV * DIRS // LANES
HALF = BV // 2
QUART = BV // 4
VMEM_LIMIT = 16 * 1024 * 1024


def group_cap(slots, rows):
    groups = (slots + (GROUP - 1) * rows) // GROUP
    return -(-groups // UNROLL) * UNROLL


def plan_spots(cap):
    places = -(-cap * GROUP // LANES) * LANES
    return places, 2 * places, 2 * places + -(-cap // LANES) * LANES


def lane_ids(rows):
    return lax.broadcasted_iota(jnp.int32, (rows, LANES), 1)


def plan_slots(vox_rows, fas_rows, cap, row_ref, side_ref, count_ref, plan_ref):
    f32, i32 = jnp.float32, jnp.int32
    slots = row_ref.shape[1]
    places = cap * GROUP
    count = count_ref[...]
    down = lax.broadcasted_iota(i32, (slots, 1), 0)
    along = lax.broadcasted_iota(i32, (1, slots), 1)
    rows_down = jnp.where(down < count, lax.rem(side_ref[:, 0:1], vox_rows), vox_rows)
    cols_down = lax.rem(side_ref[:, 1:2], fas_rows)
    rows_along = jnp.where(along < count, lax.rem(row_ref[...], vox_rows), vox_rows)
    lane = lane_ids(1)
    member = (rows_down == lane) & (lane < vox_rows)
    counts = jnp.sum(member.astype(i32), axis=0, keepdims=True)
    groups = (counts + GROUP - 1) // GROUP
    earlier = lax.broadcasted_iota(i32, (LANES, LANES), 0) < lane_ids(LANES)
    start = jnp.dot(
        jnp.broadcast_to(groups, (8, LANES)).astype(f32).astype(jnp.bfloat16),
        earlier.astype(f32).astype(jnp.bfloat16),
        preferred_element_type=f32,
    )[0:1].astype(i32)
    rank = jnp.sum(
        ((rows_along == rows_down) & (along < down)).astype(i32), axis=1, keepdims=True
    )
    first = jnp.sum(jnp.where(member, start, 0), axis=1, keepdims=True)
    place = jnp.where(rows_down < vox_rows, first * GROUP + rank, -1)
    spots = lax.broadcasted_iota(i32, (1, places), 1)
    chosen = place == spots
    slot_at, row_at, turns_at = plan_spots(cap)
    plan_ref[:, 0:places] = jnp.sum(jnp.where(chosen, cols_down, 0), axis=0, keepdims=True)
    slot = jnp.sum(jnp.where(chosen, down + 1, 0), axis=0, keepdims=True) - 1
    plan_ref[:, slot_at : slot_at + places] = slot
    heads = lax.broadcasted_iota(i32, (1, cap), 1) * GROUP
    row = jnp.sum(jnp.where(place == heads, rows_down, 0), axis=0, keepdims=True)
    plan_ref[:, row_at : row_at + cap] = row
    total = jnp.sum(groups, axis=1, keepdims=True)
    turns = (total + UNROLL - 1) // UNROLL
    plan_ref[:, turns_at:] = jnp.broadcast_to(turns, (1, LANES))


def setup_kernel(
    vox_rows,
    fas_rows,
    cap,
    row_ref,
    side_ref,
    count_ref,
    coef_ref,
    atom_ref,
    dict_ref,
    cp_ref,
    at_ref,
    a_ref,
    meta_ref,
    plan_ref,
    sem,
):
    plan_slots(vox_rows, fas_rows, cap, row_ref, side_ref, count_ref, plan_ref)
    plan = pltpu.make_async_copy(plan_ref, meta_ref, sem)
    plan.start()
    plan.wait()
    slot_at, _, turns_at = plan_spots(cap)
    atoms_pad = dict_ref.shape[1]
    left32 = lane_ids(HALF) < BF
    left1 = lane_ids(1) < BF
    atom_ids = lax.broadcasted_iota(jnp.int16, (atoms_pad, LANES), 0)

    def build(q):
        tops, bottoms, marks = [], [], []
        for pair in range(GROUP // 2):
            s0 = meta_ref[0, slot_at + q * GROUP + 2 * pair]
            s1 = meta_ref[0, slot_at + q * GROUP + 2 * pair + 1]
            k0 = jnp.maximum(s0, 0)
            k1 = jnp.maximum(s1, 0)
            m0 = (s0 >= 0).astype(jnp.float32)
            m1 = (s1 >= 0).astype(jnp.float32)
            c0 = coef_ref[k0].astype(jnp.float32) * m0
            c1 = coef_ref[k1].astype(jnp.float32) * m1
            tops.append(jnp.where(left32, c0, pltpu.roll(c1, BF, 1)))
            bottoms.append(jnp.where(left32, pltpu.roll(c0, BF, 1), c1))
            ids = jnp.where(left1, atom_ref[pl.ds(k0, 1), :], atom_ref[pl.ds(k1, 1), :])
            ids = jnp.broadcast_to(ids, (atoms_pad, LANES)).astype(jnp.int16)
            marks.append(jnp.where(atom_ids == ids, jnp.bfloat16(1), jnp.bfloat16(0)))
        top = jnp.concatenate(tops, axis=1)
        bottom = jnp.concatenate(bottoms, axis=1)
        cp_ref[q] = jnp.concatenate([top, bottom], axis=0).astype(jnp.bfloat16)
        marked = jnp.concatenate(marks, axis=1)
        table = jnp.dot(dict_ref[...], marked, preferred_element_type=jnp.float32)
        at_ref[q] = table.astype(jnp.bfloat16)
        a_ref[q] = table.astype(jnp.bfloat16).T

    def turn(t, carry):
        for n in range(BUILD):
            build(t * BUILD + n)
        return carry

    lax.fori_loop(0, meta_ref[0, turns_at] * (UNROLL // BUILD), turn, 0)


def spread_table(values, table_ref):
    rows = values.shape[0]
    left = lane_ids(rows) < BF
    turned = pltpu.roll(values, BF, 1)
    table_ref[pl.ds(0, rows, stride=2), :] = jnp.where(left, values, turned)
    table_ref[pl.ds(1, rows, stride=2), :] = jnp.where(left, turned, values)


def run_forward(cap, meta_ref, cp_ref, a_ref, table_ref, acc_ref):
    left = lane_ids(1) < BF
    _, row_at, turns_at = plan_spots(cap)

    def turn(t, carry):
        outs = []
        for n in range(UNROLL):
            q = t * UNROLL + n
            u = []
            for pair in range(GROUP // 2):
                p = q * GROUP + 2 * pair
                u0 = table_ref[pl.ds(meta_ref[0, p], 1), :]
                u1 = table_ref[pl.ds(meta_ref[0, p + 1], 1), :]
                u.append(jnp.where(left, u0, u1))
            scaled = cp_ref[q].astype(jnp.float32) * jnp.concatenate(u, axis=1)
            high = scaled.astype(jnp.bfloat16)
            low = (scaled - high.astype(jnp.float32)).astype(jnp.bfloat16)
            both = jnp.concatenate([high, low], axis=0)
            out = jnp.dot(both, a_ref[q], preferred_element_type=jnp.float32)
            outs.append(out[:BV] + out[BV:])
        for n in range(UNROLL):
            r = meta_ref[0, row_at + t * UNROLL + n]
            acc_ref[r] = acc_ref[r] + outs[n]
        return carry

    lax.fori_loop(0, meta_ref[0, turns_at], turn, 0)


def packed_row(acc_ref, r):
    lane = lane_ids(QUART)
    last = acc_ref[r, 3 * QUART :, :]
    return [
        jnp.where(
            lane < DIRS,
            acc_ref[r, i * QUART : (i + 1) * QUART, :],
            pltpu.roll(last, DIRS - 32 * i, 1),
        )
        for i in range(3)
    ]


def pack_rows(acc_ref, out_refs):
    parts = len(out_refs)
    rows = acc_ref.shape[0] // parts
    place = lax.rem(lax.axis_index("fas"), parts) if parts > 1 else 0
    for s in range(parts):
        for n in range(rows):
            r = (place ^ s) * rows + n if parts > 1 else n
            for i, piece in enumerate(packed_row(acc_ref, r)):
                out_refs[s][pl.ds(n * PACK + i * QUART, QUART), :] = piece


def flat_rows(acc_ref, f, out_ref):
    lane = lane_ids(acc_ref.shape[0])
    voxels = out_ref.shape[1] // DIRS
    for g in range(voxels // 4):
        first = f * (voxels // 2) + 2 * g
        x = [acc_ref[:, i % 2 * HALF + i // 2 + first, :] for i in range(4)]
        tiles = [
            jnp.where(lane < 96, x[0], pltpu.roll(x[1], 96, 1)),
            jnp.where(lane < 64, pltpu.roll(x[1], 96, 1), pltpu.roll(x[2], 64, 1)),
            jnp.where(lane < 32, pltpu.roll(x[2], 64, 1), pltpu.roll(x[3], 32, 1)),
        ]
        out_ref[:, 4 * g * DIRS : 4 * (g + 1) * DIRS] = jnp.concatenate(tiles, axis=1)


def flat_parts(acc_ref, out_refs):
    parts = len(out_refs)
    if parts == 1:
        for f in range(out_refs[0].shape[0]):
            flat_rows(acc_ref, f, out_refs[0].at[f])
        return
    me = lax.axis_index("fas")
    place = lax.rem(me, parts)
    for s in range(parts):
        for other in range(2):
            f = ((me // parts) ^ other) * parts + (place ^ s)
            flat_rows(acc_ref, f, out_refs[s].at[other])


def first_kernel(cap, meta_ref, w_ref, sig_ref, cp_ref, a_ref, *refs):
    *out_refs, table_ref, acc_ref = refs
    spread_table(w_ref[...], table_ref)
    acc_ref[...] = sig_ref[...]
    run_forward(cap, meta_ref, cp_ref, a_ref, table_ref, acc_ref)
    pack_rows(acc_ref, out_refs)


def image_kernel(cap, meta_ref, g_ref, w_ref, cp_ref, a_ref, p_ref, sq_ref, *refs):
    *out_refs, table_ref, acc_ref = refs
    gradient = g_ref[...]
    projected = jnp.where((w_ref[...] > 0) | (gradient < 0), gradient, 0.0)
    p_ref[...] = projected
    sq_ref[...] = jnp.sum((projected * projected).reshape(-1, 8, LANES), axis=0)
    spread_table(projected, table_ref)
    acc_ref[...] = jnp.zeros_like(acc_ref)
    run_forward(cap, meta_ref, cp_ref, a_ref, table_ref, acc_ref)
    pack_rows(acc_ref, out_refs)


def update_kernel(
    cap,
    vox_total,
    last,
    meta_ref,
    sums_ref,
    p_ref,
    w_ref,
    sig_ref,
    cp_ref,
    a_ref,
    new_ref,
    *refs,
):
    *out_refs, table_ref, acc_ref = refs
    sums = jnp.sum(sums_ref[...], axis=0)
    left = lane_ids(1) < BF
    image_sq = jnp.sum(jnp.where(left, sums, 0.0), keepdims=True)
    grad_sq = jnp.sum(jnp.where(left, 0.0, sums), keepdims=True) * (1.0 / vox_total)
    step = grad_sq / (image_sq + 1e-6)
    updated = jnp.maximum(w_ref[...] - step * p_ref[...], 0.0)
    new_ref[...] = updated
    spread_table(updated, table_ref)
    acc_ref[...] = sig_ref[...]
    run_forward(cap, meta_ref, cp_ref, a_ref, table_ref, acc_ref)
    if last:
        flat_parts(acc_ref, out_refs)
    else:
        pack_rows(acc_ref, out_refs)


def backward_kernel(cap, vox_rows, meta_ref, cp_ref, at_ref, *refs):
    *res_refs, out_ref, split_ref, left_ref, right_ref = refs
    lane = lane_ids(QUART)
    parts = len(res_refs)
    rows = vox_rows // parts
    place = lax.rem(lax.axis_index("fas"), parts) if parts > 1 else 0
    for s, n in [(s, n) for s in range(parts) for n in range(rows)]:
        r = (place ^ s) * rows + n if parts > 1 else n
        packed = [res_refs[s][pl.ds(n * PACK + i * QUART, QUART), :] for i in range(3)]
        turned = [pltpu.roll(packed[i], 32 * (i + 1), 1) for i in range(3)]
        last = jnp.where(lane < 32, turned[0], jnp.where(lane < 64, turned[1], turned[2]))
        whole = jnp.concatenate(packed + [last], axis=0)
        whole = jnp.where(lane_ids(BV) < DIRS, whole, 0.0)
        high = whole.astype(jnp.bfloat16)
        low = (whole - high.astype(jnp.float32)).astype(jnp.bfloat16)
        split_ref[r] = jnp.concatenate([high, low], axis=0)
    left_ref[...] = jnp.zeros_like(left_ref)
    right_ref[...] = jnp.zeros_like(right_ref)
    _, row_at, turns_at = plan_spots(cap)

    def turn(t, carry):
        sums = []
        for n in range(UNROLL):
            q = t * UNROLL + n
            r = meta_ref[0, row_at + q]
            part = jnp.dot(split_ref[r], at_ref[q], preferred_element_type=jnp.float32)
            part = (part[:BV] + part[BV:]) * cp_ref[q].astype(jnp.float32)
            sums.append(jnp.sum(part, axis=0, keepdims=True))
        for n in range(UNROLL):
            for pair in range(GROUP // 2):
                p = (t * UNROLL + n) * GROUP + 2 * pair
                row = sums[n][:, pair * LANES : (pair + 1) * LANES]
                c0 = pl.ds(meta_ref[0, p], 1)
                left_ref[c0, :] = left_ref[c0, :] + row
                c1 = pl.ds(meta_ref[0, p + 1], 1)
                right_ref[c1, :] = right_ref[c1, :] + row
        return carry

    lax.fori_loop(0, meta_ref[0, turns_at], turn, 0)
    rows = out_ref.shape[0]
    left = lane_ids(rows) < BF
    even = [ref[pl.ds(0, rows, stride=2), :] for ref in (left_ref, right_ref)]
    odd = [ref[pl.ds(1, rows, stride=2), :] for ref in (left_ref, right_ref)]
    even = even[0] + pltpu.roll(even[1], BF, 1)
    odd = pltpu.roll(odd[0], BF, 1) + odd[1]
    out_ref[...] = jnp.where(left, even, odd)


def share_kernel(shares_ref, out_ref):
    out_ref[...] = jnp.sum(shares_ref[...], axis=0)


def sum_kernel(*refs):
    *in_refs, out_ref = refs
    total = in_refs[0][...]
    for ref in in_refs[1:]:
        total = total + ref[...]
    out_ref[...] = total


def split_kernel(*refs):
    *in_refs, own_ref, send_ref = refs
    for i, out_ref in enumerate((own_ref, send_ref)):
        total = in_refs[0][i]
        for ref in in_refs[1:]:
            total = total + ref[i]
        out_ref[...] = total


def spread_kernel(mine_ref, other_ref, out_ref):
    total = mine_ref[...] + other_ref[...]
    for i in range(out_ref.shape[0]):
        out_ref[i] = total


def join_kernel(sq_ref, *refs):
    *in_refs, out_ref = refs
    total = in_refs[0][...]
    for ref in in_refs[1:]:
        total = total + ref[...]
    if len(total.shape) == 3:
        total = jnp.sum(total, axis=0)
    rows = total.shape[0]
    out_ref[:rows, :] = total
    out_ref[rows:, :] = sq_ref[...]


def norm_kernel(mine_ref, other_ref, out_ref):
    rows = mine_ref.shape[0] - 8
    image = mine_ref[:rows, :] + other_ref[:rows, :]
    image_sq = jnp.sum(image * image, axis=0, keepdims=True)
    proj_sq = jnp.sum(mine_ref[rows:, :] + other_ref[rows:, :], axis=0, keepdims=True)
    image_sq = image_sq + pltpu.roll(image_sq, BF, 1)
    proj_sq = proj_sq + pltpu.roll(proj_sq, BF, 1)
    sums = jnp.where(lane_ids(1) < BF, image_sq, proj_sq)
    out_ref[...] = jnp.broadcast_to(sums[None], out_ref.shape)


def call(kernel, outs, ins, scratch=()):
    spaces = {"v": pltpu.VMEM, "s": pltpu.SMEM, "m": pltpu.SMEM, "n": pltpu.VMEM}
    run = pl.pallas_call(
        kernel,
        out_shape=tuple(
            jax.ShapeDtypeStruct(shape, dtype) if kind == "n" else spaces[kind](shape, dtype)
            for shape, dtype, kind in outs
        ),
        in_specs=[pl.BlockSpec(memory_space=spaces[kind]) for kind in ins],
        out_specs=tuple(pl.BlockSpec(memory_space=spaces[kind]) for _, _, kind in outs),
        scratch_shapes=list(scratch),
        compiler_params=pltpu.CompilerParams(vmem_limit_bytes=VMEM_LIMIT),
    )

    def placed(*args):
        return run(
            *(
                pltpu.with_memory_space_constraint(x, spaces[kind]) if kind in "vm" else x
                for x, kind in zip(args, ins)
            )
        )

    return placed


def local(
    n_vox,
    n_fas,
    signal,
    initial_weights,
    coefficients,
    block_rows,
    block_cols,
    block_atoms,
    block_count,
    dictionary,
):
    f32, bf16, i32 = jnp.float32, jnp.bfloat16, jnp.int32
    vox_rows = signal.shape[0]
    fas_rows = initial_weights.shape[0] // BF
    slots = coefficients.shape[0]
    cap = group_cap(slots, vox_rows)
    atoms = dictionary.shape[0]
    atoms_pad = -(-atoms // LANES) * LANES
    wide = GROUP * BF
    half_rows = fas_rows // 2

    coef_view = coefficients.reshape(slots, HALF, LANES)
    atom_view = jnp.concatenate([block_atoms, block_atoms], axis=1)
    dict_t = jnp.pad(dictionary.T, ((0, LANES - DIRS), (0, atoms_pad - atoms)))
    fas_place = lax.axis_index("fas")
    side = jnp.stack([block_rows, block_cols], axis=1)
    side = jnp.pad(side, ((0, 0), (0, LANES - 2)))
    plan_size = plan_spots(cap)[2] + LANES
    cp, at, a, meta = call(
        functools.partial(setup_kernel, vox_rows, fas_rows, cap),
        [
            ((cap, BV, wide), bf16, "v"),
            ((cap, LANES, wide), bf16, "v"),
            ((cap, wide, LANES), bf16, "v"),
            ((1, plan_size), i32, "m"),
        ],
        "nvnvvv",
        [pltpu.VMEM((1, plan_size), i32), pltpu.SemaphoreType.DMA],
    )(block_rows[None], side, block_count[None], coef_view, atom_view, dict_t)

    own = signal.shape[1] // DIRS // 2
    negative = -signal.reshape(vox_rows, own, 2, DIRS).transpose(0, 2, 1, 3)
    negative = jnp.pad(negative, ((0, 0), (0, 0), (0, 0), (0, LANES - DIRS)))
    sig = lax.dynamic_update_slice(
        jnp.zeros((vox_rows, 2, HALF, LANES), f32), negative, (0, 0, fas_place * own, 0)
    ).reshape(vox_rows, BV, LANES)

    image_rows = vox_rows * PACK
    table = pltpu.VMEM((fas_rows, LANES), f32)
    acc = pltpu.VMEM((vox_rows, BV, LANES), f32)
    image_out = ((image_rows, LANES), f32, "v")
    flat_out = ((half_rows, LANES), f32, "v")

    def swap(x, axis, groups=None):
        return lax.all_to_all(x, axis, 0, 0, axis_index_groups=groups)

    half = n_fas // 2
    halves = [list(range(half)), list(range(half, n_fas))]
    both_axes = [[i * n_fas + f for i in range(n_vox) for f in group] for group in halves]
    across = [(i, (i + half) % n_fas) for i in range(n_fas)]
    half_share = image_rows // half

    parts = half if half in (2, 4) else 1
    share_out = ((half_share, LANES), f32, "v")
    image_outs = [share_out] * parts if parts > 1 else [image_out]

    flat_count = 2 if parts > 1 else n_fas
    flat_outs = [((flat_count, *signal.shape), f32, "v")] * parts

    def to_place(x, s):
        return lax.ppermute(x, "fas", [(i, i ^ s) for i in range(n_fas)])

    def gather_shares(partial):
        if parts > 1:
            return [partial[0]] + [to_place(partial[s], s) for s in range(1, parts)]
        return [swap(partial[0].reshape(half, half_share, LANES), "fas", halves)]

    def sum_all(partial):
        shares = gather_shares(partial)
        if parts > 1:
            (mine,) = call(sum_kernel, [share_out], "v" * parts)(*shares)
            other = lax.ppermute(mine, "fas", across)
            (total,) = call(sum_kernel, [share_out], "vv")(mine, other)
            return [total] + [to_place(total, s) for s in range(1, parts)]
        (mine,) = call(share_kernel, [share_out], "v")(*shares)
        other = lax.ppermute(mine, "fas", across)
        (total,) = call(spread_kernel, [((half, half_share, LANES), f32, "v")], "vv")(mine, other)
        return [swap(total, "fas", halves).reshape(image_rows, LANES)]

    weights = initial_weights.reshape(half_rows, LANES)
    partial = call(
        functools.partial(first_kernel, cap), image_outs, "mvvvv", [table, acc]
    )(meta, weights, sig, cp, a)
    for sweep in range(ITERS):
        last = sweep == ITERS - 1
        whole = sum_all(partial)
        (gradient,) = call(
            functools.partial(backward_kernel, cap, vox_rows),
            [flat_out],
            "mvv" + "v" * parts,
            [pltpu.VMEM((vox_rows, 2 * BV, LANES), bf16), table, table],
        )(meta, cp, at, *whole)
        bit = 1
        while bit < n_vox:
            gradient = gradient + lax.ppermute(
                gradient, "vox", [(i, i ^ bit) for i in range(n_vox)]
            )
            bit *= 2
        projected, proj_sq, *image = call(
            functools.partial(image_kernel, cap),
            [flat_out, ((8, LANES), f32, "v"), *image_outs],
            "mvvvv",
            [table, acc],
        )(meta, gradient, weights, cp, a)
        shares = gather_shares(image)
        (mine,) = call(
            join_kernel, [((half_share + 8, LANES), f32, "v")], "v" * (1 + len(shares))
        )(proj_sq, *shares)
        other = lax.ppermute(mine, "fas", across)
        (sums,) = call(norm_kernel, [((n_vox * half, 1, LANES), f32, "v")], "vv")(mine, other)
        sums = swap(sums, ("vox", "fas"), both_axes)
        outs = flat_outs if last else image_outs
        weights, *partial = call(
            functools.partial(update_kernel, cap, n_vox, last),
            [flat_out if not last else (*flat_out[:2], "n"), *outs],
            "mvvvvvv",
            [table, acc],
        )(meta, sums, projected, weights, sig, cp, a)
    if parts > 1:
        shares = [partial[0]] + [to_place(partial[s], s) for s in range(1, parts)]
        piece = (signal.shape, f32, "v")
        own, send = call(split_kernel, [piece, piece], "v" * parts)(*shares)
        other = lax.ppermute(send, "fas", across)
        (final,) = call(sum_kernel, [(signal.shape, f32, "n")], "vv")(own, other)
    else:
        final = jnp.sum(swap(partial[0], "fas"), axis=0)
    return (weights.reshape(-1), final)


def solution(mesh):
    placed = (
        P("vox", "fas"),
        P("fas"),
        P(("vox", "fas"), None),
        P(("vox", "fas")),
        P(("vox", "fas")),
        P(("vox", "fas"), None),
        P(("vox", "fas")),
        P(),
    )
    return jax.shard_map(
        functools.partial(local, mesh.shape["vox"], mesh.shape["fas"]),
        mesh=mesh,
        in_specs=placed,
        out_specs=(P("fas"), P("vox", "fas")),
        check_vma=False,
    )
```

```python
import functools

import jax
import jax.numpy as jnp
from jax import lax
from jax.experimental import pallas as pl
from jax.experimental.pallas import tpu as pltpu
from jax.sharding import PartitionSpec as P

BV = 64
BF = 64
DIRS = 96
ITERS = 5
LANES = 128
GROUP = 4
BUILD = 19
UNROLL = 38
PACK = BV * DIRS // LANES
HALF = BV // 2
QUART = BV // 4
TURN = (0, 3, 1, 2)
VMEM_LIMIT = 16 * 1024 * 1024


def group_cap(slots, rows):
    groups = (slots + (GROUP - 1) * rows) // GROUP
    return -(-groups // UNROLL) * UNROLL


def plan_spots(cap):
    places = -(-cap * GROUP // LANES) * LANES
    return places, 2 * places, 2 * places + -(-cap // LANES) * LANES


def lane_ids(rows):
    return lax.broadcasted_iota(jnp.int32, (rows, LANES), 1)


def plan_slots(vox_rows, fas_rows, cap, row_ref, side_ref, count_ref, plan_ref):
    f32, i32 = jnp.float32, jnp.int32
    slots = row_ref.shape[1]
    places = cap * GROUP
    count = count_ref[...]
    down = lax.broadcasted_iota(i32, (slots, 1), 0)
    along = lax.broadcasted_iota(i32, (1, slots), 1)
    rows_down = jnp.where(down < count, lax.rem(side_ref[:, 0:1], vox_rows), vox_rows)
    cols_down = lax.rem(side_ref[:, 1:2], fas_rows)
    rows_along = jnp.where(along < count, lax.rem(row_ref[...], vox_rows), vox_rows)
    lane = lane_ids(1)
    member = (rows_down == lane) & (lane < vox_rows)
    counts = jnp.sum(member.astype(i32), axis=0, keepdims=True)
    groups = (counts + GROUP - 1) // GROUP
    earlier = lax.broadcasted_iota(i32, (LANES, LANES), 0) < lane_ids(LANES)
    start = jnp.dot(
        jnp.broadcast_to(groups, (8, LANES)).astype(f32).astype(jnp.bfloat16),
        earlier.astype(f32).astype(jnp.bfloat16),
        preferred_element_type=f32,
    )[0:1].astype(i32)
    rank = jnp.sum(
        ((rows_along == rows_down) & (along < down)).astype(i32), axis=1, keepdims=True
    )
    first = jnp.sum(jnp.where(member, start, 0), axis=1, keepdims=True)
    place = jnp.where(rows_down < vox_rows, first * GROUP + rank, -1)
    spots = lax.broadcasted_iota(i32, (1, places), 1)
    chosen = place == spots
    slot_at, row_at, turns_at = plan_spots(cap)
    plan_ref[:, 0:places] = jnp.sum(jnp.where(chosen, cols_down, 0), axis=0, keepdims=True)
    slot = jnp.sum(jnp.where(chosen, down + 1, 0), axis=0, keepdims=True) - 1
    plan_ref[:, slot_at : slot_at + places] = slot
    heads = lax.broadcasted_iota(i32, (1, cap), 1) * GROUP
    row = jnp.sum(jnp.where(place == heads, rows_down, 0), axis=0, keepdims=True)
    plan_ref[:, row_at : row_at + cap] = row
    total = jnp.sum(groups, axis=1, keepdims=True)
    turns = (total + UNROLL - 1) // UNROLL
    plan_ref[:, turns_at:] = jnp.broadcast_to(turns, (1, LANES))


def setup_kernel(
    vox_rows,
    fas_rows,
    cap,
    row_ref,
    side_ref,
    count_ref,
    coef_ref,
    atom_ref,
    dict_ref,
    cp_ref,
    at_ref,
    a_ref,
    meta_ref,
    plan_ref,
    sem,
):
    plan_slots(vox_rows, fas_rows, cap, row_ref, side_ref, count_ref, plan_ref)
    plan = pltpu.make_async_copy(plan_ref, meta_ref, sem)
    plan.start()
    plan.wait()
    slot_at, _, turns_at = plan_spots(cap)
    atoms_pad = dict_ref.shape[1]
    left32 = lane_ids(HALF) < BF
    left1 = lane_ids(1) < BF
    atom_ids = lax.broadcasted_iota(jnp.int16, (atoms_pad, LANES), 0)

    def build(q):
        tops, bottoms, marks = [], [], []
        for pair in range(GROUP // 2):
            s0 = meta_ref[0, slot_at + q * GROUP + 2 * pair]
            s1 = meta_ref[0, slot_at + q * GROUP + 2 * pair + 1]
            k0 = jnp.maximum(s0, 0)
            k1 = jnp.maximum(s1, 0)
            m0 = (s0 >= 0).astype(jnp.float32)
            m1 = (s1 >= 0).astype(jnp.float32)
            c0 = coef_ref[k0].astype(jnp.float32) * m0
            c1 = coef_ref[k1].astype(jnp.float32) * m1
            tops.append(jnp.where(left32, c0, pltpu.roll(c1, BF, 1)))
            bottoms.append(jnp.where(left32, pltpu.roll(c0, BF, 1), c1))
            ids = jnp.where(left1, atom_ref[pl.ds(k0, 1), :], atom_ref[pl.ds(k1, 1), :])
            ids = jnp.broadcast_to(ids, (atoms_pad, LANES)).astype(jnp.int16)
            marks.append(jnp.where(atom_ids == ids, jnp.bfloat16(1), jnp.bfloat16(0)))
        top = jnp.concatenate(tops, axis=1)
        bottom = jnp.concatenate(bottoms, axis=1)
        cp_ref[q] = jnp.concatenate([top, bottom], axis=0).astype(jnp.bfloat16)
        marked = jnp.concatenate(marks, axis=1)
        table = jnp.dot(dict_ref[...], marked, preferred_element_type=jnp.float32)
        at_ref[q] = table.astype(jnp.bfloat16)
        a_ref[q] = table.astype(jnp.bfloat16).T

    def turn(t, carry):
        for n in range(BUILD):
            build(t * BUILD + n)
        return carry

    lax.fori_loop(0, meta_ref[0, turns_at] * (UNROLL // BUILD), turn, 0)


def spread_table(values, table_ref):
    rows = values.shape[0]
    left = lane_ids(rows) < BF
    turned = pltpu.roll(values, BF, 1)
    table_ref[pl.ds(0, rows, stride=2), :] = jnp.where(left, values, turned)
    table_ref[pl.ds(1, rows, stride=2), :] = jnp.where(left, turned, values)


def run_forward(cap, meta_ref, cp_ref, a_ref, table_ref, acc_ref):
    left = lane_ids(1) < BF
    _, row_at, turns_at = plan_spots(cap)

    def turn(t, carry):
        outs = []
        for n in range(UNROLL):
            q = t * UNROLL + n
            u = []
            for pair in range(GROUP // 2):
                p = q * GROUP + 2 * pair
                u0 = table_ref[pl.ds(meta_ref[0, p], 1), :]
                u1 = table_ref[pl.ds(meta_ref[0, p + 1], 1), :]
                u.append(jnp.where(left, u0, u1))
            scaled = cp_ref[q].astype(jnp.float32) * jnp.concatenate(u, axis=1)
            high = scaled.astype(jnp.bfloat16)
            low = (scaled - high.astype(jnp.float32)).astype(jnp.bfloat16)
            both = jnp.concatenate([high, low], axis=0)
            out = jnp.dot(both, a_ref[q], preferred_element_type=jnp.float32)
            outs.append(out[:BV] + out[BV:])
        for n in range(UNROLL):
            r = meta_ref[0, row_at + t * UNROLL + n]
            acc_ref[r] = acc_ref[r] + outs[n]
        return carry

    lax.fori_loop(0, meta_ref[0, turns_at], turn, 0)


def packed_row(acc_ref, r):
    lane = lane_ids(QUART)
    last = acc_ref[r, 3 * QUART :, :]
    return [
        jnp.where(
            lane < DIRS,
            acc_ref[r, i * QUART : (i + 1) * QUART, :],
            pltpu.roll(last, DIRS - 32 * i, 1),
        )
        for i in range(3)
    ]


def pack_rows(acc_ref, out_refs):
    parts = len(out_refs)
    rows = acc_ref.shape[0] // parts
    place = lax.rem(lax.axis_index("fas"), parts) if parts > 1 else 0
    for s in range(parts):
        for n in range(rows):
            r = (place ^ TURN[s]) * rows + n if parts > 1 else n
            for i, piece in enumerate(packed_row(acc_ref, r)):
                out_refs[s][pl.ds(n * PACK + i * QUART, QUART), :] = piece


def flat_rows(acc_ref, f, out_ref):
    lane = lane_ids(acc_ref.shape[0])
    voxels = out_ref.shape[1] // DIRS
    for g in range(voxels // 4):
        first = f * (voxels // 2) + 2 * g
        x = [acc_ref[:, i % 2 * HALF + i // 2 + first, :] for i in range(4)]
        tiles = [
            jnp.where(lane < 96, x[0], pltpu.roll(x[1], 96, 1)),
            jnp.where(lane < 64, pltpu.roll(x[1], 96, 1), pltpu.roll(x[2], 64, 1)),
            jnp.where(lane < 32, pltpu.roll(x[2], 64, 1), pltpu.roll(x[3], 32, 1)),
        ]
        out_ref[:, 4 * g * DIRS : 4 * (g + 1) * DIRS] = jnp.concatenate(tiles, axis=1)


def flat_parts(acc_ref, out_refs):
    parts = len(out_refs)
    if parts == 1:
        for f in range(out_refs[0].shape[0]):
            flat_rows(acc_ref, f, out_refs[0].at[f])
        return
    me = lax.axis_index("fas")
    place = lax.rem(me, parts)
    for s in range(parts):
        for other in range(2):
            f = ((me // parts) ^ other) * parts + (place ^ TURN[s])
            flat_rows(acc_ref, f, out_refs[s].at[other])


def first_kernel(cap, meta_ref, w_ref, sig_ref, cp_ref, a_ref, *refs):
    *out_refs, table_ref, acc_ref = refs
    spread_table(w_ref[...], table_ref)
    acc_ref[...] = sig_ref[...]
    run_forward(cap, meta_ref, cp_ref, a_ref, table_ref, acc_ref)
    pack_rows(acc_ref, out_refs)


def image_kernel(cap, meta_ref, g_ref, w_ref, cp_ref, a_ref, p_ref, sq_ref, *refs):
    *out_refs, table_ref, acc_ref = refs
    gradient = g_ref[...]
    projected = jnp.where((w_ref[...] > 0) | (gradient < 0), gradient, 0.0)
    p_ref[...] = projected
    sq_ref[...] = jnp.sum((projected * projected).reshape(-1, 8, LANES), axis=0)
    spread_table(projected, table_ref)
    acc_ref[...] = jnp.zeros_like(acc_ref)
    run_forward(cap, meta_ref, cp_ref, a_ref, table_ref, acc_ref)
    pack_rows(acc_ref, out_refs)


def update_kernel(
    cap,
    vox_total,
    last,
    meta_ref,
    sums_ref,
    p_ref,
    w_ref,
    sig_ref,
    cp_ref,
    a_ref,
    new_ref,
    *refs,
):
    *out_refs, table_ref, acc_ref = refs
    sums = jnp.sum(sums_ref[...], axis=0)
    left = lane_ids(1) < BF
    image_sq = jnp.sum(jnp.where(left, sums, 0.0), keepdims=True)
    grad_sq = jnp.sum(jnp.where(left, 0.0, sums), keepdims=True) * (1.0 / vox_total)
    step = grad_sq / (image_sq + 1e-6)
    updated = jnp.maximum(w_ref[...] - step * p_ref[...], 0.0)
    new_ref[...] = updated
    spread_table(updated, table_ref)
    acc_ref[...] = sig_ref[...]
    run_forward(cap, meta_ref, cp_ref, a_ref, table_ref, acc_ref)
    if last:
        flat_parts(acc_ref, out_refs)
    else:
        pack_rows(acc_ref, out_refs)


def backward_kernel(cap, vox_rows, meta_ref, cp_ref, at_ref, *refs):
    *res_refs, out_ref, split_ref, left_ref, right_ref = refs
    lane = lane_ids(QUART)
    parts = len(res_refs)
    rows = vox_rows // parts
    place = lax.rem(lax.axis_index("fas"), parts) if parts > 1 else 0
    for s, n in [(s, n) for s in range(parts) for n in range(rows)]:
        r = (place ^ TURN[s]) * rows + n if parts > 1 else n
        packed = [res_refs[s][pl.ds(n * PACK + i * QUART, QUART), :] for i in range(3)]
        turned = [pltpu.roll(packed[i], 32 * (i + 1), 1) for i in range(3)]
        last = jnp.where(lane < 32, turned[0], jnp.where(lane < 64, turned[1], turned[2]))
        whole = jnp.concatenate(packed + [last], axis=0)
        whole = jnp.where(lane_ids(BV) < DIRS, whole, 0.0)
        high = whole.astype(jnp.bfloat16)
        low = (whole - high.astype(jnp.float32)).astype(jnp.bfloat16)
        split_ref[r] = jnp.concatenate([high, low], axis=0)
    left_ref[...] = jnp.zeros_like(left_ref)
    right_ref[...] = jnp.zeros_like(right_ref)
    _, row_at, turns_at = plan_spots(cap)

    def turn(t, carry):
        sums = []
        for n in range(UNROLL):
            q = t * UNROLL + n
            r = meta_ref[0, row_at + q]
            part = jnp.dot(split_ref[r], at_ref[q], preferred_element_type=jnp.float32)
            part = (part[:BV] + part[BV:]) * cp_ref[q].astype(jnp.float32)
            sums.append(jnp.sum(part, axis=0, keepdims=True))
        for n in range(UNROLL):
            for pair in range(GROUP // 2):
                p = (t * UNROLL + n) * GROUP + 2 * pair
                row = sums[n][:, pair * LANES : (pair + 1) * LANES]
                c0 = pl.ds(meta_ref[0, p], 1)
                left_ref[c0, :] = left_ref[c0, :] + row
                c1 = pl.ds(meta_ref[0, p + 1], 1)
                right_ref[c1, :] = right_ref[c1, :] + row
        return carry

    lax.fori_loop(0, meta_ref[0, turns_at], turn, 0)
    rows = out_ref.shape[0]
    left = lane_ids(rows) < BF
    even = [ref[pl.ds(0, rows, stride=2), :] for ref in (left_ref, right_ref)]
    odd = [ref[pl.ds(1, rows, stride=2), :] for ref in (left_ref, right_ref)]
    even = even[0] + pltpu.roll(even[1], BF, 1)
    odd = pltpu.roll(odd[0], BF, 1) + odd[1]
    out_ref[...] = jnp.where(left, even, odd)


def share_kernel(shares_ref, out_ref):
    out_ref[...] = jnp.sum(shares_ref[...], axis=0)


def sum_kernel(*refs):
    *in_refs, out_ref = refs
    total = in_refs[0][...]
    for ref in in_refs[1:]:
        total = total + ref[...]
    out_ref[...] = total


def split_kernel(*refs):
    *in_refs, own_ref, send_ref = refs
    for i, out_ref in enumerate((own_ref, send_ref)):
        total = in_refs[0][i]
        for ref in in_refs[1:]:
            total = total + ref[i]
        out_ref[...] = total


def spread_kernel(mine_ref, other_ref, out_ref):
    total = mine_ref[...] + other_ref[...]
    for i in range(out_ref.shape[0]):
        out_ref[i] = total


def join_kernel(sq_ref, *refs):
    *in_refs, out_ref = refs
    total = in_refs[0][...]
    for ref in in_refs[1:]:
        total = total + ref[...]
    if len(total.shape) == 3:
        total = jnp.sum(total, axis=0)
    rows = total.shape[0]
    out_ref[:rows, :] = total
    out_ref[rows:, :] = sq_ref[...]


def norm_kernel(mine_ref, other_ref, out_ref):
    rows = mine_ref.shape[0] - 8
    image = mine_ref[:rows, :] + other_ref[:rows, :]
    image_sq = jnp.sum(image * image, axis=0, keepdims=True)
    proj_sq = jnp.sum(mine_ref[rows:, :] + other_ref[rows:, :], axis=0, keepdims=True)
    image_sq = image_sq + pltpu.roll(image_sq, BF, 1)
    proj_sq = proj_sq + pltpu.roll(proj_sq, BF, 1)
    sums = jnp.where(lane_ids(1) < BF, image_sq, proj_sq)
    out_ref[...] = jnp.broadcast_to(sums[None], out_ref.shape)


def call(kernel, outs, ins, scratch=()):
    spaces = {"v": pltpu.VMEM, "s": pltpu.SMEM, "m": pltpu.SMEM, "n": pltpu.VMEM}
    run = pl.pallas_call(
        kernel,
        out_shape=tuple(
            jax.ShapeDtypeStruct(shape, dtype) if kind == "n" else spaces[kind](shape, dtype)
            for shape, dtype, kind in outs
        ),
        in_specs=[pl.BlockSpec(memory_space=spaces[kind]) for kind in ins],
        out_specs=tuple(pl.BlockSpec(memory_space=spaces[kind]) for _, _, kind in outs),
        scratch_shapes=list(scratch),
        compiler_params=pltpu.CompilerParams(vmem_limit_bytes=VMEM_LIMIT),
    )

    def placed(*args):
        return run(
            *(
                pltpu.with_memory_space_constraint(x, spaces[kind]) if kind in "vm" else x
                for x, kind in zip(args, ins)
            )
        )

    return placed


def local(
    n_vox,
    n_fas,
    signal,
    initial_weights,
    coefficients,
    block_rows,
    block_cols,
    block_atoms,
    block_count,
    dictionary,
):
    f32, bf16, i32 = jnp.float32, jnp.bfloat16, jnp.int32
    vox_rows = signal.shape[0]
    fas_rows = initial_weights.shape[0] // BF
    slots = coefficients.shape[0]
    cap = group_cap(slots, vox_rows)
    atoms = dictionary.shape[0]
    atoms_pad = -(-atoms // LANES) * LANES
    wide = GROUP * BF
    half_rows = fas_rows // 2

    coef_view = coefficients.reshape(slots, HALF, LANES)
    atom_view = jnp.concatenate([block_atoms, block_atoms], axis=1)
    dict_t = jnp.pad(dictionary.T, ((0, LANES - DIRS), (0, atoms_pad - atoms)))
    fas_place = lax.axis_index("fas")
    side = jnp.stack([block_rows, block_cols], axis=1)
    side = jnp.pad(side, ((0, 0), (0, LANES - 2)))
    plan_size = plan_spots(cap)[2] + LANES
    cp, at, a, meta = call(
        functools.partial(setup_kernel, vox_rows, fas_rows, cap),
        [
            ((cap, BV, wide), bf16, "v"),
            ((cap, LANES, wide), bf16, "v"),
            ((cap, wide, LANES), bf16, "v"),
            ((1, plan_size), i32, "m"),
        ],
        "nvnvvv",
        [pltpu.VMEM((1, plan_size), i32), pltpu.SemaphoreType.DMA],
    )(block_rows[None], side, block_count[None], coef_view, atom_view, dict_t)

    own = signal.shape[1] // DIRS // 2
    negative = -signal.reshape(vox_rows, own, 2, DIRS).transpose(0, 2, 1, 3)
    negative = jnp.pad(negative, ((0, 0), (0, 0), (0, 0), (0, LANES - DIRS)))
    sig = lax.dynamic_update_slice(
        jnp.zeros((vox_rows, 2, HALF, LANES), f32), negative, (0, 0, fas_place * own, 0)
    ).reshape(vox_rows, BV, LANES)

    image_rows = vox_rows * PACK
    table = pltpu.VMEM((fas_rows, LANES), f32)
    acc = pltpu.VMEM((vox_rows, BV, LANES), f32)
    image_out = ((image_rows, LANES), f32, "v")
    flat_out = ((half_rows, LANES), f32, "v")

    def swap(x, axis, groups=None):
        return lax.all_to_all(x, axis, 0, 0, axis_index_groups=groups)

    half = n_fas // 2
    halves = [list(range(half)), list(range(half, n_fas))]
    both_axes = [[i * n_fas + f for i in range(n_vox) for f in group] for group in halves]
    across = [(i, (i + half) % n_fas) for i in range(n_fas)]
    half_share = image_rows // half

    parts = half if half == 4 else 1
    share_out = ((half_share, LANES), f32, "v")
    image_outs = [share_out] * parts if parts > 1 else [image_out]

    flat_count = 2 if parts > 1 else n_fas
    flat_outs = [((flat_count, *signal.shape), f32, "v")] * parts

    def to_place(x, s):
        return lax.ppermute(x, "fas", [(i, i ^ TURN[s]) for i in range(n_fas)])

    def gather_shares(partial):
        if parts > 1:
            return [partial[0]] + [to_place(partial[s], s) for s in range(1, parts)]
        return [swap(partial[0].reshape(half, half_share, LANES), "fas", halves)]

    def sum_all(partial):
        shares = gather_shares(partial)
        if parts > 1:
            (mine,) = call(sum_kernel, [share_out], "v" * parts)(*shares)
            other = lax.ppermute(mine, "fas", across)
            (total,) = call(sum_kernel, [share_out], "vv")(mine, other)
            return [total] + [to_place(total, s) for s in range(1, parts)]
        (mine,) = call(share_kernel, [share_out], "v")(*shares)
        other = lax.ppermute(mine, "fas", across)
        (total,) = call(spread_kernel, [((half, half_share, LANES), f32, "v")], "vv")(mine, other)
        return [swap(total, "fas", halves).reshape(image_rows, LANES)]

    weights = initial_weights.reshape(half_rows, LANES)
    partial = call(
        functools.partial(first_kernel, cap), image_outs, "mvvvv", [table, acc]
    )(meta, weights, sig, cp, a)
    for sweep in range(ITERS):
        last = sweep == ITERS - 1
        whole = sum_all(partial)
        (gradient,) = call(
            functools.partial(backward_kernel, cap, vox_rows),
            [flat_out],
            "mvv" + "v" * parts,
            [pltpu.VMEM((vox_rows, 2 * BV, LANES), bf16), table, table],
        )(meta, cp, at, *whole)
        bit = 1
        while bit < n_vox:
            gradient = gradient + lax.ppermute(
                gradient, "vox", [(i, i ^ bit) for i in range(n_vox)]
            )
            bit *= 2
        projected, proj_sq, *image = call(
            functools.partial(image_kernel, cap),
            [flat_out, ((8, LANES), f32, "v"), *image_outs],
            "mvvvv",
            [table, acc],
        )(meta, gradient, weights, cp, a)
        shares = gather_shares(image)
        (mine,) = call(
            join_kernel, [((half_share + 8, LANES), f32, "v")], "v" * (1 + len(shares))
        )(proj_sq, *shares)
        other = lax.ppermute(mine, "fas", across)
        (sums,) = call(norm_kernel, [((n_vox * half, 1, LANES), f32, "v")], "vv")(mine, other)
        sums = swap(sums, ("vox", "fas"), both_axes)
        outs = flat_outs if last else image_outs
        weights, *partial = call(
            functools.partial(update_kernel, cap, n_vox, last),
            [flat_out if not last else (*flat_out[:2], "n"), *outs],
            "mvvvvvv",
            [table, acc],
        )(meta, sums, projected, weights, sig, cp, a)
    if parts > 1:
        shares = [partial[0]] + [to_place(partial[s], s) for s in range(1, parts)]
        piece = (signal.shape, f32, "v")
        own, send = call(split_kernel, [piece, piece], "v" * parts)(*shares)
        other = lax.ppermute(send, "fas", across)
        (final,) = call(sum_kernel, [(signal.shape, f32, "n")], "vv")(own, other)
    else:
        final = jnp.sum(swap(partial[0], "fas"), axis=0)
    return (weights.reshape(-1), final)


def solution(mesh):
    placed = (
        P("vox", "fas"),
        P("fas"),
        P(("vox", "fas"), None),
        P(("vox", "fas")),
        P(("vox", "fas")),
        P(("vox", "fas"), None),
        P(("vox", "fas")),
        P(),
    )
    return jax.shard_map(
        functools.partial(local, mesh.shape["vox"], mesh.shape["fas"]),
        mesh=mesh,
        in_specs=placed,
        out_specs=(P("fas"), P("vox", "fas")),
        check_vma=False,
    )
```

```python
import functools

import jax
import jax.numpy as jnp
from jax import lax
from jax.experimental import pallas as pl
from jax.experimental.pallas import tpu as pltpu
from jax.sharding import PartitionSpec as P

BV = 64
BF = 64
DIRS = 96
ITERS = 5
LANES = 128
GROUP = 4
BUILD = 38
UNROLL = 38
PACK = BV * DIRS // LANES
HALF = BV // 2
QUART = BV // 4
TURN = (0, 3, 1, 2)
VMEM_LIMIT = 16 * 1024 * 1024


def group_cap(slots, rows):
    groups = (slots + (GROUP - 1) * rows) // GROUP
    return -(-groups // (2 * UNROLL)) * 2 * UNROLL


def plan_spots(cap):
    places = -(-cap * GROUP // LANES) * LANES
    return places, 2 * places, 2 * places + -(-cap // LANES) * LANES


def lane_ids(rows):
    return lax.broadcasted_iota(jnp.int32, (rows, LANES), 1)


def plan_slots(vox_rows, fas_rows, cap, row_ref, side_ref, count_ref, plan_ref):
    f32, i32 = jnp.float32, jnp.int32
    slots = row_ref.shape[1]
    places = cap * GROUP
    count = count_ref[...]
    down = lax.broadcasted_iota(i32, (slots, 1), 0)
    along = lax.broadcasted_iota(i32, (1, slots), 1)
    rows_down = jnp.where(down < count, lax.rem(side_ref[:, 0:1], vox_rows), vox_rows)
    cols_down = lax.rem(side_ref[:, 1:2], fas_rows)
    rows_along = jnp.where(along < count, lax.rem(row_ref[...], vox_rows), vox_rows)
    lane = lane_ids(1)
    member = (rows_down == lane) & (lane < vox_rows)
    counts = jnp.sum(member.astype(i32), axis=0, keepdims=True)
    groups = (counts + GROUP - 1) // GROUP
    earlier = lax.broadcasted_iota(i32, (LANES, LANES), 0) < lane_ids(LANES)
    start = jnp.dot(
        jnp.broadcast_to(groups, (8, LANES)).astype(f32).astype(jnp.bfloat16),
        earlier.astype(f32).astype(jnp.bfloat16),
        preferred_element_type=f32,
    )[0:1].astype(i32)
    rank = jnp.sum(
        ((rows_along == rows_down) & (along < down)).astype(i32), axis=1, keepdims=True
    )
    first = jnp.sum(jnp.where(member, start, 0), axis=1, keepdims=True)
    place = jnp.where(rows_down < vox_rows, first * GROUP + rank, -1)
    spots = lax.broadcasted_iota(i32, (1, places), 1)
    chosen = place == spots
    slot_at, row_at, turns_at = plan_spots(cap)
    plan_ref[:, 0:places] = jnp.sum(jnp.where(chosen, cols_down, 0), axis=0, keepdims=True)
    slot = jnp.sum(jnp.where(chosen, down + 1, 0), axis=0, keepdims=True) - 1
    plan_ref[:, slot_at : slot_at + places] = slot
    heads = lax.broadcasted_iota(i32, (1, cap), 1) * GROUP
    row = jnp.sum(jnp.where(place == heads, rows_down, 0), axis=0, keepdims=True)
    plan_ref[:, row_at : row_at + cap] = row
    total = jnp.sum(groups, axis=1, keepdims=True)
    turns = (total + 2 * UNROLL - 1) // (2 * UNROLL) * 2
    plan_ref[:, turns_at:] = jnp.broadcast_to(turns, (1, LANES))


def setup_kernel(
    vox_rows,
    fas_rows,
    cap,
    row_ref,
    side_ref,
    count_ref,
    coef_ref,
    atom_ref,
    dict_ref,
    cp_ref,
    at_ref,
    a_ref,
    meta_ref,
    plan_ref,
    sem,
):
    plan_slots(vox_rows, fas_rows, cap, row_ref, side_ref, count_ref, plan_ref)
    plan = pltpu.make_async_copy(plan_ref, meta_ref, sem)
    plan.start()
    plan.wait()
    slot_at, _, turns_at = plan_spots(cap)
    atoms_pad = dict_ref.shape[1]
    left32 = lane_ids(HALF) < BF
    left1 = lane_ids(1) < BF
    atom_ids = lax.broadcasted_iota(jnp.int16, (atoms_pad, LANES), 0)

    def build(q):
        tops, bottoms, marks = [], [], []
        for pair in range(GROUP // 2):
            s0 = meta_ref[0, slot_at + q * GROUP + 2 * pair]
            s1 = meta_ref[0, slot_at + q * GROUP + 2 * pair + 1]
            k0 = jnp.maximum(s0, 0)
            k1 = jnp.maximum(s1, 0)
            m0 = (s0 >= 0).astype(jnp.float32)
            m1 = (s1 >= 0).astype(jnp.float32)
            c0 = coef_ref[k0].astype(jnp.float32) * m0
            c1 = coef_ref[k1].astype(jnp.float32) * m1
            tops.append(jnp.where(left32, c0, pltpu.roll(c1, BF, 1)))
            bottoms.append(jnp.where(left32, pltpu.roll(c0, BF, 1), c1))
            ids = jnp.where(left1, atom_ref[pl.ds(k0, 1), :], atom_ref[pl.ds(k1, 1), :])
            ids = jnp.broadcast_to(ids, (atoms_pad, LANES)).astype(jnp.int16)
            marks.append(jnp.where(atom_ids == ids, jnp.bfloat16(1), jnp.bfloat16(0)))
        top = jnp.concatenate(tops, axis=1)
        bottom = jnp.concatenate(bottoms, axis=1)
        cp_ref[q] = jnp.concatenate([top, bottom], axis=0).astype(jnp.bfloat16)
        marked = jnp.concatenate(marks, axis=1)
        table = jnp.dot(dict_ref[...], marked, preferred_element_type=jnp.float32)
        at_ref[q] = table.astype(jnp.bfloat16)
        a_ref[q] = table.astype(jnp.bfloat16).T

    def turn(t, carry):
        for n in range(BUILD):
            build(t * BUILD + n)
        return carry

    lax.fori_loop(0, meta_ref[0, turns_at] * (UNROLL // BUILD), turn, 0)


def spread_table(values, table_ref):
    rows = values.shape[0]
    left = lane_ids(rows) < BF
    turned = pltpu.roll(values, BF, 1)
    table_ref[pl.ds(0, rows, stride=2), :] = jnp.where(left, values, turned)
    table_ref[pl.ds(1, rows, stride=2), :] = jnp.where(left, turned, values)


def run_forward(cap, meta_ref, cp_ref, a_ref, table_ref, acc_ref):
    left = lane_ids(1) < BF
    _, row_at, turns_at = plan_spots(cap)

    def turn(t, carry):
        outs = []
        for n in range(UNROLL):
            q = t * UNROLL + n
            u = []
            for pair in range(GROUP // 2):
                p = q * GROUP + 2 * pair
                u0 = table_ref[pl.ds(meta_ref[0, p], 1), :]
                u1 = table_ref[pl.ds(meta_ref[0, p + 1], 1), :]
                u.append(jnp.where(left, u0, u1))
            scaled = cp_ref[q].astype(jnp.float32) * jnp.concatenate(u, axis=1)
            high = scaled.astype(jnp.bfloat16)
            low = (scaled - high.astype(jnp.float32)).astype(jnp.bfloat16)
            both = jnp.concatenate([high, low], axis=0)
            out = jnp.dot(both, a_ref[q], preferred_element_type=jnp.float32)
            outs.append(out[:BV] + out[BV:])
        for n in range(UNROLL):
            r = meta_ref[0, row_at + t * UNROLL + n]
            acc_ref[r] = acc_ref[r] + outs[n]
        return carry

    lax.fori_loop(0, meta_ref[0, turns_at], turn, 0)


def packed_row(acc_ref, r):
    lane = lane_ids(QUART)
    last = acc_ref[r, 3 * QUART :, :]
    return [
        jnp.where(
            lane < DIRS,
            acc_ref[r, i * QUART : (i + 1) * QUART, :],
            pltpu.roll(last, DIRS - 32 * i, 1),
        )
        for i in range(3)
    ]


def pack_rows(acc_ref, out_refs):
    parts = len(out_refs)
    rows = acc_ref.shape[0] // parts
    place = lax.rem(lax.axis_index("fas"), parts) if parts > 1 else 0
    for s in range(parts):
        for n in range(rows):
            r = (place ^ TURN[s]) * rows + n if parts > 1 else n
            for i, piece in enumerate(packed_row(acc_ref, r)):
                out_refs[s][pl.ds(n * PACK + i * QUART, QUART), :] = piece


def flat_rows(acc_ref, f, out_ref):
    lane = lane_ids(acc_ref.shape[0])
    voxels = out_ref.shape[1] // DIRS
    for g in range(voxels // 4):
        first = f * (voxels // 2) + 2 * g
        x = [acc_ref[:, i % 2 * HALF + i // 2 + first, :] for i in range(4)]
        tiles = [
            jnp.where(lane < 96, x[0], pltpu.roll(x[1], 96, 1)),
            jnp.where(lane < 64, pltpu.roll(x[1], 96, 1), pltpu.roll(x[2], 64, 1)),
            jnp.where(lane < 32, pltpu.roll(x[2], 64, 1), pltpu.roll(x[3], 32, 1)),
        ]
        out_ref[:, 4 * g * DIRS : 4 * (g + 1) * DIRS] = jnp.concatenate(tiles, axis=1)


def flat_parts(acc_ref, out_refs):
    parts = len(out_refs)
    if parts == 1:
        for f in range(out_refs[0].shape[0]):
            flat_rows(acc_ref, f, out_refs[0].at[f])
        return
    me = lax.axis_index("fas")
    place = lax.rem(me, parts)
    for s in range(parts):
        for other in range(2):
            f = ((me // parts) ^ other) * parts + (place ^ TURN[s])
            flat_rows(acc_ref, f, out_refs[s].at[other])


def first_kernel(cap, meta_ref, w_ref, sig_ref, cp_ref, a_ref, *refs):
    *out_refs, table_ref, acc_ref = refs
    spread_table(w_ref[...], table_ref)
    acc_ref[...] = sig_ref[...]
    run_forward(cap, meta_ref, cp_ref, a_ref, table_ref, acc_ref)
    pack_rows(acc_ref, out_refs)


def image_kernel(cap, meta_ref, g_ref, w_ref, cp_ref, a_ref, p_ref, sq_ref, *refs):
    *out_refs, table_ref, acc_ref = refs
    gradient = g_ref[...]
    projected = jnp.where((w_ref[...] > 0) | (gradient < 0), gradient, 0.0)
    p_ref[...] = projected
    sq_ref[...] = jnp.sum((projected * projected).reshape(-1, 8, LANES), axis=0)
    spread_table(projected, table_ref)
    acc_ref[...] = jnp.zeros_like(acc_ref)
    run_forward(cap, meta_ref, cp_ref, a_ref, table_ref, acc_ref)
    pack_rows(acc_ref, out_refs)


def update_kernel(
    cap,
    vox_total,
    last,
    meta_ref,
    sums_ref,
    p_ref,
    w_ref,
    sig_ref,
    cp_ref,
    a_ref,
    new_ref,
    *refs,
):
    *out_refs, table_ref, acc_ref = refs
    sums = jnp.sum(sums_ref[...], axis=0)
    left = lane_ids(1) < BF
    image_sq = jnp.sum(jnp.where(left, sums, 0.0), keepdims=True)
    grad_sq = jnp.sum(jnp.where(left, 0.0, sums), keepdims=True) * (1.0 / vox_total)
    step = grad_sq / (image_sq + 1e-6)
    updated = jnp.maximum(w_ref[...] - step * p_ref[...], 0.0)
    new_ref[...] = updated
    spread_table(updated, table_ref)
    acc_ref[...] = sig_ref[...]
    run_forward(cap, meta_ref, cp_ref, a_ref, table_ref, acc_ref)
    if last:
        flat_parts(acc_ref, out_refs)
    else:
        pack_rows(acc_ref, out_refs)


def backward_kernel(cap, vox_rows, meta_ref, cp_ref, at_ref, *refs):
    *res_refs, out_ref, split_ref, left_ref, right_ref = refs
    lane = lane_ids(QUART)
    parts = len(res_refs)
    rows = vox_rows // parts
    place = lax.rem(lax.axis_index("fas"), parts) if parts > 1 else 0
    for s, n in [(s, n) for s in range(parts) for n in range(rows)]:
        r = (place ^ TURN[s]) * rows + n if parts > 1 else n
        packed = [res_refs[s][pl.ds(n * PACK + i * QUART, QUART), :] for i in range(3)]
        turned = [pltpu.roll(packed[i], 32 * (i + 1), 1) for i in range(3)]
        last = jnp.where(lane < 32, turned[0], jnp.where(lane < 64, turned[1], turned[2]))
        whole = jnp.concatenate(packed + [last], axis=0)
        whole = jnp.where(lane_ids(BV) < DIRS, whole, 0.0)
        high = whole.astype(jnp.bfloat16)
        low = (whole - high.astype(jnp.float32)).astype(jnp.bfloat16)
        split_ref[r] = jnp.concatenate([high, low], axis=0)
    left_ref[...] = jnp.zeros_like(left_ref)
    right_ref[...] = jnp.zeros_like(right_ref)
    _, row_at, turns_at = plan_spots(cap)

    def turn(t, carry):
        sums = []
        for n in range(2 * UNROLL):
            q = t * 2 * UNROLL + n
            r = meta_ref[0, row_at + q]
            part = jnp.dot(split_ref[r], at_ref[q], preferred_element_type=jnp.float32)
            part = (part[:BV] + part[BV:]) * cp_ref[q].astype(jnp.float32)
            sums.append(jnp.sum(part, axis=0, keepdims=True))
        for n in range(2 * UNROLL):
            for pair in range(GROUP // 2):
                p = (t * 2 * UNROLL + n) * GROUP + 2 * pair
                row = sums[n][:, pair * LANES : (pair + 1) * LANES]
                c0 = pl.ds(meta_ref[0, p], 1)
                left_ref[c0, :] = left_ref[c0, :] + row
                c1 = pl.ds(meta_ref[0, p + 1], 1)
                right_ref[c1, :] = right_ref[c1, :] + row
        return carry

    lax.fori_loop(0, meta_ref[0, turns_at] // 2, turn, 0)
    rows = out_ref.shape[0]
    left = lane_ids(rows) < BF
    even = [ref[pl.ds(0, rows, stride=2), :] for ref in (left_ref, right_ref)]
    odd = [ref[pl.ds(1, rows, stride=2), :] for ref in (left_ref, right_ref)]
    even = even[0] + pltpu.roll(even[1], BF, 1)
    odd = pltpu.roll(odd[0], BF, 1) + odd[1]
    out_ref[...] = jnp.where(left, even, odd)


def share_kernel(shares_ref, out_ref):
    out_ref[...] = jnp.sum(shares_ref[...], axis=0)


def sum_kernel(*refs):
    *in_refs, out_ref = refs
    total = in_refs[0][...]
    for ref in in_refs[1:]:
        total = total + ref[...]
    out_ref[...] = total


def split_kernel(*refs):
    *in_refs, own_ref, send_ref = refs
    for i, out_ref in enumerate((own_ref, send_ref)):
        total = in_refs[0][i]
        for ref in in_refs[1:]:
            total = total + ref[i]
        out_ref[...] = total


def spread_kernel(mine_ref, other_ref, out_ref):
    total = mine_ref[...] + other_ref[...]
    for i in range(out_ref.shape[0]):
        out_ref[i] = total


def join_kernel(sq_ref, *refs):
    *in_refs, out_ref = refs
    total = in_refs[0][...]
    for ref in in_refs[1:]:
        total = total + ref[...]
    if len(total.shape) == 3:
        total = jnp.sum(total, axis=0)
    rows = total.shape[0]
    out_ref[:rows, :] = total
    out_ref[rows:, :] = sq_ref[...]


def norm_kernel(mine_ref, other_ref, out_ref):
    rows = mine_ref.shape[0] - 8
    image = mine_ref[:rows, :] + other_ref[:rows, :]
    image_sq = jnp.sum(image * image, axis=0, keepdims=True)
    proj_sq = jnp.sum(mine_ref[rows:, :] + other_ref[rows:, :], axis=0, keepdims=True)
    image_sq = image_sq + pltpu.roll(image_sq, BF, 1)
    proj_sq = proj_sq + pltpu.roll(proj_sq, BF, 1)
    sums = jnp.where(lane_ids(1) < BF, image_sq, proj_sq)
    out_ref[...] = jnp.broadcast_to(sums[None], out_ref.shape)


def call(kernel, outs, ins, scratch=()):
    spaces = {"v": pltpu.VMEM, "s": pltpu.SMEM, "m": pltpu.SMEM, "n": pltpu.VMEM}
    run = pl.pallas_call(
        kernel,
        out_shape=tuple(
            jax.ShapeDtypeStruct(shape, dtype) if kind == "n" else spaces[kind](shape, dtype)
            for shape, dtype, kind in outs
        ),
        in_specs=[pl.BlockSpec(memory_space=spaces[kind]) for kind in ins],
        out_specs=tuple(pl.BlockSpec(memory_space=spaces[kind]) for _, _, kind in outs),
        scratch_shapes=list(scratch),
        compiler_params=pltpu.CompilerParams(vmem_limit_bytes=VMEM_LIMIT),
    )

    def placed(*args):
        return run(
            *(
                pltpu.with_memory_space_constraint(x, spaces[kind]) if kind in "vm" else x
                for x, kind in zip(args, ins)
            )
        )

    return placed


def local(
    n_vox,
    n_fas,
    signal,
    initial_weights,
    coefficients,
    block_rows,
    block_cols,
    block_atoms,
    block_count,
    dictionary,
):
    f32, bf16, i32 = jnp.float32, jnp.bfloat16, jnp.int32
    vox_rows = signal.shape[0]
    fas_rows = initial_weights.shape[0] // BF
    slots = coefficients.shape[0]
    cap = group_cap(slots, vox_rows)
    atoms = dictionary.shape[0]
    atoms_pad = -(-atoms // LANES) * LANES
    wide = GROUP * BF
    half_rows = fas_rows // 2

    coef_view = coefficients.reshape(slots, HALF, LANES)
    atom_view = jnp.concatenate([block_atoms, block_atoms], axis=1)
    dict_t = jnp.pad(dictionary.T, ((0, LANES - DIRS), (0, atoms_pad - atoms)))
    fas_place = lax.axis_index("fas")
    side = jnp.stack([block_rows, block_cols], axis=1)
    side = jnp.pad(side, ((0, 0), (0, LANES - 2)))
    plan_size = plan_spots(cap)[2] + LANES
    cp, at, a, meta = call(
        functools.partial(setup_kernel, vox_rows, fas_rows, cap),
        [
            ((cap, BV, wide), bf16, "v"),
            ((cap, LANES, wide), bf16, "v"),
            ((cap, wide, LANES), bf16, "v"),
            ((1, plan_size), i32, "m"),
        ],
        "nvnvvv",
        [pltpu.VMEM((1, plan_size), i32), pltpu.SemaphoreType.DMA],
    )(block_rows[None], side, block_count[None], coef_view, atom_view, dict_t)

    own = signal.shape[1] // DIRS // 2
    negative = -signal.reshape(vox_rows, own, 2, DIRS).transpose(0, 2, 1, 3)
    negative = jnp.pad(negative, ((0, 0), (0, 0), (0, 0), (0, LANES - DIRS)))
    sig = lax.dynamic_update_slice(
        jnp.zeros((vox_rows, 2, HALF, LANES), f32), negative, (0, 0, fas_place * own, 0)
    ).reshape(vox_rows, BV, LANES)

    image_rows = vox_rows * PACK
    table = pltpu.VMEM((fas_rows, LANES), f32)
    acc = pltpu.VMEM((vox_rows, BV, LANES), f32)
    image_out = ((image_rows, LANES), f32, "v")
    flat_out = ((half_rows, LANES), f32, "v")

    def swap(x, axis, groups=None):
        return lax.all_to_all(x, axis, 0, 0, axis_index_groups=groups)

    half = n_fas // 2
    halves = [list(range(half)), list(range(half, n_fas))]
    both_axes = [[i * n_fas + f for i in range(n_vox) for f in group] for group in halves]
    across = [(i, (i + half) % n_fas) for i in range(n_fas)]
    half_share = image_rows // half

    parts = half if half == 4 else 1
    share_out = ((half_share, LANES), f32, "v")
    image_outs = [share_out] * parts if parts > 1 else [image_out]

    flat_count = 2 if parts > 1 else n_fas
    flat_outs = [((flat_count, *signal.shape), f32, "v")] * parts

    def to_place(x, s):
        return lax.ppermute(x, "fas", [(i, i ^ TURN[s]) for i in range(n_fas)])

    def gather_shares(partial):
        if parts > 1:
            return [partial[0]] + [to_place(partial[s], s) for s in range(1, parts)]
        return [swap(partial[0].reshape(half, half_share, LANES), "fas", halves)]

    def sum_all(partial):
        shares = gather_shares(partial)
        if parts > 1:
            (mine,) = call(sum_kernel, [share_out], "v" * parts)(*shares)
            other = lax.ppermute(mine, "fas", across)
            (total,) = call(sum_kernel, [share_out], "vv")(mine, other)
            return [total] + [to_place(total, s) for s in range(1, parts)]
        (mine,) = call(share_kernel, [share_out], "v")(*shares)
        other = lax.ppermute(mine, "fas", across)
        (total,) = call(spread_kernel, [((half, half_share, LANES), f32, "v")], "vv")(mine, other)
        return [swap(total, "fas", halves).reshape(image_rows, LANES)]

    weights = initial_weights.reshape(half_rows, LANES)
    partial = call(
        functools.partial(first_kernel, cap), image_outs, "mvvvv", [table, acc]
    )(meta, weights, sig, cp, a)
    for sweep in range(ITERS):
        last = sweep == ITERS - 1
        whole = sum_all(partial)
        (gradient,) = call(
            functools.partial(backward_kernel, cap, vox_rows),
            [flat_out],
            "mvv" + "v" * parts,
            [pltpu.VMEM((vox_rows, 2 * BV, LANES), bf16), table, table],
        )(meta, cp, at, *whole)
        bit = 1
        while bit < n_vox:
            gradient = gradient + lax.ppermute(
                gradient, "vox", [(i, i ^ bit) for i in range(n_vox)]
            )
            bit *= 2
        projected, proj_sq, *image = call(
            functools.partial(image_kernel, cap),
            [flat_out, ((8, LANES), f32, "v"), *image_outs],
            "mvvvv",
            [table, acc],
        )(meta, gradient, weights, cp, a)
        shares = gather_shares(image)
        (mine,) = call(
            join_kernel, [((half_share + 8, LANES), f32, "v")], "v" * (1 + len(shares))
        )(proj_sq, *shares)
        other = lax.ppermute(mine, "fas", across)
        (sums,) = call(norm_kernel, [((n_vox * half, 1, LANES), f32, "v")], "vv")(mine, other)
        sums = swap(sums, ("vox", "fas"), both_axes)
        outs = flat_outs if last else image_outs
        weights, *partial = call(
            functools.partial(update_kernel, cap, n_vox, last),
            [flat_out if not last else (*flat_out[:2], "n"), *outs],
            "mvvvvvv",
            [table, acc],
        )(meta, sums, projected, weights, sig, cp, a)
    if parts > 1:
        shares = [partial[0]] + [to_place(partial[s], s) for s in range(1, parts)]
        piece = (signal.shape, f32, "v")
        own, send = call(split_kernel, [piece, piece], "v" * parts)(*shares)
        other = lax.ppermute(send, "fas", across)
        (final,) = call(sum_kernel, [(signal.shape, f32, "n")], "vv")(own, other)
    else:
        final = jnp.sum(swap(partial[0], "fas"), axis=0)
    return (weights.reshape(-1), final)


def solution(mesh):
    placed = (
        P("vox", "fas"),
        P("fas"),
        P(("vox", "fas"), None),
        P(("vox", "fas")),
        P(("vox", "fas")),
        P(("vox", "fas"), None),
        P(("vox", "fas")),
        P(),
    )
    return jax.shard_map(
        functools.partial(local, mesh.shape["vox"], mesh.shape["fas"]),
        mesh=mesh,
        in_specs=placed,
        out_specs=(P("fas"), P("vox", "fas")),
        check_vma=False,
    )
```
